32 devices in a mesh: fsdp: 32 (over z, y, x, core).
Axes of the slice: x: 2, y: 2, z: 4, core: 2. Of those that a mesh axis runs over, the one named last changes fastest.
Arguments:
- tokens: bfloat16 [4096, 1152], P('fsdp'), may hold values from -6 to 6
- cond: bfloat16 [96, 1152], P('fsdp'), may hold values from -6 to 6
- image_lengths: int32 [32, 3], P('fsdp'), may hold values from 1 to 102, 128 in all within a row
- ada_weight: bfloat16 [7962624], P('fsdp'), may hold values from -0.1875 to 0.1875
- ada_bias: bfloat16 [6912], P('fsdp'), may hold values from -3 to 3
- qkv_weight: bfloat16 [3981312], P('fsdp'), may hold values from -0.1875 to 0.1875
- qv_bias: bfloat16 [2304], P('fsdp'), may hold values from -3 to 3
- attn_weight: bfloat16 [1327104], P('fsdp'), may hold values from -0.5 to 0.5
- tail_bias: bfloat16 [2304], P('fsdp'), may hold values from -3 to 3
- up_weight: bfloat16 [5308416], P('fsdp'), may hold values from -0.1875 to 0.1875
- up_bias: bfloat16 [4608], P('fsdp'), may hold values from -3 to 3
- down_weight: bfloat16 [5308416], P('fsdp'), may hold values from -0.09375 to 0.09375
- projector_in: bfloat16 [2359296], P('fsdp'), may hold values from -0.1875 to 0.1875
- projector_in_bias: bfloat16 [2048], P('fsdp'), may hold values from -3 to 3
- projector_mid: bfloat16 [4194304], P('fsdp'), may hold values from -0.125 to 0.125
- projector_mid_bias: bfloat16 [2048], P('fsdp'), may hold values from -3 to 3
- projector_out: bfloat16 [1572864], P('fsdp'), may hold values from -0.125 to 0.125
- projector_out_bias: bfloat16 [768], P('fsdp'), may hold values from -3 to 3
- targets: bfloat16 [4096, 768], P('fsdp'), may hold values from -6 to 6
- out_grad: bfloat16 [4096, 1152], P('fsdp'), may hold values from -6 to 6
Outputs:
- mixed: bfloat16 [4096, 1152], P('fsdp')
- tokens_grad: bfloat16 [4096, 1152], P('fsdp')
- cond_grad: bfloat16 [96, 1152], P('fsdp')
- ada_weight_grad: float32 [7962624], P('fsdp')
- ada_bias_grad: float32 [6912], P('fsdp')
- qkv_weight_grad: float32 [3981312], P('fsdp')
- qv_bias_grad: float32 [2304], P('fsdp')
- attn_weight_grad: float32 [1327104], P('fsdp')
- tail_bias_grad: float32 [2304], P('fsdp')
- up_weight_grad: float32 [5308416], P('fsdp')
- up_bias_grad: float32 [4608], P('fsdp')
- down_weight_grad: float32 [5308416], P('fsdp')
- projector_in_grad: float32 [2359296], P('fsdp')
- projector_in_bias_grad: float32 [2048], P('fsdp')
- projector_mid_grad: float32 [4194304], P('fsdp')
- projector_mid_bias_grad: float32 [2048], P('fsdp')
- projector_out_grad: float32 [1572864], P('fsdp')
- projector_out_bias_grad: float32 [768], P('fsdp')
The draws below stay inside these ranges and needn't reach their ends.
Inputs may be any that keep to these rules, and one draw needn't show every extreme that they name: Each row of image_lengths sums to 128, and its longest image has 102 tokens.
All inputs are finite; a program needn't handle non-finite values.
Results may differ from the reference program's by a relative error of at most 0.015.
The reference program's roundings to bfloat16 on the way count: a program that leaves them out, or rounds other values in their place, can miss the bound.
Values may be sent and summed in bfloat16 or wider, within the bound.
A program may use at most 512 MiB of HBM per device.

```python
import math
import jax
import jax.numpy as jnp
import numpy as np
from jax import lax

D = 1152
HEADS = 16
HD = 72
FF = 4608
P_SIZE = 2048
Z = 768
TOK_DEV = 128
IMG_DEV = 3
LONGEST = 102
SHARDS = 32
TOKENS = 4096
IMAGES = 96


def block_levels(key, dims, pieces, least, high):
    gain, own = 1.0, jax.random.fold_in(key, 6)
    for axis_at, parts in pieces:
        heights = jnp.exp(jax.random.uniform(jax.random.fold_in(own, axis_at), (parts,), jnp.float32, least / len(pieces), high / len(pieces)))
        gain = gain * jnp.repeat(heights, dims[axis_at] // parts).reshape([-1 if axis == axis_at else 1 for axis in range(len(dims))])
    return gain


def split_up(count, total, bound, skew):
    loads = [(1 << 20) // math.isqrt(standing ** skew) + 1 for standing in range(2, count + 1)]
    surplus, counts = total - bound - (count - 1), [1] * (count - 1)
    while surplus > 0:
        candidates = [i for i in range(count - 1) if counts[i] < bound]
        mass, budget = sum([loads[i] for i in candidates]), surplus
        for i in candidates:
            more = min(bound - counts[i], max(1, budget * loads[i] // mass), surplus)
            counts[i] = counts[i] + more
            surplus = surplus - more
    return np.array([bound] + counts)


def uneven_parts(own_key, number_of, total, bound, lean):
    if number_of == 2:
        one = jax.random.randint(own_key, (), max(1, total - bound), min(bound, total - 1) + 1)
        return jnp.stack([one, total - one])
    tallies = jnp.asarray(split_up(number_of, total, bound, lean), jnp.int32)
    couples = (number_of - 1) // 2
    source_of, receiver = tallies[1:1 + 2 * couples:2], tallies[2:2 + 2 * couples:2]
    room = jnp.minimum(source_of - 1, bound - receiver)
    moved = jax.random.randint(jax.random.fold_in(own_key, 1), (couples,), 0, 1 << 20) % (room + 1)
    tallies = tallies.at[1:1 + 2 * couples:2].set(source_of - moved).at[2:2 + 2 * couples:2].set(receiver + moved)
    return tallies[jax.random.permutation(jax.random.fold_in(own_key, 2), number_of)]


def noise(stream_key, dims, deviation, limit, pieces=(), held_as=jnp.bfloat16):
    result = deviation * jax.random.normal(stream_key, dims, jnp.float32)
    if pieces:
        result = result * block_levels(stream_key, dims, pieces, -0.22, 0.18)
    return jnp.clip(result, -limit, limit).astype(held_as)


def setup_inputs(seed: int = 0) -> dict:
    arg_keys = jax.random.split(jax.random.key(seed), 21)
    return {
        "tokens": noise(arg_keys[0], (TOKENS, D), 1.0, 6.0, ((0, 32),)),
        "cond": noise(arg_keys[1], (IMAGES, D), 1.0, 6.0, ((0, 32),)),
        "image_lengths": jax.vmap(lambda own: uneven_parts(own, IMG_DEV, TOK_DEV, LONGEST, 2))(jax.random.split(arg_keys[2], SHARDS)).reshape((SHARDS, IMG_DEV)).astype(jnp.int32),
        "ada_weight": noise(arg_keys[3], (6 * D * D,), D ** -0.5, 0.1875, ((0, 32),)),
        "ada_bias": noise(arg_keys[4], (6 * D,), 0.5, 3.0, ((0, 32),)),
        "qkv_weight": noise(arg_keys[5], (3 * D * D,), D ** -0.5, 0.1875, ((0, 32),)),
        "qv_bias": noise(arg_keys[6], (2 * D,), 0.5, 3.0, ((0, 32),)),
        "attn_weight": noise(arg_keys[7], (D * D,), (D // 8) ** -0.5, 0.5, ((0, 32),)),
        "tail_bias": noise(arg_keys[8], (2 * D,), 0.5, 3.0, ((0, 32),)),
        "up_weight": noise(arg_keys[9], (D * FF,), D ** -0.5, 0.1875, ((0, 32),)),
        "up_bias": noise(arg_keys[10], (FF,), 0.5, 3.0, ((0, 32),)),
        "down_weight": noise(arg_keys[11], (FF * D,), FF ** -0.5, 0.09375, ((0, 32),)),
        "projector_in": noise(arg_keys[12], (D * P_SIZE,), D ** -0.5, 0.1875, ((0, 32),)),
        "projector_in_bias": noise(arg_keys[13], (P_SIZE,), 0.5, 3.0, ((0, 32),)),
        "projector_mid": noise(arg_keys[14], (P_SIZE * P_SIZE,), P_SIZE ** -0.5, 0.125, ((0, 32),)),
        "projector_mid_bias": noise(arg_keys[15], (P_SIZE,), 0.5, 3.0, ((0, 32),)),
        "projector_out": noise(arg_keys[16], (P_SIZE * Z,), P_SIZE ** -0.5, 0.125, ((0, 32),)),
        "projector_out_bias": noise(arg_keys[17], (Z,), 0.5, 3.0, ((0, 32),)),
        "targets": noise(arg_keys[18], (TOKENS, Z), 1.0, 6.0, ((0, 32),)),
        "out_grad": noise(arg_keys[19], (TOKENS, D), 1.0, 6.0, ((0, 32),)),
    }


EPSILON = 1e-06
PRECISE = lax.Precision.HIGHEST

@jax.custom_vjp
def low(v):
    return lax.optimization_barrier(v.astype(jnp.bfloat16)).astype(jnp.float32)

@jax.custom_vjp
def low_back(v):
    return v

def low_keep(v):
    return (low(v), None)

def low_pass(kept, grad):
    return (grad,)

def back_keep(v):
    return (v, None)

def back_low(kept, grad):
    return (low(grad),)
low.defvjp(low_keep, low_pass)
low_back.defvjp(back_keep, back_low)

def layer_norm(values):
    centred = values - lax.optimization_barrier(jnp.mean(values, axis=-1, keepdims=True))
    spread = lax.optimization_barrier(jnp.mean(centred * centred, axis=-1, keepdims=True))
    return centred * lax.rsqrt(spread + EPSILON)

def sigmoid_linear(values):
    return values * jax.nn.sigmoid(values)

def gelu_tanh(values):
    inner = 0.7978845608028654 * (values + 0.044715 * values * values * values)
    return 0.5 * values * (1.0 + jnp.tanh(inner))

def image_onehot(lengths, row_count):
    ends = jnp.cumsum(lengths).astype(jnp.int32)
    position = jnp.arange(row_count, dtype=jnp.int32)
    image_of = lax.optimization_barrier(jnp.sum((position[:, None] >= ends[None, :]).astype(jnp.int32), axis=1)).astype(jnp.int32)
    images = jnp.arange(lengths.shape[0], dtype=jnp.int32)
    return (image_of, (image_of[:, None] == images[None, :]).astype(jnp.float32))

def matmul_high(left, right):
    return jnp.dot(left, right, precision=PRECISE)

def device_block(rows_in, token_mods, lengths, target_rows, params):
    qkv_weight, qv_bias, attn_weight, tail_bias, up_weight, up_bias, down_weight, proj_in, proj_in_bias, proj_mid, proj_mid_bias, proj_out, proj_out_bias = params
    row_count = rows_in.shape[0]
    image_of, onehot = image_onehot(lengths, row_count)
    per_token = matmul_high(onehot, token_mods)
    shift_one, scale_one, gate_one, shift_two, scale_two, gate_two = jnp.split(per_token, 6, axis=1)
    first_in = low(layer_norm(rows_in) * (1.0 + scale_one) + shift_one)
    key_zero = jnp.zeros((D,), dtype=qv_bias.dtype)
    bias_full = jnp.concatenate([qv_bias[:D], key_zero, qv_bias[D:]])
    projected = low(low_back(matmul_high(first_in, qkv_weight.reshape(D, 3 * D)) + bias_full))
    queries = projected[:, :D].reshape(row_count, HEADS, HD)
    keys_all = projected[:, D:2 * D].reshape(row_count, HEADS, HD)
    values_all = projected[:, 2 * D:].reshape(row_count, HEADS, HD)
    raw_scores = low_back(jnp.einsum('qhd,khd->hqk', queries, keys_all, precision=PRECISE) * HD ** (-0.5))
    same_image = (image_of[:, None] == image_of[None, :])[None]
    masked = jnp.where(same_image, raw_scores, -1e+30)
    row_max = lax.optimization_barrier(jnp.max(masked, axis=-1, keepdims=True))
    exp_scores = jnp.exp(masked - row_max)
    attn_probs = exp_scores / lax.optimization_barrier(jnp.sum(exp_scores, axis=-1, keepdims=True))
    head_out = low(low_back(jnp.einsum('hqk,khd->qhd', low(attn_probs), values_all, precision=PRECISE)))
    head_out = head_out.reshape(row_count, D)
    branch_attn = low_back(matmul_high(head_out, attn_weight.reshape(D, D)) + tail_bias[:D])
    middle = rows_in + gate_one * branch_attn
    second_in = low(layer_norm(middle) * (1.0 + scale_two) + shift_two)
    up_pre = low_back(matmul_high(second_in, up_weight.reshape(D, FF)) + up_bias)
    up_act = low(gelu_tanh(up_pre))
    branch_mlp = low_back(matmul_high(up_act, down_weight.reshape(FF, D)) + tail_bias[D:])
    hidden = middle + gate_two * branch_mlp
    first_pre = low_back(matmul_high(low(hidden), proj_in.reshape(D, P_SIZE)) + proj_in_bias)
    first_act = low(sigmoid_linear(first_pre))
    second_pre = low_back(matmul_high(first_act, proj_mid.reshape(P_SIZE, P_SIZE)) + proj_mid_bias)
    second_act = low(sigmoid_linear(second_pre))
    features = low_back(matmul_high(second_act, proj_out.reshape(P_SIZE, Z)) + proj_out_bias)
    feature_norm = jnp.sqrt(lax.optimization_barrier(jnp.sum(features * features, axis=1)) + EPSILON)
    target_norm = jnp.sqrt(lax.optimization_barrier(jnp.sum(target_rows * target_rows, axis=1)) + EPSILON)
    cosine = lax.optimization_barrier(jnp.sum(features * target_rows, axis=1)) / (feature_norm * target_norm)
    return (hidden, -0.5 * jnp.sum(cosine))

def reference(tokens, cond, image_lengths, ada_weight, ada_bias, qkv_weight, qv_bias, attn_weight, tail_bias, up_weight, up_bias, down_weight, projector_in, projector_in_bias, projector_mid, projector_mid_bias, projector_out, projector_out_bias, targets, out_grad):
    stored_all = (ada_weight, ada_bias, qkv_weight, qv_bias, attn_weight, tail_bias, up_weight, up_bias, down_weight, projector_in, projector_in_bias, projector_mid, projector_mid_bias, projector_out, projector_out_bias)
    weights = tuple((stored.astype(jnp.float32) for stored in stored_all))
    target_values = targets.astype(jnp.float32)

    def forward(inputs, cond_values, params):
        modulation = low_back(matmul_high(low(sigmoid_linear(cond_values)), params[0].reshape(D, 6 * D)) + params[1])
        block_params = params[2:]

        def device_step(carry, sliced):
            rows_in, token_mods, lengths, target_rows = sliced
            hidden, loss_part = device_block(rows_in, token_mods, lengths, target_rows, block_params)
            return (carry + loss_part, hidden)
        sliced_all = (inputs.reshape(SHARDS, TOK_DEV, D), modulation.reshape(SHARDS, IMG_DEV, 6 * D), image_lengths, target_values.reshape(SHARDS, TOK_DEV, Z))
        loss_sum, hidden = lax.scan(jax.checkpoint(device_step), jnp.zeros((), jnp.float32), sliced_all)
        return (hidden.reshape(TOKENS, D), loss_sum)
    outputs, pullback = jax.vjp(forward, tokens.astype(jnp.float32), cond.astype(jnp.float32), weights)
    tokens_grad, cond_grad, grads = pullback((out_grad.astype(jnp.float32), jnp.ones((), jnp.float32)))
    return (outputs[0].astype(jnp.bfloat16), tokens_grad.astype(jnp.bfloat16), cond_grad.astype(jnp.bfloat16), grads[0], grads[1], grads[2], grads[3], grads[4], grads[5], grads[6], grads[7], grads[8], grads[9], grads[10], grads[11], grads[12], grads[13], grads[14])
```

```python
import functools

import jax
import jax.numpy as jnp
from jax import lax
from jax.experimental import pallas as pl
from jax.experimental.pallas import tpu as pltpu
from jax.sharding import PartitionSpec as P

D = 1152
HEADS = 16
HD = 72
FF = 4608
P_SIZE = 2048
Z = 768


EPSILON = 1e-06
PRECISE = lax.Precision.HIGHEST


def layer_norm(values):
    centred = values - jnp.mean(values, axis=-1, keepdims=True)
    spread = jnp.mean(centred * centred, axis=-1, keepdims=True)
    return centred * lax.rsqrt(spread + EPSILON)


def sigmoid_linear(values):
    return values * jax.nn.sigmoid(values)


def gelu_tanh(values):
    inner = 0.7978845608028654 * (values + 0.044715 * values * values * values)
    return 0.5 * values * (1.0 + jnp.tanh(inner))


def image_onehot(lengths, row_count):
    ends = jnp.cumsum(lengths)
    position = jnp.arange(row_count, dtype=jnp.int32)
    image_of = jnp.sum((position[:, None] >= ends[None, :]).astype(jnp.int32), axis=1)
    images = jnp.arange(lengths.shape[0], dtype=jnp.int32)
    return (image_of, (image_of[:, None] == images[None, :]).astype(jnp.float32))


def pull_back(function, point, cotangent):
    return jax.vjp(function, point)[1](cotangent)[0]


def lowered(values):
    return values.astype(jnp.bfloat16)


def matmul(left, right):
    return jnp.dot(left, right, preferred_element_type=jnp.float32)


def transposed_left(left, right):
    return lax.dot_general(
        left, right, (((0,), (0,)), ((), ())), preferred_element_type=jnp.float32
    )


def transposed_right(left, right):
    return lax.dot_general(
        left, right, (((1,), (1,)), ((), ())), preferred_element_type=jnp.float32
    )


def column_sums(values):
    return jnp.sum(values.astype(jnp.float32), axis=0)


def by_owner(values, owners):
    return values.reshape(owners, -1)


def flatten_all(pieces):
    return tuple((piece.reshape(-1) for piece in pieces))


def unpack_mix(gathered):
    return (
        gathered[0].reshape(D, 6 * D),
        gathered[1].astype(jnp.float32),
        gathered[2].reshape(D, 3 * D),
        gathered[3].astype(jnp.float32),
        gathered[4].reshape(D, D),
        gathered[5].astype(jnp.float32),
    )


def unpack_dense(gathered):
    return (
        gathered[0].reshape(D, FF),
        gathered[1].astype(jnp.float32),
        gathered[2].reshape(FF, D),
        gathered[3].reshape(D, P_SIZE),
        gathered[4].astype(jnp.float32),
        gathered[5].reshape(P_SIZE, P_SIZE),
        gathered[6].astype(jnp.float32),
        gathered[7].reshape(P_SIZE, Z),
        gathered[8].astype(jnp.float32),
    )


MESH = pl.DeviceIdType.MESH

class Place:
    def __init__(self, n):
        self.me = me = lax.axis_index("fsdp")
        self.Z = n // 8
        self.z, self.y, self.x, self.c = me // 8, (me // 4) % 2, (me // 2) % 2, me % 2
        self.xp = me + 2 - 4 * self.x
        self.yp = me + 4 - 8 * self.y
        self.cp = me + 1 - 2 * self.c

def barrier(pc):
    sem = pltpu.get_barrier_semaphore()
    for q in (pc.xp, pc.yp, pc.cp):
        pl.semaphore_signal(sem, inc=1, device_id=(q,), device_id_type=MESH)
    @pl.when(pc.z > 0)
    def _():
        pl.semaphore_signal(sem, inc=1, device_id=(pc.me - 8,), device_id_type=MESH)
    @pl.when(pc.z < pc.Z - 1)
    def _():
        pl.semaphore_signal(sem, inc=1, device_id=(pc.me + 8,), device_id_type=MESH)
    ends = (pc.z == 0).astype(jnp.int32) + (pc.z == pc.Z - 1).astype(jnp.int32)
    pl.semaphore_wait(sem, 5 - ends)

def region(out, quart, zs, y, x, c, off, w):
    if quart:
        q = out.shape[3] // 4
        col = pl.multiple_of((x * 2 + c) * q + off, 128)
        return out.at[zs, y, :, pl.ds(col, w)]
    return out.at[zs, y, x, c, :, pl.ds(off, w)]

def ag_kernel(n, quarts, rounds, offs, *refs):
    na = len(quarts)
    ins, outs = refs[:na], refs[na:2 * na]
    lsem, zs_sem, zr_sem, xs_sem, xr_sem, cs_sem, cr_sem = refs[2 * na:]
    pc = Place(n)
    Z = pc.Z
    z, y, x, c = pc.z, pc.y, pc.x, pc.c
    barrier(pc)
    def reg(r, zs, y_, x_, c_=None):
        a, off, w = rounds[r]
        return region(outs[a], quarts[a], zs, y_, x_, c if c_ is None else c_, off, w)
    def own_in(r):
        a, off, w = rounds[r]
        return ins[a].at[:, pl.ds(off, w)]
    def rcopy(src, dst, ss, rs, dev):
        return pltpu.make_async_remote_copy(src_ref=src, dst_ref=dst, send_sem=ss, recv_sem=rs, device_id=(dev,), device_id_type=MESH)
    def zcopy(r, side, s, src=None):
        org = z - s if side == 0 else z + s
        dst = reg(r, org, y, x)
        return rcopy(own_in(r) if s == 0 else dst, dst, zs_sem.at[r, side, s], zr_sem.at[r, side, s], pc.me + (8 if side == 0 else -8))
    def zrecv(r, side, s):
        org = z - 1 - s if side == 0 else z + 1 + s
        d = reg(r, org, y, x)
        rcopy(d, d, zs_sem.at[r, side, s], zr_sem.at[r, side, s], pc.me).wait_recv()
    def local(r):
        return pltpu.make_async_copy(own_in(r), reg(r, z, y, x), lsem.at[r])
    allz = slice(None); lo = slice(0, Z // 2); hi = slice(Z // 2, Z)
    def xy(r, k):
        if k == 0:
            d = reg(r, allz, y, x); return rcopy(d, d, xs_sem.at[r, 0], xr_sem.at[r, 0], pc.xp)
        if k == 1:
            d = reg(r, allz, y, x); return rcopy(d, d, xs_sem.at[r, 1], xr_sem.at[r, 1], pc.yp)
        if k == 2:
            d = reg(r, lo, y, 1 - x); return rcopy(d, d, xs_sem.at[r, 2], xr_sem.at[r, 2], pc.yp)
        d = reg(r, hi, 1 - y, x); return rcopy(d, d, xs_sem.at[r, 3], xr_sem.at[r, 3], pc.xp)
    def core(r, k):
        d = reg(r, allz, y if k in (0, 1) else 1 - y, x if k in (0, 2) else 1 - x)
        return rcopy(d, d, cs_sem.at[r, k], cr_sem.at[r, k], pc.cp)
    R = len(rounds)
    def zstart(r, s):
        @pl.when((z - s >= 0) & (z < Z - 1))
        def _(): zcopy(r, 0, s).start()
        @pl.when((z + s <= Z - 1) & (z > 0))
        def _(): zcopy(r, 1, s).start()
    def zwait(r, s):
        @pl.when(z - 1 - s >= 0)
        def _(): zrecv(r, 0, s)
        @pl.when(z + 1 + s <= Z - 1)
        def _(): zrecv(r, 1, s)
    def stage(r, s):
        if s == 0:
            local(r).start()
            zstart(r, 0)
        elif s < Z - 1:
            zwait(r, s - 1)
            zstart(r, s)
        elif s == Z - 1:
            zwait(r, s - 1)
            local(r).wait()
            xy(r, 0).start(); xy(r, 1).start(); core(r, 0).start()
        elif s == Z:
            xy(r, 0).wait_recv(); xy(r, 2).start(); core(r, 1).start()
            xy(r, 1).wait_recv(); xy(r, 3).start(); core(r, 2).start()
        elif s == Z + 1:
            xy(r, 2).wait_recv(); xy(r, 3).wait_recv(); core(r, 3).start()
        elif s == Z + 2:
            for k in range(4): core(r, k).wait_recv()
    S = Z + 3
    last = R - 1 + offs[S - 1]
    for t in range(last + 1):
        for s in reversed(range(S)):
            r = t - offs[s]
            if 0 <= r < R:
                stage(r, s)
    for r in range(R):
        for s in range(Z - 1):
            @pl.when((z - s >= 0) & (z < Z - 1))
            def _(): zcopy(r, 0, s).wait_send()
            @pl.when((z + s <= Z - 1) & (z > 0))
            def _(): zcopy(r, 1, s).wait_send()
        for k in range(4):
            xy(r, k).wait_send(); core(r, k).wait_send()

def all_gather(n, shards, quarts, rounds, offs, cid):
    Z = n // 8
    shapes = []
    for sh, qt in zip(shards, quarts):
        k, w = sh.shape
        shapes.append(jax.ShapeDtypeStruct((Z, 2, k, 4 * w) if qt else (Z, 2, 2, 2, k, w), sh.dtype))
    R = len(rounds)
    D = pltpu.SemaphoreType.DMA
    return pl.pallas_call(
        functools.partial(ag_kernel, n, quarts, rounds, offs),
        out_shape=shapes,
        in_specs=[pl.BlockSpec(memory_space=pltpu.HBM)] * len(shards),
        out_specs=[pl.BlockSpec(memory_space=pltpu.HBM)] * len(shards),
        scratch_shapes=[D((R,)), D((R, 2, Z - 1)), D((R, 2, Z - 1)), D((R, 4)), D((R, 4)), D((R, 4)), D((R, 4))],
        compiler_params=pltpu.CompilerParams(collective_id=cid, has_side_effects=True),
    )(*shards)


def rs_kernel(n, quarts, rounds, cls, slots, offs, *refs):
    na = len(quarts)
    ncls = len(slots)
    R = len(rounds)
    ins, outs = refs[:na], refs[na:2 * na]
    rest = list(refs[2 * na:])
    S0 = rest[:ncls]; rest = rest[ncls:]
    CR = rest[:ncls]; rest = rest[ncls:]
    XR = rest[:R]; rest = rest[R:]
    ZR = rest[:R]; rest = rest[R:]
    lsem, cs, cr, xs, xr, zs_, zr, credit = rest
    pc = Place(n)
    Z = pc.Z; H = Z // 2
    z, y, x, c = pc.z, pc.y, pc.x, pc.c
    barrier(pc)
    slot, seen = [], [0] * ncls
    prev = []
    for r in range(R):
        k = cls[r]
        slot.append(seen[k] % slots[k])
        prior = [q for q in range(r) if cls[q] == k and (slot[q] == seen[k] % slots[k])]
        prev.append(prior[-1] if prior else None)
        seen[k] += 1
    def rcopy(src, dst, ss, rs, dev):
        return pltpu.make_async_remote_copy(src_ref=src, dst_ref=dst, send_sem=ss, recv_sem=rs, device_id=(dev,), device_id_type=MESH)
    def s0(r): return S0[cls[r]].at[slot[r]]
    def crb(r): return CR[cls[r]].at[slot[r]]
    def src(r, x_, c_):
        a, off, w = rounds[r]
        return region(ins[a], quarts[a], slice(None), slice(None), x_, c_, off, w)
    def load(r, x_): return pltpu.make_async_copy(src(r, x_, c), s0(r).at[x_], lsem.at[r, x_])
    def core(r, x_): return rcopy(src(r, x_, 1 - c), crb(r).at[x_], cs.at[r, x_], cr.at[r, x_], pc.cp)
    def xy(r, k):
        b = s0(r)
        if k == 0: return rcopy(b.at[1 - x, 0:H, 1 - y], XR[r].at[0:H], xs.at[r, 0], xr.at[r, 0], pc.yp)
        if k == 1: return rcopy(b.at[1 - x, H:Z, 1 - y], XR[r].at[H:Z], xs.at[r, 1], xr.at[r, 1], pc.xp)
        if k == 2: return rcopy(b.at[1 - x, :, y], XR[r].at[Z:2 * Z], xs.at[r, 2], xr.at[r, 2], pc.xp)
        return rcopy(b.at[x, :, 1 - y], XR[r].at[2 * Z:3 * Z], xs.at[r, 3], xr.at[r, 3], pc.yp)
    def zc(r, side, d):
        return rcopy(XR[r].at[Z + d], ZR[r].at[side, d], zs_.at[r, side, d], zr.at[r, side, d], jnp.clip(pc.me + (8 if side == 0 else -8), 0, n - 1))
    def waits_send(r):
        for k in range(2): core(r, k).wait_send()
        for k in range(4): xy(r, k).wait_send()
    def zwaits_send(r):
        for d in range(Z):
            @pl.when(d > z)
            def _(): zc(r, 0, d).wait_send()
            @pl.when(d < z)
            def _(): zc(r, 1, d).wait_send()
    def zstep(r, s):
        for side in (0, 1):
            p = s if side == 0 else Z - 1 - s
            @pl.when(z == p)
            def _():
                for d in range(Z):
                    if (d > p) if side == 0 else (d < p):
                        if s > 0:
                            zc(r, side, d).wait_recv()
                            XR[r][Z + d] = XR[r][Z + d] + ZR[r][side, d]
                        zc(r, side, d).start()
    def stage(r, s):
        b, cb = s0(r), crb(r)
        if s == 0:
            if prev[r] is not None:
                waits_send(prev[r])
                pl.semaphore_wait(credit, 1)
            for k in range(2):
                core(r, k).start(); load(r, k).start()
        elif s == 1:
            for k in range(2):
                load(r, k).wait(); core(r, k).wait_recv()
            def add(i, _):
                xx, zz, yy = i // (2 * Z), (i // 2) % Z, i % 2
                b[xx, zz, yy] = b[xx, zz, yy] + cb[xx, zz, yy]
                return _
            lax.fori_loop(0, 4 * Z, add, 0)
            if any(prev[q] == r for q in range(R)):
                pl.semaphore_signal(credit, inc=1, device_id=(pc.cp,), device_id_type=MESH)
            xy(r, 0).start(); xy(r, 1).start()
        elif s == 2:
            xy(r, 0).wait_recv()
            def add(i, _):
                b[1 - x, i, y] = b[1 - x, i, y] + XR[r][i]
                return _
            lax.fori_loop(0, H, add, 0)
            xy(r, 2).start()
            xy(r, 1).wait_recv()
            def add(i, _):
                b[x, i, 1 - y] = b[x, i, 1 - y] + XR[r][i]
                return _
            lax.fori_loop(H, Z, add, 0)
            xy(r, 3).start()
        elif s == 3:
            xy(r, 2).wait_recv(); xy(r, 3).wait_recv()
            def add(i, _):
                XR[r][Z + i] = b[x, i, y] + XR[r][Z + i] + XR[r][2 * Z + i]
                return _
            lax.fori_loop(0, Z, add, 0)
            zstep(r, 0)
        elif s < Z + 2:
            zstep(r, s - 3)
        else:
            a, off, w = rounds[r]
            for d in range(Z):
                @pl.when(d == z)
                def _():
                    tot = XR[r][Z + d].astype(jnp.float32)
                    if d > 0:
                        zc(r, 0, d).wait_recv()
                        tot = tot + ZR[r][0, d].astype(jnp.float32)
                    if d < Z - 1:
                        zc(r, 1, d).wait_recv()
                        tot = tot + ZR[r][1, d].astype(jnp.float32)
                    outs[a][:, off:off + w] = tot
    S = Z + 3
    last = R - 1 + offs[S - 1]
    for t in range(last + 1):
        for s in reversed(range(S)):
            r = t - offs[s]
            if 0 <= r < R:
                stage(r, s)
    for r in range(R):
        zwaits_send(r)
        if not any(prev[q] == r for q in range(R)):
            waits_send(r)

def reduce_scatter(n, grads, quarts, rounds, cls, slots, offs, cid):
    Z = n // 8
    shapes, R = [], len(rounds)
    for g, qt in zip(grads, quarts):
        shapes.append(jax.ShapeDtypeStruct((g.shape[2], g.shape[3] // 4) if qt else g.shape[4:], jnp.float32))
    dims = []
    for a, off, w in rounds:
        dims.append((shapes[a].shape[0], w))
    cdims = [next(dims[r] for r in range(R) if cls[r] == k) for k in range(len(slots))]
    for r in range(R): assert dims[r] == cdims[cls[r]], (r, dims[r], cdims)
    D = pltpu.SemaphoreType.DMA
    bf = jnp.bfloat16
    scratch = [pltpu.VMEM((slots[k], 2, Z, 2) + cdims[k], bf) for k in range(len(slots))] * 2
    scratch += [pltpu.VMEM((3 * Z,) + dims[r], bf) for r in range(R)]
    scratch += [pltpu.VMEM((2, Z) + dims[r], bf) for r in range(R)]
    scratch += [D((R, 2)), D((R, 2)), D((R, 2)), D((R, 4)), D((R, 4)), D((R, 2, Z)), D((R, 2, Z)), pltpu.SemaphoreType.REGULAR]
    return pl.pallas_call(
        functools.partial(rs_kernel, n, quarts, rounds, cls, slots, offs),
        out_shape=shapes,
        in_specs=[pl.BlockSpec(memory_space=pltpu.HBM)] * len(grads),
        out_specs=[pl.BlockSpec(memory_space=pltpu.VMEM)] * len(grads),
        scratch_shapes=scratch,
        compiler_params=pltpu.CompilerParams(collective_id=cid, has_side_effects=True, vmem_limit_bytes=62 * 2**20),
    )(*grads)

GATHER_ROUNDS = ((0, 0, 128),) + tuple(
    (array, at * width, width)
    for array, width, count in ((1, 384, 3), (2, 384, 3), (3, 384, 3), (4, 512, 1), (5, 1024, 2), (6, 768, 1))
    for at in range(count)
)
SCATTER_ROUNDS = tuple(
    (array, at * width, width)
    for array, width, count in ((0, 768, 1), (1, 1024, 2), (2, 512, 1), (3, 384, 3), (4, 384, 3), (5, 384, 3), (6, 128, 1))
    for at in range(count)
)
SCATTER_CLASSES = (0, 1, 1, 2, 3, 3, 3, 3, 3, 3, 3, 3, 3, 4)
SCATTER_SLOTS = (1, 2, 1, 3, 1)


def per_device(
    tokens,
    cond,
    image_lengths,
    ada_weight,
    ada_bias,
    qkv_weight,
    qv_bias,
    attn_weight,
    tail_bias,
    up_weight,
    up_bias,
    down_weight,
    projector_in,
    projector_in_bias,
    projector_mid,
    projector_mid_bias,
    projector_out,
    projector_out_bias,
    targets,
    out_grad,
):
    owners = lax.axis_size("fsdp")
    mix_gathered = (
        lax.all_gather(ada_weight, "fsdp", axis=0, tiled=True),
        lax.all_gather(ada_bias, "fsdp", axis=0, tiled=True),
        lax.all_gather(qkv_weight, "fsdp", axis=0, tiled=True),
        lax.all_gather(qv_bias, "fsdp", axis=0, tiled=True),
        lax.all_gather(attn_weight, "fsdp", axis=0, tiled=True),
        lax.all_gather(tail_bias, "fsdp", axis=0, tiled=True),
    )
    mix_full = unpack_mix(mix_gathered)
    ada_full, ada_bias_full, qkv_full, qv_full, attn_full, tail_full = mix_full
    row_count = tokens.shape[0]
    cond_values = cond.astype(jnp.float32)
    cond_low = lowered(sigmoid_linear(cond_values))
    modulation = matmul(cond_low, ada_full) + ada_bias_full
    image_of, onehot = image_onehot(image_lengths[0], row_count)
    per_token = jnp.dot(onehot, modulation, precision=PRECISE)
    shift_one, scale_one, gate_one, shift_two, scale_two, gate_two = jnp.split(per_token, 6, axis=1)
    inputs = tokens.astype(jnp.float32)
    normed_one = layer_norm(inputs)
    first_in = lowered(normed_one * (1.0 + scale_one) + shift_one)
    key_zero = jnp.zeros((D,), jnp.float32)
    bias_full = jnp.concatenate([qv_full[:D], key_zero, qv_full[D:]])
    projected = lowered(matmul(first_in, qkv_full) + bias_full)
    queries = projected[:, :D].reshape(row_count, HEADS, HD)
    keys_all = projected[:, D : 2 * D].reshape(row_count, HEADS, HD)
    values_all = projected[:, 2 * D :].reshape(row_count, HEADS, HD)
    same_image = (image_of[:, None] == image_of[None, :])[None]
    score_scale = HD ** (-0.5)

    def masked_scores():
        raw_scores = (
            jnp.einsum("qhd,khd->hqk", queries, keys_all, preferred_element_type=jnp.float32)
            * score_scale
        )
        return jnp.where(same_image, raw_scores, -1e30)

    masked = masked_scores()
    row_max = jnp.max(masked, axis=-1, keepdims=True)
    exp_scores = jnp.exp(masked - row_max)
    row_total = jnp.sum(exp_scores, axis=-1, keepdims=True)
    attn_probs = exp_scores / row_total
    head_out = jnp.einsum(
        "hqk,khd->qhd", lowered(attn_probs), values_all, preferred_element_type=jnp.float32
    )
    heads_low = lowered(head_out.reshape(row_count, D))
    branch_attn = matmul(heads_low, attn_full) + tail_full[:D]
    middle = inputs + gate_one * branch_attn
    normed_two = layer_norm(middle)
    second_in = lowered(normed_two * (1.0 + scale_two) + shift_two)
    dense_gathered = (
        lax.all_gather(up_weight, "fsdp", axis=0, tiled=True),
        lax.all_gather(up_bias, "fsdp", axis=0, tiled=True),
        lax.all_gather(down_weight, "fsdp", axis=0, tiled=True),
        lax.all_gather(projector_in, "fsdp", axis=0, tiled=True),
        lax.all_gather(projector_in_bias, "fsdp", axis=0, tiled=True),
        lax.all_gather(projector_mid, "fsdp", axis=0, tiled=True),
        lax.all_gather(projector_mid_bias, "fsdp", axis=0, tiled=True),
        lax.all_gather(projector_out, "fsdp", axis=0, tiled=True),
        lax.all_gather(projector_out_bias, "fsdp", axis=0, tiled=True),
    )
    dense_full = unpack_dense(dense_gathered)
    (
        up_full,
        up_bias_full,
        down_full,
        proj_in_full,
        proj_in_bias_full,
        proj_mid_full,
        proj_mid_bias_full,
        proj_out_full,
        proj_out_bias_full,
    ) = dense_full
    up_pre = matmul(second_in, up_full) + up_bias_full
    up_act = lowered(gelu_tanh(up_pre))
    branch_mlp = matmul(up_act, down_full) + tail_full[D:]
    hidden = middle + gate_two * branch_mlp
    mixed = lowered(hidden)
    first_pre = matmul(mixed, proj_in_full) + proj_in_bias_full
    first_act = lowered(sigmoid_linear(first_pre))
    second_pre = matmul(first_act, proj_mid_full) + proj_mid_bias_full
    second_act = lowered(sigmoid_linear(second_pre))
    features = matmul(second_act, proj_out_full) + proj_out_bias_full
    target_values = targets.astype(jnp.float32)

    def cosine_loss(values):
        value_norm = jnp.sqrt(jnp.sum(values * values, axis=1) + EPSILON)
        target_norm = jnp.sqrt(jnp.sum(target_values * target_values, axis=1) + EPSILON)
        return -0.5 * jnp.sum(jnp.sum(values * target_values, axis=1) / (value_norm * target_norm))

    feature_grad = lowered(jax.grad(cosine_loss)(features))
    dense_again = (
        lax.all_gather(up_weight, "fsdp", axis=0, tiled=True),
        lax.all_gather(up_bias, "fsdp", axis=0, tiled=True),
        lax.all_gather(down_weight, "fsdp", axis=0, tiled=True),
        lax.all_gather(projector_in, "fsdp", axis=0, tiled=True),
        lax.all_gather(projector_in_bias, "fsdp", axis=0, tiled=True),
        lax.all_gather(projector_mid, "fsdp", axis=0, tiled=True),
        lax.all_gather(projector_mid_bias, "fsdp", axis=0, tiled=True),
        lax.all_gather(projector_out, "fsdp", axis=0, tiled=True),
        lax.all_gather(projector_out_bias, "fsdp", axis=0, tiled=True),
    )
    dense_back = unpack_dense(dense_again)
    up_back = dense_back[0]
    down_back = dense_back[2]
    proj_in_back = dense_back[3]
    proj_mid_back = dense_back[5]
    proj_out_back = dense_back[7]
    grad_proj_out = transposed_left(second_act, feature_grad)
    second_back = lowered(
        pull_back(sigmoid_linear, second_pre, transposed_right(feature_grad, proj_out_back))
    )
    grad_proj_mid = transposed_left(first_act, second_back)
    first_back = lowered(
        pull_back(sigmoid_linear, first_pre, transposed_right(second_back, proj_mid_back))
    )
    grad_proj_in = transposed_left(mixed, first_back)
    hidden_grad = out_grad.astype(jnp.float32) + transposed_right(first_back, proj_in_back)
    gate_two_grad = hidden_grad * branch_mlp
    branch_mlp_grad = lowered(hidden_grad * gate_two)
    grad_down = transposed_left(up_act, branch_mlp_grad)
    up_grad = lowered(pull_back(gelu_tanh, up_pre, transposed_right(branch_mlp_grad, down_back)))
    grad_up = transposed_left(second_in, up_grad)
    second_in_grad = transposed_right(up_grad, up_back)
    middle_grad = hidden_grad + pull_back(layer_norm, middle, second_in_grad * (1.0 + scale_two))
    up_rows = by_owner(grad_up, owners)
    up_bias_rows = by_owner(column_sums(up_grad), owners)
    down_rows = by_owner(grad_down, owners)
    proj_in_rows = by_owner(grad_proj_in, owners)
    proj_in_sums = by_owner(column_sums(first_back), owners)
    proj_mid_rows = by_owner(grad_proj_mid, owners)
    proj_mid_sums = by_owner(column_sums(second_back), owners)
    proj_out_rows = by_owner(grad_proj_out, owners)
    proj_out_sums = by_owner(column_sums(feature_grad), owners)
    dense_grads = flatten_all(
        (
            lax.psum_scatter(up_rows, "fsdp", scatter_dimension=0, tiled=True),
            lax.psum_scatter(up_bias_rows, "fsdp", scatter_dimension=0, tiled=True),
            lax.psum_scatter(down_rows, "fsdp", scatter_dimension=0, tiled=True),
            lax.psum_scatter(proj_in_rows, "fsdp", scatter_dimension=0, tiled=True),
            lax.psum_scatter(proj_in_sums, "fsdp", scatter_dimension=0, tiled=True),
            lax.psum_scatter(proj_mid_rows, "fsdp", scatter_dimension=0, tiled=True),
            lax.psum_scatter(proj_mid_sums, "fsdp", scatter_dimension=0, tiled=True),
            lax.psum_scatter(proj_out_rows, "fsdp", scatter_dimension=0, tiled=True),
            lax.psum_scatter(proj_out_sums, "fsdp", scatter_dimension=0, tiled=True),
        )
    )
    mix_again = (
        lax.all_gather(ada_weight, "fsdp", axis=0, tiled=True),
        lax.all_gather(ada_bias, "fsdp", axis=0, tiled=True),
        lax.all_gather(qkv_weight, "fsdp", axis=0, tiled=True),
        lax.all_gather(qv_bias, "fsdp", axis=0, tiled=True),
        lax.all_gather(attn_weight, "fsdp", axis=0, tiled=True),
        lax.all_gather(tail_bias, "fsdp", axis=0, tiled=True),
    )
    mix_back = unpack_mix(mix_again)
    ada_back = mix_back[0]
    qkv_back = mix_back[2]
    attn_back = mix_back[4]
    gate_one_grad = middle_grad * branch_attn
    branch_attn_grad = lowered(middle_grad * gate_one)
    grad_attn = transposed_left(heads_low, branch_attn_grad)
    heads_grad = lowered(transposed_right(branch_attn_grad, attn_back)).reshape(
        row_count, HEADS, HD
    )
    again_probs = jnp.exp(masked_scores() - row_max) / row_total
    prob_grad = jnp.einsum(
        "qhd,khd->hqk", heads_grad, values_all, preferred_element_type=jnp.float32
    )
    value_grad = jnp.einsum(
        "hqk,qhd->khd", lowered(again_probs), heads_grad, preferred_element_type=jnp.float32
    )
    score_grad = lowered(
        again_probs * (prob_grad - jnp.sum(again_probs * prob_grad, axis=-1, keepdims=True))
    )
    query_grad = (
        jnp.einsum("hqk,khd->qhd", score_grad, keys_all, preferred_element_type=jnp.float32)
        * score_scale
    )
    key_grad = (
        jnp.einsum("hqk,qhd->khd", score_grad, queries, preferred_element_type=jnp.float32)
        * score_scale
    )
    projected_grad = lowered(
        jnp.concatenate(
            [
                query_grad.reshape(row_count, D),
                key_grad.reshape(row_count, D),
                value_grad.reshape(row_count, D),
            ],
            axis=1,
        )
    )
    grad_qkv = transposed_left(first_in, projected_grad)
    projected_sums = column_sums(projected_grad)
    grad_qv_bias = jnp.concatenate([projected_sums[:D], projected_sums[2 * D :]])
    first_in_grad = transposed_right(projected_grad, qkv_back)
    input_grad = middle_grad + pull_back(layer_norm, inputs, first_in_grad * (1.0 + scale_one))
    token_mod_grad = jnp.concatenate(
        [
            first_in_grad,
            first_in_grad * normed_one,
            gate_one_grad,
            second_in_grad,
            second_in_grad * normed_two,
            gate_two_grad,
        ],
        axis=1,
    )
    modulation_grad = lowered(
        lax.dot_general(onehot, token_mod_grad, (((0,), (0,)), ((), ())), precision=PRECISE)
    )
    grad_ada = transposed_left(cond_low, modulation_grad)
    cond_grad = pull_back(
        sigmoid_linear, cond_values, transposed_right(modulation_grad, ada_back)
    ).astype(jnp.bfloat16)
    grad_tail = jnp.concatenate([column_sums(branch_attn_grad), column_sums(branch_mlp_grad)])
    ada_rows = by_owner(grad_ada, owners)
    ada_sums = by_owner(column_sums(modulation_grad), owners)
    qkv_rows = by_owner(grad_qkv, owners)
    qv_rows = by_owner(grad_qv_bias, owners)
    attn_rows = by_owner(grad_attn, owners)
    tail_rows = by_owner(grad_tail, owners)
    mix_grads = flatten_all(
        (
            lax.psum_scatter(ada_rows, "fsdp", scatter_dimension=0, tiled=True),
            lax.psum_scatter(ada_sums, "fsdp", scatter_dimension=0, tiled=True),
            lax.psum_scatter(qkv_rows, "fsdp", scatter_dimension=0, tiled=True),
            lax.psum_scatter(qv_rows, "fsdp", scatter_dimension=0, tiled=True),
            lax.psum_scatter(attn_rows, "fsdp", scatter_dimension=0, tiled=True),
            lax.psum_scatter(tail_rows, "fsdp", scatter_dimension=0, tiled=True),
        )
    )
    return (
        mixed,
        input_grad.astype(jnp.bfloat16),
        cond_grad,
        mix_grads[0],
        mix_grads[1],
        mix_grads[2],
        mix_grads[3],
        mix_grads[4],
        mix_grads[5],
        dense_grads[0],
        dense_grads[1],
        dense_grads[2],
        dense_grads[3],
        dense_grads[4],
        dense_grads[5],
        dense_grads[6],
        dense_grads[7],
        dense_grads[8],
    )


def per_device_kernels(
    tokens,
    cond,
    image_lengths,
    ada_weight,
    ada_bias,
    qkv_weight,
    qv_bias,
    attn_weight,
    tail_bias,
    up_weight,
    up_bias,
    down_weight,
    projector_in,
    projector_in_bias,
    projector_mid,
    projector_mid_bias,
    projector_out,
    projector_out_bias,
    targets,
    out_grad,
):
    owners = lax.axis_size("fsdp")
    me = lax.axis_index("fsdp")
    groups = [[4 * g + i for i in range(4)] for g in range(owners // 4)]
    row_count = tokens.shape[0]
    rows = D // owners
    row_sharded = jnp.concatenate(
        [
            qkv_weight.reshape(rows, 3 * D),
            attn_weight.reshape(rows, D),
            up_weight.reshape(rows, FF),
            projector_in.reshape(rows, P_SIZE),
        ],
        axis=1,
    )
    quarters = jnp.concatenate(
        [part.reshape(rows, 4, -1) for part in jnp.split(row_sharded, (4 * D, 8 * D), axis=1)], axis=2
    ).transpose(1, 0, 2)
    quarters = lax.all_to_all(
        quarters, "fsdp", 0, 0, axis_index_groups=groups, tiled=True
    ).reshape(4 * rows, -1)
    bias_row = jnp.concatenate(
        [ada_bias, qv_bias, tail_bias, up_bias, projector_in_bias, projector_mid_bias, projector_out_bias]
    )
    bias_width = bias_row.shape[0]
    bias_row = jnp.pad(bias_row, (0, 2048 - bias_width)).reshape(16, 128)
    gathered = all_gather(
        owners,
        (
            bias_row,
            quarters[:, :D],
            quarters[:, D : 2 * D],
            down_weight.reshape(-1, D),
            quarters[:, 2 * D :],
            projector_mid.reshape(-1, P_SIZE),
            projector_out.reshape(-1, Z),
        ),
        (False, True, True, False, True, False, False),
        GATHER_ROUNDS,
        (0, 1, 2, 3, 5, 7, 8),
        1,
    )
    bias_all = gathered[0].reshape(owners, 2048)[:, :bias_width].astype(jnp.float32)
    widths = (6 * D, 2 * D, 2 * D, FF, P_SIZE, P_SIZE, Z)
    ends, at = [], 0
    for width in widths:
        at += width // owners
        ends.append(at)
    (
        ada_bias_full, qv_full, tail_full, up_bias_full, proj_in_bias_full, proj_mid_bias_full, proj_out_bias_full
    ) = [part.reshape(-1) for part in jnp.split(bias_all, ends[:-1], axis=1)]
    first_full = gathered[1].reshape(D, 4 * D)
    qkv_full, attn_full = first_full[:, : 3 * D], first_full[:, 3 * D :]
    up_full = gathered[2].reshape(D, FF)
    down_full = gathered[3].reshape(FF, D)
    proj_in_full = gathered[4].reshape(D, P_SIZE)
    proj_mid_full = gathered[5].reshape(P_SIZE, P_SIZE)
    proj_out_full = gathered[6].reshape(P_SIZE, Z)
    cond_values = cond.astype(jnp.float32)
    cond_low = lowered(sigmoid_linear(cond_values))
    cond_all = lax.all_gather(cond_low, "fsdp", axis=0, tiled=True)
    cond_mine = lax.dynamic_slice(cond_all, (0, me * rows), (cond_all.shape[0], rows))
    ada_mine = ada_weight.reshape(rows, 6 * D)
    modulation = (
        lax.psum_scatter(matmul(cond_mine, ada_mine), "fsdp", scatter_dimension=0, tiled=True)
        + ada_bias_full
    )
    image_of, onehot = image_onehot(image_lengths[0], row_count)
    per_token = jnp.dot(onehot, modulation, precision=PRECISE)
    shift_one, scale_one, gate_one, shift_two, scale_two, gate_two = jnp.split(per_token, 6, axis=1)
    inputs = tokens.astype(jnp.float32)
    normed_one = layer_norm(inputs)
    first_in = lowered(normed_one * (1.0 + scale_one) + shift_one)
    key_zero = jnp.zeros((D,), jnp.float32)
    bias_full = jnp.concatenate([qv_full[:D], key_zero, qv_full[D:]])
    projected = lowered(matmul(first_in, qkv_full) + bias_full)
    queries = projected[:, :D].reshape(row_count, HEADS, HD)
    keys_all = projected[:, D : 2 * D].reshape(row_count, HEADS, HD)
    values_all = projected[:, 2 * D :].reshape(row_count, HEADS, HD)
    same_image = (image_of[:, None] == image_of[None, :])[None]
    score_scale = HD ** (-0.5)

    def masked_scores():
        raw_scores = (
            jnp.einsum("qhd,khd->hqk", queries, keys_all, preferred_element_type=jnp.float32)
            * score_scale
        )
        return jnp.where(same_image, raw_scores, -1e30)

    masked = masked_scores()
    row_max = jnp.max(masked, axis=-1, keepdims=True)
    exp_scores = jnp.exp(masked - row_max)
    row_total = jnp.sum(exp_scores, axis=-1, keepdims=True)
    attn_probs = exp_scores / row_total
    head_out = jnp.einsum(
        "hqk,khd->qhd", lowered(attn_probs), values_all, preferred_element_type=jnp.float32
    )
    heads_low = lowered(head_out.reshape(row_count, D))
    branch_attn = matmul(heads_low, attn_full) + tail_full[:D]
    middle = inputs + gate_one * branch_attn
    normed_two = layer_norm(middle)
    second_in = lowered(normed_two * (1.0 + scale_two) + shift_two)
    up_pre = matmul(second_in, up_full) + up_bias_full
    up_act = lowered(gelu_tanh(up_pre))
    branch_mlp = matmul(up_act, down_full) + tail_full[D:]
    hidden = middle + gate_two * branch_mlp
    mixed = lowered(hidden)
    first_pre = matmul(mixed, proj_in_full) + proj_in_bias_full
    first_act = lowered(sigmoid_linear(first_pre))
    second_pre = matmul(first_act, proj_mid_full) + proj_mid_bias_full
    second_act = lowered(sigmoid_linear(second_pre))
    features = matmul(second_act, proj_out_full) + proj_out_bias_full
    target_values = targets.astype(jnp.float32)

    def cosine_loss(values):
        value_norm = jnp.sqrt(jnp.sum(values * values, axis=1) + EPSILON)
        target_norm = jnp.sqrt(jnp.sum(target_values * target_values, axis=1) + EPSILON)
        return -0.5 * jnp.sum(jnp.sum(values * target_values, axis=1) / (value_norm * target_norm))

    feature_grad = lowered(jax.grad(cosine_loss)(features))
    grad_proj_out = transposed_left(second_act, feature_grad)
    second_back = lowered(
        pull_back(sigmoid_linear, second_pre, transposed_right(feature_grad, proj_out_full))
    )
    grad_proj_mid = transposed_left(first_act, second_back)
    first_back = lowered(
        pull_back(sigmoid_linear, first_pre, transposed_right(second_back, proj_mid_full))
    )
    grad_proj_in = transposed_left(mixed, first_back)
    hidden_grad = out_grad.astype(jnp.float32) + transposed_right(first_back, proj_in_full)
    gate_two_grad = hidden_grad * branch_mlp
    branch_mlp_grad = lowered(hidden_grad * gate_two)
    grad_down = transposed_left(up_act, branch_mlp_grad)
    up_grad = lowered(pull_back(gelu_tanh, up_pre, transposed_right(branch_mlp_grad, down_full)))
    grad_up = transposed_left(second_in, up_grad)
    second_in_grad = transposed_right(up_grad, up_full)
    middle_grad = hidden_grad + pull_back(layer_norm, middle, second_in_grad * (1.0 + scale_two))
    gate_one_grad = middle_grad * branch_attn
    branch_attn_grad = lowered(middle_grad * gate_one)
    grad_attn = transposed_left(heads_low, branch_attn_grad)
    heads_grad = lowered(transposed_right(branch_attn_grad, attn_full)).reshape(
        row_count, HEADS, HD
    )
    again_probs = jnp.exp(masked_scores() - row_max) / row_total
    prob_grad = jnp.einsum(
        "qhd,khd->hqk", heads_grad, values_all, preferred_element_type=jnp.float32
    )
    value_grad = jnp.einsum(
        "hqk,qhd->khd", lowered(again_probs), heads_grad, preferred_element_type=jnp.float32
    )
    score_grad = lowered(
        again_probs * (prob_grad - jnp.sum(again_probs * prob_grad, axis=-1, keepdims=True))
    )
    query_grad = (
        jnp.einsum("hqk,khd->qhd", score_grad, keys_all, preferred_element_type=jnp.float32)
        * score_scale
    )
    key_grad = (
        jnp.einsum("hqk,qhd->khd", score_grad, queries, preferred_element_type=jnp.float32)
        * score_scale
    )
    projected_grad = lowered(
        jnp.concatenate(
            [
                query_grad.reshape(row_count, D),
                key_grad.reshape(row_count, D),
                value_grad.reshape(row_count, D),
            ],
            axis=1,
        )
    )
    grad_qkv = transposed_left(first_in, projected_grad)
    projected_sums = column_sums(projected_grad)
    grad_qv_bias = jnp.concatenate([projected_sums[:D], projected_sums[2 * D :]])
    first_in_grad = transposed_right(projected_grad, qkv_full)
    input_grad = middle_grad + pull_back(layer_norm, inputs, first_in_grad * (1.0 + scale_one))
    token_mod_grad = jnp.concatenate(
        [
            first_in_grad,
            first_in_grad * normed_one,
            gate_one_grad,
            second_in_grad,
            second_in_grad * normed_two,
            gate_two_grad,
        ],
        axis=1,
    )
    modulation_grad = lowered(
        lax.dot_general(onehot, token_mod_grad, (((0,), (0,)), ((), ())), precision=PRECISE)
    )
    modulation_all = lax.all_gather(modulation_grad, "fsdp", axis=0, tiled=True)
    grad_ada = transposed_left(cond_mine, modulation_all)
    cond_back = transposed_right(modulation_all, ada_mine)
    cond_back = lax.all_to_all(cond_back, "fsdp", 0, 1, tiled=True)
    cond_grad = pull_back(sigmoid_linear, cond_values, cond_back).astype(jnp.bfloat16)
    grad_ada_bias = lax.dynamic_slice(
        column_sums(modulation_all), (me * (6 * D // owners),), (6 * D // owners,)
    )
    grad_tail = jnp.concatenate([column_sums(branch_attn_grad), column_sums(branch_mlp_grad)])
    bias_grads = jnp.concatenate(
        [
            by_owner(part, owners)
            for part in (
                grad_qv_bias,
                grad_tail,
                column_sums(up_grad),
                column_sums(first_back),
                column_sums(second_back),
                column_sums(feature_grad),
            )
        ],
        axis=1,
    )
    bias_grads = jnp.pad(bias_grads, ((0, 0), (0, 2048 - bias_grads.shape[1])))
    lines = owners // 8
    summed = reduce_scatter(
        owners,
        (
            lowered(grad_proj_out).reshape(lines, 2, 2, 2, -1, Z),
            lowered(grad_proj_mid).reshape(lines, 2, 2, 2, -1, P_SIZE),
            lowered(grad_proj_in).reshape(lines, 2, -1, P_SIZE),
            lowered(grad_down).reshape(lines, 2, 2, 2, -1, D),
            lowered(grad_up).reshape(lines, 2, -1, FF),
            jnp.concatenate([lowered(grad_qkv), lowered(grad_attn)], axis=1).reshape(lines, 2, -1, 4 * D),
            lowered(bias_grads).reshape(lines, 2, 2, 2, 16, 128),
        ),
        (False, False, True, False, True, True, False),
        SCATTER_ROUNDS,
        SCATTER_CLASSES,
        SCATTER_SLOTS,
        (0, 1, 2, 3, 4, 5, 6),
        2,
    )
    back = jnp.concatenate([summed[5], summed[4], summed[2]], axis=1)
    back = lax.all_to_all(back, "fsdp", 0, 0, axis_index_groups=groups, tiled=True)
    back = back.reshape(4, rows, -1).transpose(1, 0, 2)
    first_rows = back[:, :, :D].reshape(rows, 4 * D)
    up_rows = back[:, :, D : 2 * D].reshape(-1)
    proj_in_rows = back[:, :, 2 * D :].reshape(-1)
    small = summed[6].reshape(-1)
    small_parts, at = [], 0
    for width in widths[1:]:
        small_parts.append(small[at : at + width // owners])
        at += width // owners
    qv_sum, tail_sum, up_bias_sum, in_sum, mid_sum, out_sum = small_parts
    return (
        mixed,
        input_grad.astype(jnp.bfloat16),
        cond_grad,
        grad_ada.reshape(-1),
        grad_ada_bias,
        first_rows[:, : 3 * D].reshape(-1),
        qv_sum,
        first_rows[:, 3 * D :].reshape(-1),
        tail_sum,
        up_rows,
        up_bias_sum,
        summed[3].reshape(-1),
        proj_in_rows,
        in_sum,
        summed[1].reshape(-1),
        mid_sum,
        summed[0].reshape(-1),
        out_sum,
    )


def solution(mesh):
    in_specs = (
        P("fsdp", None),
        P("fsdp", None),
        P("fsdp", None),
        P("fsdp"),
        P("fsdp"),
        P("fsdp"),
        P("fsdp"),
        P("fsdp"),
        P("fsdp"),
        P("fsdp"),
        P("fsdp"),
        P("fsdp"),
        P("fsdp"),
        P("fsdp"),
        P("fsdp"),
        P("fsdp"),
        P("fsdp"),
        P("fsdp"),
        P("fsdp", None),
        P("fsdp", None),
    )
    out_specs = (
        P("fsdp", None),
        P("fsdp", None),
        P("fsdp", None),
        P("fsdp"),
        P("fsdp"),
        P("fsdp"),
        P("fsdp"),
        P("fsdp"),
        P("fsdp"),
        P("fsdp"),
        P("fsdp"),
        P("fsdp"),
        P("fsdp"),
        P("fsdp"),
        P("fsdp"),
        P("fsdp"),
        P("fsdp"),
        P("fsdp"),
    )
    owners = mesh.shape["fsdp"]
    program = per_device_kernels if owners % 16 == 0 and D % owners == 0 else per_device
    return jax.shard_map(
        program, mesh=mesh, in_specs=in_specs, out_specs=out_specs, check_vma=False
    )
```

```python
import functools

import jax
import jax.numpy as jnp
from jax import lax
from jax.experimental import pallas as pl
from jax.experimental.pallas import tpu as pltpu
from jax.sharding import PartitionSpec as P

D = 1152
HEADS = 16
HD = 72
FF = 4608
P_SIZE = 2048
Z = 768
Z_OUT = Z


EPSILON = 1e-06
PRECISE = lax.Precision.HIGHEST


def layer_norm(values):
    centred = values - jnp.mean(values, axis=-1, keepdims=True)
    spread = jnp.mean(centred * centred, axis=-1, keepdims=True)
    return centred * lax.rsqrt(spread + EPSILON)


def sigmoid_linear(values):
    return values * jax.nn.sigmoid(values)


def gelu_tanh(values):
    inner = 0.7978845608028654 * (values + 0.044715 * values * values * values)
    return 0.5 * values * (1.0 + jnp.tanh(inner))


def image_onehot(lengths, row_count):
    ends = jnp.cumsum(lengths)
    position = jnp.arange(row_count, dtype=jnp.int32)
    image_of = jnp.sum((position[:, None] >= ends[None, :]).astype(jnp.int32), axis=1)
    images = jnp.arange(lengths.shape[0], dtype=jnp.int32)
    return (image_of, (image_of[:, None] == images[None, :]).astype(jnp.float32))


def pull_back(function, point, cotangent):
    return jax.vjp(function, point)[1](cotangent)[0]


def lowered(values):
    return values.astype(jnp.bfloat16)


def matmul(left, right):
    return jnp.dot(left, right, preferred_element_type=jnp.float32)


def transposed_left(left, right):
    return lax.dot_general(
        left, right, (((0,), (0,)), ((), ())), preferred_element_type=jnp.float32
    )


def transposed_right(left, right):
    return lax.dot_general(
        left, right, (((1,), (1,)), ((), ())), preferred_element_type=jnp.float32
    )


def column_sums(values):
    return jnp.sum(values.astype(jnp.float32), axis=0)


def by_owner(values, owners):
    return values.reshape(owners, -1)


def flatten_all(pieces):
    return tuple((piece.reshape(-1) for piece in pieces))


def unpack_mix(gathered):
    return (
        gathered[0].reshape(D, 6 * D),
        gathered[1].astype(jnp.float32),
        gathered[2].reshape(D, 3 * D),
        gathered[3].astype(jnp.float32),
        gathered[4].reshape(D, D),
        gathered[5].astype(jnp.float32),
    )


def unpack_dense(gathered):
    return (
        gathered[0].reshape(D, FF),
        gathered[1].astype(jnp.float32),
        gathered[2].reshape(FF, D),
        gathered[3].reshape(D, P_SIZE),
        gathered[4].astype(jnp.float32),
        gathered[5].reshape(P_SIZE, P_SIZE),
        gathered[6].astype(jnp.float32),
        gathered[7].reshape(P_SIZE, Z),
        gathered[8].astype(jnp.float32),
    )


MESH = pl.DeviceIdType.MESH

class Place:
    def __init__(self, n):
        self.me = me = lax.axis_index("fsdp")
        self.Z = n // 8
        self.z, self.y, self.x, self.c = me // 8, (me // 4) % 2, (me // 2) % 2, me % 2
        self.xp = me + 2 - 4 * self.x
        self.yp = me + 4 - 8 * self.y
        self.cp = me + 1 - 2 * self.c

def barrier(pc):
    sem = pltpu.get_barrier_semaphore()
    for q in (pc.xp, pc.yp, pc.cp):
        pl.semaphore_signal(sem, inc=1, device_id=(q,), device_id_type=MESH)
    @pl.when(pc.z > 0)
    def _():
        pl.semaphore_signal(sem, inc=1, device_id=(pc.me - 8,), device_id_type=MESH)
    @pl.when(pc.z < pc.Z - 1)
    def _():
        pl.semaphore_signal(sem, inc=1, device_id=(pc.me + 8,), device_id_type=MESH)
    ends = (pc.z == 0).astype(jnp.int32) + (pc.z == pc.Z - 1).astype(jnp.int32)
    pl.semaphore_wait(sem, 5 - ends)

def region(out, quart, zs, y, x, c, off, w):
    if quart:
        q = out.shape[3] // 4
        col = pl.multiple_of((x * 2 + c) * q + off, 128)
        return out.at[zs, y, :, pl.ds(col, w)]
    return out.at[zs, y, x, c, :, pl.ds(off, w)]


CHUNKS = (
    tuple((0, 384 * i, 384, 1) for i in range(3))
    + tuple((1, 384 * i, 384, 1) for i in range(3))
    + tuple((2, 384 * i, 384, 1) for i in range(3))
    + ((3, 0, 384, 1), (3, 384, 128, 1))
    + ((4, 0, 768, 2), (4, 768, 768, 2), (4, 1536, 512, 2))
    + ((5, 0, 768, 2),)
)
QUARTERED = (True, True, False, True, False, False)

def dot(a, b):
    return jnp.dot(a, b, preferred_element_type=jnp.float32)

def dot_nt(a, b):
    return lax.dot_general(a, b, (((1,), (1,)), ((), ())), preferred_element_type=jnp.float32)

def norm_parts(values):
    centred = values - jnp.mean(values, axis=-1, keepdims=True)
    spread = jnp.mean(centred * centred, axis=-1, keepdims=True)
    return centred, lax.rsqrt(spread + EPSILON)

def token_rows(onehot, mod, k):
    cols = slice(k * D, (k + 1) * D)
    total = onehot[:, 0:1] * mod[0:1, cols]
    for i in range(1, mod.shape[0]):
        total = total + onehot[:, i:i + 1] * mod[i:i + 1, cols]
    return total

def head_window(h):
    start = jnp.minimum((h * HD) // 128 * 128, D - 256)
    start = pl.multiple_of(start, 128)
    lane = lax.broadcasted_iota(jnp.int32, (1, 256), 1) + start
    return start, (lane >= h * HD) & (lane < h * HD + HD)

def gather_program(n, ins, outs, sems, rounds, quarts):
    lsem, zs_sem, zr_sem, xs_sem, xr_sem, cs_sem, cr_sem = sems
    pc = Place(n)
    Z = pc.Z
    z, y, x, c = pc.z, pc.y, pc.x, pc.c
    def reg(r, zs, y_, x_, c_=None):
        a, off, w = rounds[r][:3]
        return region(outs[a], quarts[a], zs, y_, x_, c if c_ is None else c_, off, w)
    def own_in(r):
        a, off, w = rounds[r][:3]
        return ins[a].at[:, pl.ds(off, w)]
    def rcopy(src, dst, ss, rs, dev):
        return pltpu.make_async_remote_copy(src_ref=src, dst_ref=dst, send_sem=ss, recv_sem=rs, device_id=(dev,), device_id_type=MESH)
    def zcopy(r, side, s):
        org = z - s if side == 0 else z + s
        dst = reg(r, org, y, x)
        return rcopy(own_in(r) if s == 0 else dst, dst, zs_sem.at[r, side, s], zr_sem.at[r, side, s], pc.me + (8 if side == 0 else -8))
    def zrecv(r, side, s):
        org = z - 1 - s if side == 0 else z + 1 + s
        d = reg(r, org, y, x)
        rcopy(d, d, zs_sem.at[r, side, s], zr_sem.at[r, side, s], pc.me).wait_recv()
    def local(r):
        return pltpu.make_async_copy(own_in(r), reg(r, z, y, x), lsem.at[r])
    allz = slice(None); lo = slice(0, Z // 2); hi = slice(Z // 2, Z)
    def xy(r, k):
        if k < 2: d = reg(r, allz, y, x)
        elif k == 2: d = reg(r, lo, y, 1 - x)
        else: d = reg(r, hi, 1 - y, x)
        return rcopy(d, d, xs_sem.at[r, k], xr_sem.at[r, k], pc.xp if k in (0, 3) else pc.yp)
    def core(r, k):
        d = reg(r, allz, y if k in (0, 1) else 1 - y, x if k in (0, 2) else 1 - x)
        return rcopy(d, d, cs_sem.at[r, k], cr_sem.at[r, k], pc.cp)
    def zstart(r, s):
        @pl.when((z - s >= 0) & (z < Z - 1))
        def _(): zcopy(r, 0, s).start()
        @pl.when((z + s <= Z - 1) & (z > 0))
        def _(): zcopy(r, 1, s).start()
    def zwait(r, s):
        @pl.when(z - 1 - s >= 0)
        def _(): zrecv(r, 0, s)
        @pl.when(z + 1 + s <= Z - 1)
        def _(): zrecv(r, 1, s)
    def stage(r, s):
        if s == 0:
            local(r).start()
            zstart(r, 0)
        elif s < Z - 1:
            zwait(r, s - 1)
            zstart(r, s)
        elif s == Z - 1:
            zwait(r, s - 1)
            local(r).wait()
            xy(r, 0).start(); xy(r, 1).start(); core(r, 0).start()
        elif s == Z:
            xy(r, 0).wait_recv(); xy(r, 2).start(); core(r, 1).start()
            xy(r, 1).wait_recv(); xy(r, 3).start(); core(r, 2).start()
        elif s == Z + 1:
            xy(r, 2).wait_recv(); xy(r, 3).wait_recv(); core(r, 3).start()
        elif s == Z + 2:
            for k in range(4): core(r, k).wait_recv()
    def finish(r):
        for s in range(Z - 1):
            @pl.when((z - s >= 0) & (z < Z - 1))
            def _(): zcopy(r, 0, s).wait_send()
            @pl.when((z + s <= Z - 1) & (z > 0))
            def _(): zcopy(r, 1, s).wait_send()
        for k in range(4):
            xy(r, k).wait_send(); core(r, k).wait_send()
    return stage, finish, Z + 3

def weight_loads(chunk, full, slot, attn_slot, sem, parts=range(4)):
    a, off, w, stacks = chunk
    ref, cps = full[a], []
    for j in parts:
        if QUARTERED[a]:
            dst = attn_slot if a == 0 and j == 3 else slot.at[j, :, :, :, pl.ds(0, w)]
            cps.append((ref.at[:, :, :, pl.ds(j * (ref.shape[3] // 4) + off, w)], dst))
        else:
            rows, sw = ref.shape[4], w // stacks
            for s in range(stacks):
                cps.append((ref.at[:, :, j // 2, j % 2, :, pl.ds(off + s * sw, sw)],
                            slot.at[j, :, :, pl.ds(s * rows, rows), pl.ds(0, sw)]))
    return [pltpu.make_async_copy(s, d, sem.at[k]) for k, (s, d) in enumerate(cps)]

def chunk_weight(chunk, slot, attn_slot, rows, part):
    a, off, w, stacks = chunk
    if QUARTERED[a]:
        value = attn_slot[...] if a == 0 and part == 3 else slot[part, :, :, :, 0:w]
        return value.reshape(-1, w)
    sw = w // stacks
    value = slot[:, :, :, part * rows:(part + 1) * rows, 0:sw]
    Z = value.shape[1]
    return jnp.concatenate([value[j, zz, yy] for zz in range(Z) for yy in range(2) for j in range(4)], axis=0)

def scatter_program(n, R, G, CR, XR, ZR, keep, sems, final):
    cs, cr, xs, xr, zs_, zr, credit = sems
    keep_g, keep_c, keep_x = keep
    pc = Place(n)
    Z = pc.Z; H = Z // 2
    z, y, x, c = pc.z, pc.y, pc.x, pc.c
    up_dev = jnp.minimum(pc.me + 8, n - 1)
    down_dev = jnp.maximum(pc.me - 8, 0)
    def rcopy(src, dst, ss, rs, dev):
        return pltpu.make_async_remote_copy(src_ref=src, dst_ref=dst, send_sem=ss, recv_sem=rs, device_id=(dev,), device_id_type=MESH)
    def signal(k, dev):
        pl.semaphore_signal(credit.at[k], inc=1, device_id=(dev,), device_id_type=MESH)
    def core(r): return rcopy(G(r).at[1 - c], CR(r), cs.at[r], cr.at[r], pc.cp)
    def xy(r, k):
        b, xb = G(r).at[c], XR(r)
        if k == 0: return rcopy(b.at[1 - x, 0:H, 1 - y], xb.at[0:H], xs.at[r, 0], xr.at[r, 0], pc.yp)
        if k == 1: return rcopy(b.at[1 - x, H:Z, 1 - y], xb.at[H:Z], xs.at[r, 1], xr.at[r, 1], pc.xp)
        if k == 2: return rcopy(b.at[1 - x, :, y], xb.at[Z:2 * Z], xs.at[r, 2], xr.at[r, 2], pc.xp)
        return rcopy(b.at[x, :, 1 - y], xb.at[2 * Z:3 * Z], xs.at[r, 3], xr.at[r, 3], pc.yp)
    def zc(r, side, d):
        return rcopy(XR(r).at[Z + d], ZR(r).at[side, d], zs_.at[r, side, d], zr.at[r, side, d], up_dev if side == 0 else down_dev)
    def waits_send(r):
        core(r).wait_send()
        for k in range(4): xy(r, k).wait_send()
    def zwaits_send(r):
        for d in range(Z):
            @pl.when(d > z)
            def _(): zc(r, 0, d).wait_send()
            @pl.when(d < z)
            def _(): zc(r, 1, d).wait_send()
    def zstep(r, s):
        for side in (0, 1):
            p = s if side == 0 else Z - 1 - s
            @pl.when(z == p)
            def _():
                if r >= keep_x and (p < Z - 1 if side == 0 else p > 0):
                    pl.semaphore_wait(credit.at[3 + side], 1)
                for d in range(Z):
                    if (d > p) if side == 0 else (d < p):
                        if s > 0:
                            zc(r, side, d).wait_recv()
                            XR(r)[Z + d] = XR(r)[Z + d] + ZR(r)[side, d]
                        zc(r, side, d).start()
    def before(r):
        if r >= keep_g:
            waits_send(r - keep_g)
    def stage(r, s):
        b = G(r).at[c]
        if s == 0:
            if r >= keep_c:
                pl.semaphore_wait(credit.at[0], 1)
            core(r).start()
        elif s == 1:
            core(r).wait_recv()
            def add(i, carry):
                xx, zz, yy = i // (2 * Z), (i // 2) % Z, i % 2
                b[xx, zz, yy] = b[xx, zz, yy] + CR(r)[xx, zz, yy]
                return carry
            lax.fori_loop(0, 4 * Z, add, 0)
            if r + keep_c < R:
                signal(0, pc.cp)
            if r >= keep_x:
                pl.semaphore_wait(credit.at[1], 1)
                pl.semaphore_wait(credit.at[2], 1)
            xy(r, 0).start(); xy(r, 1).start()
        elif s == 2:
            xy(r, 0).wait_recv()
            def add(i, carry):
                b[1 - x, i, y] = b[1 - x, i, y] + XR(r)[i]
                return carry
            lax.fori_loop(0, H, add, 0)
            xy(r, 2).start()
            xy(r, 1).wait_recv()
            def add(i, carry):
                b[x, i, 1 - y] = b[x, i, 1 - y] + XR(r)[i]
                return carry
            lax.fori_loop(H, Z, add, 0)
            xy(r, 3).start()
        elif s == 3:
            xy(r, 2).wait_recv(); xy(r, 3).wait_recv()
            def add(i, carry):
                XR(r)[Z + i] = b[x, i, y] + XR(r)[Z + i] + XR(r)[2 * Z + i]
                return carry
            lax.fori_loop(0, Z, add, 0)
            zstep(r, 0)
        elif s < Z + 2:
            zstep(r, s - 3)
        else:
            for d in range(Z):
                @pl.when(d == z)
                def _():
                    tot = XR(r)[Z + d].astype(jnp.float32)
                    if d > 0:
                        zc(r, 0, d).wait_recv()
                        tot = tot + ZR(r)[0, d].astype(jnp.float32)
                    if d < Z - 1:
                        zc(r, 1, d).wait_recv()
                        tot = tot + ZR(r)[1, d].astype(jnp.float32)
                    final(r, tot)
            zwaits_send(r)
            if r + keep_x < R:
                signal(1, pc.xp)
                signal(2, pc.yp)
                @pl.when(z < Z - 1)
                def _(): signal(4, up_dev)
                @pl.when(z > 0)
                def _(): signal(3, down_dev)
    def finish():
        for r in range(max(0, R - keep_g), R):
            waits_send(r)
    return before, stage, finish, Z + 3

def scatter_sems(R, Z):
    D_ = pltpu.SemaphoreType.DMA
    return [D_((R,)), D_((R,)), D_((R, 4)), D_((R, 4)), D_((R, 2, Z)), D_((R, 2, Z)), pltpu.SemaphoreType.REGULAR((5,))]

def forward_kernel(n, offs, *refs):
    rounds = CHUNKS
    ins, refs = refs[:6], refs[6:]
    tokens, onehot, same, mod_part, ada_b, qkv_b, tail_b, up_b, in_b, mid_b, out_b = refs[:11]
    refs = refs[11:]
    full, refs = refs[:6], refs[6:]
    (first_in, projected, heads, branch_attn, middle, second_in, up_pre, up_act, branch_mlp, mixed,
     first_pre, first_act, second_pre, second_act, features, mod) = refs[:16]
    refs = refs[16:]
    slots, attn_w, mod_own, mod_core, mod_xy, mod_line, load_sem = refs[:7]
    stage, finish, S = gather_program(n, ins, full, refs[7:14], rounds, QUARTERED)
    images = mod.shape[0]

    def mod_final(r, tot):
        for i in range(images):
            for k in range(6 * D // 128):
                row = i * (6 * D // 128) + k
                mod[i:i + 1, 128 * k:128 * (k + 1)] = tot[row:row + 1] + ada_b[:, 128 * k:128 * (k + 1)]
    _, mod_stage, mod_finish, _ = scatter_program(
        n, 1, lambda r: mod_own, lambda r: mod_core, lambda r: mod_xy, lambda r: mod_line, (1, 1, 1), refs[14:], mod_final)
    mod_own[...] = mod_part[...]
    barrier(Place(n))
    R, Z = len(rounds), n // 8
    last_of = {a: max(r for r in range(R) if rounds[r][0] == a) for a in range(6)}

    def loads(r):
        a, off, w, _ = rounds[r]
        return weight_loads(rounds[r], full, slots.at[r % 2], attn_w.at[off // 384] if a == 0 else None, load_sem.at[r % 2])

    def prepare():
        oh, md = onehot[...], mod
        values = tokens[...].astype(jnp.float32)
        centred, scale = norm_parts(values)
        first_in[...] = (centred * scale * (1.0 + token_rows(oh, md, 1)) + token_rows(oh, md, 0)).astype(jnp.bfloat16)

    def attention():
        def head(h, carry):
            start, inside = head_window(h)
            q = projected[:, pl.ds(start, 256)]
            k = projected[:, pl.ds(pl.multiple_of(start + D, 128), 256)]
            v = projected[:, pl.ds(pl.multiple_of(start + 2 * D, 128), 256)]
            q = jnp.where(inside, q, jnp.zeros_like(q))
            scores = jnp.where(same[...] > 0.0, dot_nt(q, k) * HD ** (-0.5), -1e30)
            e = jnp.exp(scores - jnp.max(scores, axis=-1, keepdims=True))
            p = (e / jnp.sum(e, axis=-1, keepdims=True)).astype(jnp.bfloat16)
            o = dot(p, v).astype(jnp.bfloat16)
            heads[:, pl.ds(start, 256)] = jnp.where(inside, o, heads[:, pl.ds(start, 256)])
            return carry
        heads[...] = jnp.zeros_like(heads)
        lax.fori_loop(0, HEADS, head, 0)
        for i in range(3):
            w = attn_w[i].reshape(D, 384)
            branch_attn[:, 384 * i:384 * (i + 1)] = dot(heads[...], w) + tail_b[:, 384 * i:384 * (i + 1)]
        oh, md = onehot[...], mod
        mid = tokens[...].astype(jnp.float32) + token_rows(oh, md, 2) * branch_attn[...]
        middle[...] = mid
        centred, scale = norm_parts(mid)
        second_in[...] = (centred * scale * (1.0 + token_rows(oh, md, 4)) + token_rows(oh, md, 3)).astype(jnp.bfloat16)

    def compute(r):
        a, off, w, stacks = rounds[r]
        slot = slots.at[r % 2]
        if a == 0:
            for j in range(3):
                cols = slice(j * D + off, j * D + off + w)
                projected[:, cols] = (dot(first_in[...], chunk_weight(rounds[r], slot, None, 0, j)) + qkv_b[:, cols]).astype(jnp.bfloat16)
            if r == last_of[0]:
                attention()
        elif a == 1:
            for j in range(4):
                cols = slice(j * (FF // 4) + off, j * (FF // 4) + off + w)
                pre = dot(second_in[...], chunk_weight(rounds[r], slot, None, 0, j)) + up_b[:, cols]
                up_pre[:, cols] = pre
                up_act[:, cols] = gelu_tanh(pre).astype(jnp.bfloat16)
        elif a == 2:
            cols = slice(off, off + w)
            branch_mlp[:, cols] = dot(up_act[...], chunk_weight(rounds[r], slot, None, FF // n, 0)) + tail_b[:, D + off:D + off + w]
            if r == last_of[2]:
                hidden = middle[...] + token_rows(onehot[...], mod, 5) * branch_mlp[...]
                mixed[...] = hidden.astype(jnp.bfloat16)
        elif a == 3:
            for j in range(4):
                cols = slice(j * (P_SIZE // 4) + off, j * (P_SIZE // 4) + off + w)
                pre = dot(mixed[...], chunk_weight(rounds[r], slot, None, 0, j)) + in_b[:, cols]
                first_pre[:, cols] = pre
                first_act[:, cols] = sigmoid_linear(pre).astype(jnp.bfloat16)
        elif a == 4:
            sw = w // stacks
            for s in range(stacks):
                cols = slice(off + s * sw, off + (s + 1) * sw)
                pre = dot(first_act[...], chunk_weight(rounds[r], slot, None, P_SIZE // n, s)) + mid_b[:, cols]
                second_pre[:, cols] = pre
                second_act[:, cols] = sigmoid_linear(pre).astype(jnp.bfloat16)
        else:
            sw = w // stacks
            for s in range(stacks):
                cols = slice(off + s * sw, off + (s + 1) * sw)
                features[:, cols] = dot(second_act[...], chunk_weight(rounds[r], slot, None, P_SIZE // n, s)) + out_b[:, cols]

    offs = offs + (offs[-1] + 1, offs[-1] + 2)
    for t in range(R + offs[-1]):
        for s in list(reversed(range(S))) + [S, S + 1]:
            r = t - offs[s]
            if not 0 <= r < R:
                continue
            if s < S:
                stage(r, s)
            elif s == S:
                for cp in loads(r): cp.start()
            else:
                for cp in loads(r): cp.wait()
                compute(r)
        if t < Z + 3:
            mod_stage(0, t)
        if t == Z + 3:
            prepare()
    for r in range(R):
        finish(r)
    mod_finish()

def forward(n, images, shards, small, offs, cid):
    Z, R = n // 8, len(CHUNKS)
    f32, bf = jnp.float32, jnp.bfloat16
    tok = small[0].shape[0]
    shapes = []
    for sh, qt in zip(shards, QUARTERED):
        k, w = sh.shape
        shapes.append(jax.ShapeDtypeStruct((Z, 2, k, 4 * w) if qt else (Z, 2, 2, 2, k, w), sh.dtype))
    acts = [(D, bf), (3 * D, bf), (D, bf), (D, f32), (D, f32), (D, bf), (FF, f32), (FF, bf), (D, f32), (D, bf),
            (P_SIZE, f32), (P_SIZE, bf), (P_SIZE, f32), (P_SIZE, bf), (Z_OUT, f32)]
    mod_dims = small[3].shape[-2:]
    shapes += [jax.ShapeDtypeStruct((tok, w), dt) for w, dt in acts]
    shapes.append(jax.ShapeDtypeStruct((images, 6 * D), f32))
    D_ = pltpu.SemaphoreType.DMA
    hbm, vmem = pl.BlockSpec(memory_space=pltpu.HBM), pl.BlockSpec(memory_space=pltpu.VMEM)
    return pl.pallas_call(
        functools.partial(forward_kernel, n, offs),
        out_shape=shapes,
        in_specs=[hbm] * 6 + [vmem] * len(small),
        out_specs=[hbm] * 6 + [vmem] * (len(acts) + 1),
        scratch_shapes=[
            pltpu.VMEM((2, 4, Z, 2, 144, 384), bf),
            pltpu.VMEM((3, Z, 2, 144, 384), bf),
            pltpu.VMEM((2, 2, Z, 2) + mod_dims, f32),
            pltpu.VMEM((2, Z, 2) + mod_dims, f32),
            pltpu.VMEM((3 * Z,) + mod_dims, f32),
            pltpu.VMEM((2, Z) + mod_dims, f32),
            D_((2, 8)),
            D_((R,)), D_((R, 2, Z - 1)), D_((R, 2, Z - 1)), D_((R, 4)), D_((R, 4)), D_((R, 4)), D_((R, 4)),
        ] + scatter_sems(1, Z),
        compiler_params=pltpu.CompilerParams(collective_id=cid, has_side_effects=True, vmem_limit_bytes=56 * 2**20),
    )(*shards, *small)


BACK_CHUNKS = (
    ((5, 0, 768, 2),)
    + ((4, 0, 768, 2), (4, 768, 768, 2), (4, 1536, 512, 2))
    + ((3, 0, 384, 1), (3, 384, 128, 1))
    + tuple((2, 384 * i, 384, 1) for i in range(3))
    + tuple((1, 384 * i, 384, 1) for i in range(3))
    + tuple((0, 384 * i, 384, 1) for i in range(3))
)
CHAIN = BACK_CHUNKS[:12] + tuple((6, 384 * i, 384, 1) for i in range(3)) + BACK_CHUNKS[12:]

def dot_tn(a, b):
    return lax.dot_general(a, b, (((0,), (0,)), ((), ())), preferred_element_type=jnp.float32)

def norm_back(centred, scale, grad):
    normed = centred * scale
    inner = jnp.mean(grad * normed, axis=-1, keepdims=True)
    return scale * (grad - jnp.mean(grad, axis=-1, keepdims=True) - normed * inner)

def sigmoid_linear_slope(v):
    s = jax.nn.sigmoid(v)
    return s * (1.0 + v * (1.0 - s))

def gelu_slope(v):
    t = jnp.tanh(0.7978845608028654 * (v + 0.044715 * v * v * v))
    return 0.5 * (1.0 + t) + 0.5 * v * (1.0 - t * t) * 0.7978845608028654 * (1.0 + 3.0 * 0.044715 * v * v)

def backward_kernel(n, images, chain_per_tick, scatter_offs, mod_offs, *refs):
    Z = n // 8
    full, refs = refs[:6], refs[6:]
    (tokens, onehot, same, mod, targets, out_grad, first_in, projected, heads, branch_attn, middle, second_in,
     up_pre, up_act, branch_mlp, mixed, first_pre, first_act, second_pre, second_act, features) = refs[:21]
    refs = refs[21:]
    outs, refs = refs[:6], refs[6:]
    tokens_grad, qkv_sums, attn_sums, mlp_sums, up_sums, in_sums, mid_sums, out_sums, mod_all = refs[:9]
    refs = refs[9:]
    (slots, load_sem, G_, CR_, XR_, ZR_, feature_grad, second_back, first_back, hidden_grad, mlp_grad, up_grad,
     middle_grad, attn_grad, heads_grad, projected_grad, wide, narrow, mod_grad, mod_rows, mod_lines) = refs[:21]
    refs = refs[21:]
    rounds, R = BACK_CHUNKS, len(BACK_CHUNKS)
    bf = jnp.bfloat16
    pc = Place(n)

    def dims(r):
        a, off, w, stacks = rounds[r]
        return ((FF // n if QUARTERED[a] or a == 2 else stacks * (P_SIZE // n)), w // stacks)
    keep = (G_.shape[0], CR_.shape[0], XR_.shape[0])
    def cut(ref, r):
        rows, w = dims(r)
        lead = (slice(None),) * (len(ref.shape) - 3)
        return ref.at[(r % ref.shape[0],) + lead + (slice(0, rows), slice(0, w))]
    def final(r, tot):
        a, off, w, stacks = rounds[r]
        rows, sw = dims(r)
        rows = rows // stacks
        for s in range(stacks):
            outs[a][:, off + s * sw:off + (s + 1) * sw] = tot[s * rows:(s + 1) * rows]
    before, stage, finish, S = scatter_program(
        n, R, lambda r: cut(G_, r), lambda r: cut(CR_, r), lambda r: cut(XR_, r), lambda r: cut(ZR_, r), keep, refs[:7], final)
    mod_stage, mod_finish, _ = gather_program(n, [mod_rows], [mod_all], refs[7:], ((0, 0, 128),), (False,))
    barrier(pc)
    mod_lines[...] = jnp.zeros_like(mod_lines)

    def image_sums(k, value):
        cols = slice(k * D, (k + 1) * D)
        for i in range(images):
            mod_grad[i:i + 1, cols] = jnp.sum(value * onehot[:, i:i + 1], axis=0, keepdims=True)

    def sums(value):
        return jnp.sum(value.astype(jnp.float32), axis=0, keepdims=True)

    def start_chain():
        f, t = features[...], targets[...].astype(jnp.float32)
        f_norm = jnp.sqrt(jnp.sum(f * f, axis=1, keepdims=True) + EPSILON)
        t_norm = jnp.sqrt(jnp.sum(t * t, axis=1, keepdims=True) + EPSILON)
        inner = jnp.sum(f * t, axis=1, keepdims=True)
        grad = -0.5 * (t / (f_norm * t_norm) - f * (inner / (f_norm * f_norm * f_norm * t_norm)))
        feature_grad[...] = grad.astype(bf)
        out_sums[...] = sums(feature_grad[...])

    def attention_back():
        projected_grad[...] = jnp.zeros_like(projected_grad)
        def head(h, carry):
            start, inside = head_window(h)
            at_q, at_k, at_v = [pl.ds(pl.multiple_of(start + i * D, 128), 256) for i in range(3)]
            q, k, v = projected[:, at_q], projected[:, at_k], projected[:, at_v]
            q = jnp.where(inside, q, jnp.zeros_like(q))
            g = heads_grad[:, at_q]
            g = jnp.where(inside, g, jnp.zeros_like(g))
            scores = jnp.where(same[...] > 0.0, dot_nt(q, k) * HD ** (-0.5), -1e30)
            e = jnp.exp(scores - jnp.max(scores, axis=-1, keepdims=True))
            p = e / jnp.sum(e, axis=-1, keepdims=True)
            pg = dot_nt(g, v)
            sg = (p * (pg - jnp.sum(p * pg, axis=-1, keepdims=True))).astype(bf)
            for at, value in (
                (at_q, dot(sg, k) * HD ** (-0.5)),
                (at_k, dot_tn(sg, q) * HD ** (-0.5)),
                (at_v, dot_tn(p.astype(bf), g)),
            ):
                projected_grad[:, at] = jnp.where(inside, value.astype(bf), projected_grad[:, at])
            return carry
        lax.fori_loop(0, HEADS, head, 0)
        qkv_sums[...] = sums(projected_grad[...])

    C = len(CHAIN)
    last = {a: max(k for k in range(C) if CHAIN[k][0] == a) for a in range(7)}
    first = {a: min(k for k in range(C) if CHAIN[k][0] == a) for a in range(7)}

    def chain_loads(k):
        a, off, w, stacks = CHAIN[k]
        slot, sem = slots.at[k % 2], load_sem.at[k % 2]
        if a == 6:
            return weight_loads((0, off, w, stacks), full, slot, slot.at[3], sem, (3,))
        return weight_loads((a, off, w, stacks), full, slot, slot.at[3], sem, range(3) if a == 0 else range(4))

    def accumulate(acc, cols, new, k, a):
        acc[:, cols] = new if k == first[a] else acc[:, cols] + new

    def chain(k):
        a, off, w, stacks = CHAIN[k]
        slot = slots.at[k % 2]
        sw = w // stacks
        if a in (4, 5):
            grad = second_back if a == 4 else feature_grad
            new = None
            for s in range(stacks):
                part = dot_nt(grad[:, off + s * sw:off + (s + 1) * sw], chunk_weight(CHAIN[k], slot, None, P_SIZE // n, s))
                new = part if new is None else new + part
            accumulate(wide, slice(0, P_SIZE), new, k, a)
            if k == last[a]:
                target, pre = (second_back, second_pre) if a == 5 else (first_back, first_pre)
                target[...] = (wide[:, 0:P_SIZE] * sigmoid_linear_slope(pre[...])).astype(bf)
                (mid_sums if a == 5 else in_sums)[...] = sums(target[...])
        elif a == 2:
            for q in range(4):
                weight = chunk_weight(CHAIN[k], slot, None, FF // n, 0)[q * D:(q + 1) * D]
                accumulate(wide, slice(q * D, (q + 1) * D), dot_nt(mlp_grad[:, off:off + w], weight), k, a)
            if k == last[a]:
                for q in range(4):
                    cols = slice(q * D, (q + 1) * D)
                    up_grad[:, cols] = (wide[:, cols] * gelu_slope(up_pre[:, cols])).astype(bf)
                up_sums[...] = sums(up_grad[...])
        else:
            src, parts, width = {3: (first_back, range(4), P_SIZE // 4), 1: (up_grad, range(4), FF // 4),
                                 0: (projected_grad, range(3), D), 6: (attn_grad, range(3, 4), D)}[a]
            new = None
            for j in parts:
                col = off if a == 6 else j * width + off
                weight = slot[j, :, :, :, 0:w].reshape(-1, w)
                part = dot_nt(src[:, col:col + w], weight)
                new = part if new is None else new + part
            accumulate(narrow, slice(0, D), new, k, a)
            if k == last[a]:
                oh = onehot[...]
                if a == 3:
                    hg = out_grad[...].astype(jnp.float32) + narrow[...]
                    hidden_grad[...] = hg
                    mlp_grad[...] = (hg * token_rows(oh, mod, 5)).astype(bf)
                    mlp_sums[...] = sums(mlp_grad[...])
                    image_sums(5, hg * branch_mlp[...])
                elif a == 1:
                    g = narrow[...]
                    centred, scale = norm_parts(middle[...])
                    image_sums(3, g)
                    image_sums(4, g * (centred * scale))
                    mg = hidden_grad[...] + norm_back(centred, scale, g * (1.0 + token_rows(oh, mod, 4)))
                    middle_grad[...] = mg
                    attn_grad[...] = (mg * token_rows(oh, mod, 2)).astype(bf)
                    attn_sums[...] = sums(attn_grad[...])
                    image_sums(2, mg * branch_attn[...])
                elif a == 6:
                    heads_grad[...] = narrow[...].astype(bf)
                    attention_back()
                else:
                    g = narrow[...]
                    centred, scale = norm_parts(tokens[...].astype(jnp.float32))
                    image_sums(0, g)
                    image_sums(1, g * (centred * scale))
                    tg = middle_grad[...] + norm_back(centred, scale, g * (1.0 + token_rows(oh, mod, 1)))
                    tokens_grad[...] = tg.astype(bf)
                    stacked = mod_grad[...]
                    rows = 6 * D // 128
                    for i in range(images):
                        for k in range(rows):
                            mod_lines[i * rows + k:i * rows + k + 1] = stacked[i:i + 1, 128 * k:128 * (k + 1)]
                    mod_rows[...] = mod_lines[...].astype(bf)

    def produce(r):
        a, off, w, stacks = rounds[r]
        before(r)
        left, right = {5: (second_act, feature_grad), 4: (first_act, second_back), 3: (mixed, first_back), 2: (up_act, mlp_grad),
                       1: (second_in, up_grad), 0: (first_in, projected_grad)}[a]
        rows, sw = dims(r)
        g = cut(G_, r)
        if QUARTERED[a]:
            for j in range(4):
                if a == 0 and j == 3:
                    value = dot_tn(heads[...], attn_grad[:, off:off + w])
                else:
                    q = {3: P_SIZE // 4, 1: FF // 4, 0: D}[a]
                    value = dot_tn(left[...], right[:, j * q + off:j * q + off + w])
                g[j % 2, j // 2] = value.astype(bf).reshape(Z, 2, rows, w)
        else:
            rows = rows // stacks
            per = 1152 if a == 2 else 1024
            for s in range(stacks):
                for part in range(left.shape[1] // per):
                    value = dot_tn(left[:, part * per:(part + 1) * per], right[:, off + s * sw:off + (s + 1) * sw]).astype(bf)
                    for i in range(per // rows):
                        d = part * (per // rows) + i
                        g[d % 2, (d // 2) % 2, d // 8, (d // 4) % 2, s * rows:(s + 1) * rows] = value[i * rows:(i + 1) * rows]

    need = {5: 0, 4: first[4], 3: first[3], 2: first[2], 1: first[1], 0: first[0]}
    done = 0
    mod_start = None
    for cp in chain_loads(0): cp.start()
    start_chain()
    t = 0
    while True:
        busy = False
        for s in reversed(range(1, S)):
            r = t - scatter_offs[s]
            if 0 <= r < R:
                stage(r, s); busy = True
        if t < R:
            busy = True
            while done < need[rounds[t][0]]:
                done = advance(done, chain_loads, chain, C)
            produce(t)
            stage(t, 0)
        for _ in range(chain_per_tick):
            if done < C:
                done = advance(done, chain_loads, chain, C)
        if done == C and mod_start is None:
            mod_start = t
        if mod_start is not None:
            for s in reversed(range(Z + 3)):
                if t - mod_start == mod_offs[s]:
                    mod_stage(0, s)
            busy = busy or t - mod_start < mod_offs[-1]
        if not busy:
            break
        t += 1
    finish()
    mod_finish(0)

def advance(k, chain_loads, chain, total):
    if k + 1 < total:
        for cp in chain_loads(k + 1): cp.start()
    for cp in chain_loads(k): cp.wait()
    chain(k)
    return k + 1

def backward(n, images, weights, acts, mod_height, plan, cid):
    Z, R = n // 8, len(BACK_CHUNKS)
    f32, bf = jnp.float32, jnp.bfloat16
    tok = acts[0].shape[0]
    chain_per_tick, scatter_offs, mod_offs, keep = plan
    shapes = [jax.ShapeDtypeStruct((w.shape[2], w.shape[3] // 4) if qt else w.shape[4:], f32) for w, qt in zip(weights, QUARTERED)]
    shapes.append(jax.ShapeDtypeStruct((tok, D), bf))
    shapes += [jax.ShapeDtypeStruct((1, w), f32) for w in (3 * D, D, D, FF, P_SIZE, P_SIZE, Z_OUT)]
    hbm, vmem = pl.BlockSpec(memory_space=pltpu.HBM), pl.BlockSpec(memory_space=pltpu.VMEM)
    shapes.append(jax.ShapeDtypeStruct((Z, 2, 2, 2, mod_height, 128), bf))
    D_ = pltpu.SemaphoreType.DMA
    V = pltpu.VMEM
    return pl.pallas_call(
        functools.partial(backward_kernel, n, images, chain_per_tick, scatter_offs, mod_offs),
        out_shape=shapes,
        in_specs=[hbm] * 6 + [vmem] * len(acts),
        out_specs=[vmem] * 14 + [hbm],
        scratch_shapes=[
            V((2, 4, Z, 2, 144, 384), bf),
            D_((2, 8)),
            V((keep[0], 2, 2, Z, 2, 144, 384), bf),
            V((keep[1], 2, Z, 2, 144, 384), bf),
            V((keep[2], 3 * Z, 144, 384), bf),
            V((keep[2], 2, Z, 144, 384), bf),
            V((tok, Z_OUT), bf), V((tok, P_SIZE), bf), V((tok, P_SIZE), bf), V((tok, D), f32), V((tok, D), bf), V((tok, FF), bf),
            V((tok, D), f32), V((tok, D), bf), V((tok, D), bf), V((tok, 3 * D), bf), V((tok, FF), f32), V((tok, D), f32),
            V((images, 6 * D), f32), V((mod_height, 128), bf), V((mod_height, 128), f32),
        ] + scatter_sems(R, Z)
        + [D_((1,)), D_((1, 2, Z - 1)), D_((1, 2, Z - 1)), D_((1, 4)), D_((1, 4)), D_((1, 4)), D_((1, 4))],
        compiler_params=pltpu.CompilerParams(collective_id=cid, has_side_effects=True, vmem_limit_bytes=61 * 2**20),
    )(*weights, *acts)


def per_device(
    tokens,
    cond,
    image_lengths,
    ada_weight,
    ada_bias,
    qkv_weight,
    qv_bias,
    attn_weight,
    tail_bias,
    up_weight,
    up_bias,
    down_weight,
    projector_in,
    projector_in_bias,
    projector_mid,
    projector_mid_bias,
    projector_out,
    projector_out_bias,
    targets,
    out_grad,
):
    owners = lax.axis_size("fsdp")
    mix_gathered = (
        lax.all_gather(ada_weight, "fsdp", axis=0, tiled=True),
        lax.all_gather(ada_bias, "fsdp", axis=0, tiled=True),
        lax.all_gather(qkv_weight, "fsdp", axis=0, tiled=True),
        lax.all_gather(qv_bias, "fsdp", axis=0, tiled=True),
        lax.all_gather(attn_weight, "fsdp", axis=0, tiled=True),
        lax.all_gather(tail_bias, "fsdp", axis=0, tiled=True),
    )
    mix_full = unpack_mix(mix_gathered)
    ada_full, ada_bias_full, qkv_full, qv_full, attn_full, tail_full = mix_full
    row_count = tokens.shape[0]
    cond_values = cond.astype(jnp.float32)
    cond_low = lowered(sigmoid_linear(cond_values))
    modulation = matmul(cond_low, ada_full) + ada_bias_full
    image_of, onehot = image_onehot(image_lengths[0], row_count)
    per_token = jnp.dot(onehot, modulation, precision=PRECISE)
    shift_one, scale_one, gate_one, shift_two, scale_two, gate_two = jnp.split(per_token, 6, axis=1)
    inputs = tokens.astype(jnp.float32)
    normed_one = layer_norm(inputs)
    first_in = lowered(normed_one * (1.0 + scale_one) + shift_one)
    key_zero = jnp.zeros((D,), jnp.float32)
    bias_full = jnp.concatenate([qv_full[:D], key_zero, qv_full[D:]])
    projected = lowered(matmul(first_in, qkv_full) + bias_full)
    queries = projected[:, :D].reshape(row_count, HEADS, HD)
    keys_all = projected[:, D : 2 * D].reshape(row_count, HEADS, HD)
    values_all = projected[:, 2 * D :].reshape(row_count, HEADS, HD)
    same_image = (image_of[:, None] == image_of[None, :])[None]
    score_scale = HD ** (-0.5)

    def masked_scores():
        raw_scores = (
            jnp.einsum("qhd,khd->hqk", queries, keys_all, preferred_element_type=jnp.float32)
            * score_scale
        )
        return jnp.where(same_image, raw_scores, -1e30)

    masked = masked_scores()
    row_max = jnp.max(masked, axis=-1, keepdims=True)
    exp_scores = jnp.exp(masked - row_max)
    row_total = jnp.sum(exp_scores, axis=-1, keepdims=True)
    attn_probs = exp_scores / row_total
    head_out = jnp.einsum(
        "hqk,khd->qhd", lowered(attn_probs), values_all, preferred_element_type=jnp.float32
    )
    heads_low = lowered(head_out.reshape(row_count, D))
    branch_attn = matmul(heads_low, attn_full) + tail_full[:D]
    middle = inputs + gate_one * branch_attn
    normed_two = layer_norm(middle)
    second_in = lowered(normed_two * (1.0 + scale_two) + shift_two)
    dense_gathered = (
        lax.all_gather(up_weight, "fsdp", axis=0, tiled=True),
        lax.all_gather(up_bias, "fsdp", axis=0, tiled=True),
        lax.all_gather(down_weight, "fsdp", axis=0, tiled=True),
        lax.all_gather(projector_in, "fsdp", axis=0, tiled=True),
        lax.all_gather(projector_in_bias, "fsdp", axis=0, tiled=True),
        lax.all_gather(projector_mid, "fsdp", axis=0, tiled=True),
        lax.all_gather(projector_mid_bias, "fsdp", axis=0, tiled=True),
        lax.all_gather(projector_out, "fsdp", axis=0, tiled=True),
        lax.all_gather(projector_out_bias, "fsdp", axis=0, tiled=True),
    )
    dense_full = unpack_dense(dense_gathered)
    (
        up_full,
        up_bias_full,
        down_full,
        proj_in_full,
        proj_in_bias_full,
        proj_mid_full,
        proj_mid_bias_full,
        proj_out_full,
        proj_out_bias_full,
    ) = dense_full
    up_pre = matmul(second_in, up_full) + up_bias_full
    up_act = lowered(gelu_tanh(up_pre))
    branch_mlp = matmul(up_act, down_full) + tail_full[D:]
    hidden = middle + gate_two * branch_mlp
    mixed = lowered(hidden)
    first_pre = matmul(mixed, proj_in_full) + proj_in_bias_full
    first_act = lowered(sigmoid_linear(first_pre))
    second_pre = matmul(first_act, proj_mid_full) + proj_mid_bias_full
    second_act = lowered(sigmoid_linear(second_pre))
    features = matmul(second_act, proj_out_full) + proj_out_bias_full
    target_values = targets.astype(jnp.float32)

    def cosine_loss(values):
        value_norm = jnp.sqrt(jnp.sum(values * values, axis=1) + EPSILON)
        target_norm = jnp.sqrt(jnp.sum(target_values * target_values, axis=1) + EPSILON)
        return -0.5 * jnp.sum(jnp.sum(values * target_values, axis=1) / (value_norm * target_norm))

    feature_grad = lowered(jax.grad(cosine_loss)(features))
    dense_again = (
        lax.all_gather(up_weight, "fsdp", axis=0, tiled=True),
        lax.all_gather(up_bias, "fsdp", axis=0, tiled=True),
        lax.all_gather(down_weight, "fsdp", axis=0, tiled=True),
        lax.all_gather(projector_in, "fsdp", axis=0, tiled=True),
        lax.all_gather(projector_in_bias, "fsdp", axis=0, tiled=True),
        lax.all_gather(projector_mid, "fsdp", axis=0, tiled=True),
        lax.all_gather(projector_mid_bias, "fsdp", axis=0, tiled=True),
        lax.all_gather(projector_out, "fsdp", axis=0, tiled=True),
        lax.all_gather(projector_out_bias, "fsdp", axis=0, tiled=True),
    )
    dense_back = unpack_dense(dense_again)
    up_back = dense_back[0]
    down_back = dense_back[2]
    proj_in_back = dense_back[3]
    proj_mid_back = dense_back[5]
    proj_out_back = dense_back[7]
    grad_proj_out = transposed_left(second_act, feature_grad)
    second_back = lowered(
        pull_back(sigmoid_linear, second_pre, transposed_right(feature_grad, proj_out_back))
    )
    grad_proj_mid = transposed_left(first_act, second_back)
    first_back = lowered(
        pull_back(sigmoid_linear, first_pre, transposed_right(second_back, proj_mid_back))
    )
    grad_proj_in = transposed_left(mixed, first_back)
    hidden_grad = out_grad.astype(jnp.float32) + transposed_right(first_back, proj_in_back)
    gate_two_grad = hidden_grad * branch_mlp
    branch_mlp_grad = lowered(hidden_grad * gate_two)
    grad_down = transposed_left(up_act, branch_mlp_grad)
    up_grad = lowered(pull_back(gelu_tanh, up_pre, transposed_right(branch_mlp_grad, down_back)))
    grad_up = transposed_left(second_in, up_grad)
    second_in_grad = transposed_right(up_grad, up_back)
    middle_grad = hidden_grad + pull_back(layer_norm, middle, second_in_grad * (1.0 + scale_two))
    up_rows = by_owner(grad_up, owners)
    up_bias_rows = by_owner(column_sums(up_grad), owners)
    down_rows = by_owner(grad_down, owners)
    proj_in_rows = by_owner(grad_proj_in, owners)
    proj_in_sums = by_owner(column_sums(first_back), owners)
    proj_mid_rows = by_owner(grad_proj_mid, owners)
    proj_mid_sums = by_owner(column_sums(second_back), owners)
    proj_out_rows = by_owner(grad_proj_out, owners)
    proj_out_sums = by_owner(column_sums(feature_grad), owners)
    dense_grads = flatten_all(
        (
            lax.psum_scatter(up_rows, "fsdp", scatter_dimension=0, tiled=True),
            lax.psum_scatter(up_bias_rows, "fsdp", scatter_dimension=0, tiled=True),
            lax.psum_scatter(down_rows, "fsdp", scatter_dimension=0, tiled=True),
            lax.psum_scatter(proj_in_rows, "fsdp", scatter_dimension=0, tiled=True),
            lax.psum_scatter(proj_in_sums, "fsdp", scatter_dimension=0, tiled=True),
            lax.psum_scatter(proj_mid_rows, "fsdp", scatter_dimension=0, tiled=True),
            lax.psum_scatter(proj_mid_sums, "fsdp", scatter_dimension=0, tiled=True),
            lax.psum_scatter(proj_out_rows, "fsdp", scatter_dimension=0, tiled=True),
            lax.psum_scatter(proj_out_sums, "fsdp", scatter_dimension=0, tiled=True),
        )
    )
    mix_again = (
        lax.all_gather(ada_weight, "fsdp", axis=0, tiled=True),
        lax.all_gather(ada_bias, "fsdp", axis=0, tiled=True),
        lax.all_gather(qkv_weight, "fsdp", axis=0, tiled=True),
        lax.all_gather(qv_bias, "fsdp", axis=0, tiled=True),
        lax.all_gather(attn_weight, "fsdp", axis=0, tiled=True),
        lax.all_gather(tail_bias, "fsdp", axis=0, tiled=True),
    )
    mix_back = unpack_mix(mix_again)
    ada_back = mix_back[0]
    qkv_back = mix_back[2]
    attn_back = mix_back[4]
    gate_one_grad = middle_grad * branch_attn
    branch_attn_grad = lowered(middle_grad * gate_one)
    grad_attn = transposed_left(heads_low, branch_attn_grad)
    heads_grad = lowered(transposed_right(branch_attn_grad, attn_back)).reshape(
        row_count, HEADS, HD
    )
    again_probs = jnp.exp(masked_scores() - row_max) / row_total
    prob_grad = jnp.einsum(
        "qhd,khd->hqk", heads_grad, values_all, preferred_element_type=jnp.float32
    )
    value_grad = jnp.einsum(
        "hqk,qhd->khd", lowered(again_probs), heads_grad, preferred_element_type=jnp.float32
    )
    score_grad = lowered(
        again_probs * (prob_grad - jnp.sum(again_probs * prob_grad, axis=-1, keepdims=True))
    )
    query_grad = (
        jnp.einsum("hqk,khd->qhd", score_grad, keys_all, preferred_element_type=jnp.float32)
        * score_scale
    )
    key_grad = (
        jnp.einsum("hqk,qhd->khd", score_grad, queries, preferred_element_type=jnp.float32)
        * score_scale
    )
    projected_grad = lowered(
        jnp.concatenate(
            [
                query_grad.reshape(row_count, D),
                key_grad.reshape(row_count, D),
                value_grad.reshape(row_count, D),
            ],
            axis=1,
        )
    )
    grad_qkv = transposed_left(first_in, projected_grad)
    projected_sums = column_sums(projected_grad)
    grad_qv_bias = jnp.concatenate([projected_sums[:D], projected_sums[2 * D :]])
    first_in_grad = transposed_right(projected_grad, qkv_back)
    input_grad = middle_grad + pull_back(layer_norm, inputs, first_in_grad * (1.0 + scale_one))
    token_mod_grad = jnp.concatenate(
        [
            first_in_grad,
            first_in_grad * normed_one,
            gate_one_grad,
            second_in_grad,
            second_in_grad * normed_two,
            gate_two_grad,
        ],
        axis=1,
    )
    modulation_grad = lowered(
        lax.dot_general(onehot, token_mod_grad, (((0,), (0,)), ((), ())), precision=PRECISE)
    )
    grad_ada = transposed_left(cond_low, modulation_grad)
    cond_grad = pull_back(
        sigmoid_linear, cond_values, transposed_right(modulation_grad, ada_back)
    ).astype(jnp.bfloat16)
    grad_tail = jnp.concatenate([column_sums(branch_attn_grad), column_sums(branch_mlp_grad)])
    ada_rows = by_owner(grad_ada, owners)
    ada_sums = by_owner(column_sums(modulation_grad), owners)
    qkv_rows = by_owner(grad_qkv, owners)
    qv_rows = by_owner(grad_qv_bias, owners)
    attn_rows = by_owner(grad_attn, owners)
    tail_rows = by_owner(grad_tail, owners)
    mix_grads = flatten_all(
        (
            lax.psum_scatter(ada_rows, "fsdp", scatter_dimension=0, tiled=True),
            lax.psum_scatter(ada_sums, "fsdp", scatter_dimension=0, tiled=True),
            lax.psum_scatter(qkv_rows, "fsdp", scatter_dimension=0, tiled=True),
            lax.psum_scatter(qv_rows, "fsdp", scatter_dimension=0, tiled=True),
            lax.psum_scatter(attn_rows, "fsdp", scatter_dimension=0, tiled=True),
            lax.psum_scatter(tail_rows, "fsdp", scatter_dimension=0, tiled=True),
        )
    )
    return (
        mixed,
        input_grad.astype(jnp.bfloat16),
        cond_grad,
        mix_grads[0],
        mix_grads[1],
        mix_grads[2],
        mix_grads[3],
        mix_grads[4],
        mix_grads[5],
        dense_grads[0],
        dense_grads[1],
        dense_grads[2],
        dense_grads[3],
        dense_grads[4],
        dense_grads[5],
        dense_grads[6],
        dense_grads[7],
        dense_grads[8],
    )


def per_device_kernels(
    tokens,
    cond,
    image_lengths,
    ada_weight,
    ada_bias,
    qkv_weight,
    qv_bias,
    attn_weight,
    tail_bias,
    up_weight,
    up_bias,
    down_weight,
    projector_in,
    projector_in_bias,
    projector_mid,
    projector_mid_bias,
    projector_out,
    projector_out_bias,
    targets,
    out_grad,
):
    owners = lax.axis_size("fsdp")
    me = lax.axis_index("fsdp")
    groups = [[4 * g + i for i in range(4)] for g in range(owners // 4)]
    row_count = tokens.shape[0]
    rows = D // owners
    row_sharded = jnp.concatenate(
        [
            qkv_weight.reshape(rows, 3 * D),
            attn_weight.reshape(rows, D),
            up_weight.reshape(rows, FF),
            projector_in.reshape(rows, P_SIZE),
        ],
        axis=1,
    )
    quarters = jnp.concatenate(
        [part.reshape(rows, 4, -1) for part in jnp.split(row_sharded, (4 * D, 8 * D), axis=1)], axis=2
    ).transpose(1, 0, 2)
    quarters = lax.all_to_all(
        quarters, "fsdp", 0, 0, axis_index_groups=groups, tiled=True
    ).reshape(4 * rows, -1)
    bias_row = jnp.concatenate(
        [ada_bias, qv_bias, tail_bias, up_bias, projector_in_bias, projector_mid_bias, projector_out_bias]
    )
    bias_width = bias_row.shape[0]
    images = cond.shape[0]
    cond_values = cond.astype(jnp.float32)
    cond_low = lowered(sigmoid_linear(cond_values))
    cond_parts = cond_low.reshape(images, owners, rows).transpose(1, 0, 2).reshape(owners, -1)
    received = lax.all_to_all(
        jnp.concatenate([jnp.broadcast_to(bias_row, (owners, bias_width)), cond_parts], axis=1),
        "fsdp", 0, 0, tiled=True,
    )
    bias_all = received[:, :bias_width].astype(jnp.float32)
    cond_mine = received[:, bias_width:].reshape(owners * images, rows)
    widths = (6 * D, 2 * D, 2 * D, FF, P_SIZE, P_SIZE, Z)
    ends, at = [], 0
    for width in widths:
        at += width // owners
        ends.append(at)
    (
        ada_bias_full, qv_full, tail_full, up_bias_full, proj_in_bias_full, proj_mid_bias_full, proj_out_bias_full
    ) = [part.reshape(-1) for part in jnp.split(bias_all, ends[:-1], axis=1)]
    ada_mine = ada_weight.reshape(rows, 6 * D)
    lines = owners // 8
    used = images * 6 * D // 128
    mod_height = -(-used // 16) * 16
    mod_part = matmul(cond_mine, ada_mine).reshape(lines, 2, 2, 2, used, 128)
    mod_part = jnp.pad(
        mod_part.transpose(3, 2, 0, 1, 4, 5), ((0, 0),) * 4 + ((0, mod_height - used), (0, 0))
    )
    image_of, onehot = image_onehot(image_lengths[0], row_count)
    key_zero = jnp.zeros((D,), jnp.float32)
    bias_full = jnp.concatenate([qv_full[:D], key_zero, qv_full[D:]])
    same_image = (image_of[:, None] == image_of[None, :]).astype(jnp.float32)
    onehot = jnp.pad(onehot, ((0, 0), (0, 128 - onehot.shape[1])))
    results = forward(
        owners,
        images,
        (
            quarters[:, :D],
            quarters[:, D : 2 * D],
            down_weight.reshape(-1, D),
            quarters[:, 2 * D :],
            projector_mid.reshape(-1, P_SIZE),
            projector_out.reshape(-1, Z),
        ),
        (
            tokens,
            onehot,
            same_image,
            mod_part,
            ada_bias_full[None],
            bias_full[None],
            tail_full[None],
            up_bias_full[None],
            proj_in_bias_full[None],
            proj_mid_bias_full[None],
            proj_out_bias_full[None],
        ),
        (0, 1, 2, 3, 5, 7, 8),
        1,
    )
    mixed = results[15]
    modulation = results[21]
    sums = backward(
        owners,
        images,
        results[:6],
        (tokens, onehot, same_image, modulation, targets, out_grad) + tuple(results[6:21]),
        mod_height,
        (2, (0, 1, 2, 3, 4, 5, 6), (0, 1, 2, 3, 4, 5, 6), (3, 2, 6)),
        2,
    )
    first_sum, up_sum, down_sum, in_sum, mid_sum, out_sum, tokens_grad = sums[:7]
    qkv_cols, attn_cols, mlp_cols, up_cols, in_cols, mid_cols, out_cols = [part[0] for part in sums[7:14]]
    modulation_all = sums[14].reshape(owners, mod_height, 128)[:, :used].reshape(owners * images, 6 * D)
    grad_ada = transposed_left(cond_mine, modulation_all)
    cond_back = transposed_right(modulation_all, ada_mine).reshape(owners, images * rows)
    bias_parts = [
        by_owner(part, owners)
        for part in (
            jnp.concatenate([qkv_cols[:D], qkv_cols[2 * D :]]),
            jnp.concatenate([attn_cols, mlp_cols]),
            up_cols,
            in_cols,
            mid_cols,
            out_cols,
        )
    ]
    received = lax.all_to_all(jnp.concatenate([cond_back] + bias_parts, axis=1), "fsdp", 0, 0, tiled=True)
    cond_back = received[:, : images * rows].reshape(owners, images, rows).transpose(1, 0, 2).reshape(images, D)
    cond_grad = pull_back(sigmoid_linear, cond_values, cond_back).astype(jnp.bfloat16)
    small = jnp.sum(received[:, images * rows :], axis=0)
    grad_ada_bias = lax.dynamic_slice(
        column_sums(modulation_all), (me * (6 * D // owners),), (6 * D // owners,)
    )
    back = jnp.concatenate([first_sum, up_sum, in_sum], axis=1)
    back = lax.all_to_all(back, "fsdp", 0, 0, axis_index_groups=groups, tiled=True)
    back = back.reshape(4, rows, -1).transpose(1, 0, 2)
    first_rows = back[:, :, :D].reshape(rows, 4 * D)
    small_parts, at = [], 0
    for width in widths[1:]:
        small_parts.append(small[at : at + width // owners])
        at += width // owners
    qv_small, tail_small, up_small, in_small, mid_small, out_small = small_parts
    return (
        mixed,
        tokens_grad,
        cond_grad,
        grad_ada.reshape(-1),
        grad_ada_bias,
        first_rows[:, : 3 * D].reshape(-1),
        qv_small,
        first_rows[:, 3 * D :].reshape(-1),
        tail_small,
        back[:, :, D : 2 * D].reshape(-1),
        up_small,
        down_sum.reshape(-1),
        back[:, :, 2 * D :].reshape(-1),
        in_small,
        mid_sum.reshape(-1),
        mid_small,
        out_sum.reshape(-1),
        out_small,
    )


def solution(mesh):
    in_specs = (
        P("fsdp", None),
        P("fsdp", None),
        P("fsdp", None),
        P("fsdp"),
        P("fsdp"),
        P("fsdp"),
        P("fsdp"),
        P("fsdp"),
        P("fsdp"),
        P("fsdp"),
        P("fsdp"),
        P("fsdp"),
        P("fsdp"),
        P("fsdp"),
        P("fsdp"),
        P("fsdp"),
        P("fsdp"),
        P("fsdp"),
        P("fsdp", None),
        P("fsdp", None),
    )
    out_specs = (
        P("fsdp", None),
        P("fsdp", None),
        P("fsdp", None),
        P("fsdp"),
        P("fsdp"),
        P("fsdp"),
        P("fsdp"),
        P("fsdp"),
        P("fsdp"),
        P("fsdp"),
        P("fsdp"),
        P("fsdp"),
        P("fsdp"),
        P("fsdp"),
        P("fsdp"),
        P("fsdp"),
        P("fsdp"),
        P("fsdp"),
    )
    owners = mesh.shape["fsdp"]
    program = per_device_kernels if owners % 16 == 0 and D % owners == 0 else per_device
    return jax.shard_map(
        program, mesh=mesh, in_specs=in_specs, out_specs=out_specs, check_vma=False
    )
```

```python
import functools

import jax
import jax.numpy as jnp
from jax import lax
from jax.experimental import pallas as pl
from jax.experimental.pallas import tpu as pltpu
from jax.sharding import PartitionSpec as P

D = 1152
HEADS = 16
HD = 72
FF = 4608
P_SIZE = 2048
Z = 768
Z_OUT = Z


EPSILON = 1e-06
PRECISE = lax.Precision.HIGHEST


def layer_norm(values):
    centred = values - jnp.mean(values, axis=-1, keepdims=True)
    spread = jnp.mean(centred * centred, axis=-1, keepdims=True)
    return centred * lax.rsqrt(spread + EPSILON)


def sigmoid_linear(values):
    return values * jax.nn.sigmoid(values)


def gelu_tanh(values):
    inner = 0.7978845608028654 * (values + 0.044715 * values * values * values)
    return 0.5 * values * (1.0 + jnp.tanh(inner))


def image_onehot(lengths, row_count):
    ends = jnp.cumsum(lengths)
    position = jnp.arange(row_count, dtype=jnp.int32)
    image_of = jnp.sum((position[:, None] >= ends[None, :]).astype(jnp.int32), axis=1)
    images = jnp.arange(lengths.shape[0], dtype=jnp.int32)
    return (image_of, (image_of[:, None] == images[None, :]).astype(jnp.float32))


def pull_back(function, point, cotangent):
    return jax.vjp(function, point)[1](cotangent)[0]


def lowered(values):
    return values.astype(jnp.bfloat16)


def matmul(left, right):
    return jnp.dot(left, right, preferred_element_type=jnp.float32)


def transposed_left(left, right):
    return lax.dot_general(
        left, right, (((0,), (0,)), ((), ())), preferred_element_type=jnp.float32
    )


def transposed_right(left, right):
    return lax.dot_general(
        left, right, (((1,), (1,)), ((), ())), preferred_element_type=jnp.float32
    )


def column_sums(values):
    return jnp.sum(values.astype(jnp.float32), axis=0)


def by_owner(values, owners):
    return values.reshape(owners, -1)


def flatten_all(pieces):
    return tuple((piece.reshape(-1) for piece in pieces))


def unpack_mix(gathered):
    return (
        gathered[0].reshape(D, 6 * D),
        gathered[1].astype(jnp.float32),
        gathered[2].reshape(D, 3 * D),
        gathered[3].astype(jnp.float32),
        gathered[4].reshape(D, D),
        gathered[5].astype(jnp.float32),
    )


def unpack_dense(gathered):
    return (
        gathered[0].reshape(D, FF),
        gathered[1].astype(jnp.float32),
        gathered[2].reshape(FF, D),
        gathered[3].reshape(D, P_SIZE),
        gathered[4].astype(jnp.float32),
        gathered[5].reshape(P_SIZE, P_SIZE),
        gathered[6].astype(jnp.float32),
        gathered[7].reshape(P_SIZE, Z),
        gathered[8].astype(jnp.float32),
    )


MESH = pl.DeviceIdType.MESH

class Place:
    def __init__(self, n):
        self.me = me = lax.axis_index("fsdp")
        self.Z = n // 8
        self.z, self.y, self.x, self.c = me // 8, (me // 4) % 2, (me // 2) % 2, me % 2
        self.xp = me + 2 - 4 * self.x
        self.yp = me + 4 - 8 * self.y
        self.cp = me + 1 - 2 * self.c

def barrier(pc, everyone=0):
    sem = pltpu.get_barrier_semaphore()
    if everyone:
        def greet(k, carry):
            pl.semaphore_signal(sem, inc=1, device_id=(lax.rem(pc.me + k, everyone),), device_id_type=MESH)
            return carry
        lax.fori_loop(1, everyone, greet, 0)
        pl.semaphore_wait(sem, everyone - 1)
        return
    for q in (pc.xp, pc.yp, pc.cp):
        pl.semaphore_signal(sem, inc=1, device_id=(q,), device_id_type=MESH)
    @pl.when(pc.z > 0)
    def _():
        pl.semaphore_signal(sem, inc=1, device_id=(pc.me - 8,), device_id_type=MESH)
    @pl.when(pc.z < pc.Z - 1)
    def _():
        pl.semaphore_signal(sem, inc=1, device_id=(pc.me + 8,), device_id_type=MESH)
    ends = (pc.z == 0).astype(jnp.int32) + (pc.z == pc.Z - 1).astype(jnp.int32)
    pl.semaphore_wait(sem, 5 - ends)


SLABBED = (True, True, False, True, False, False)

def gather_rounds():
    out = []
    for a in range(3):
        out += [(a, 0, 384, 1, 0), (a, 384, 256, 1, 1), (a, 640, 384, 1, 0), (a, 1024, 128, 1, 0)]
    out += [(3, 0, 384, 1, 0), (3, 384, 128, 1, 1)]
    out += [(4, 0, 768, 2, 0), (4, 768, 512, 2, 1), (4, 1280, 768, 2, 0)]
    out += [(5, 0, 256, 2, 1), (5, 256, 512, 2, 0)]
    return tuple(out)
CHUNKS = gather_rounds()

def dot(a, b):
    return jnp.dot(a, b, preferred_element_type=jnp.float32)

def dot_nt(a, b):
    return lax.dot_general(a, b, (((1,), (1,)), ((), ())), preferred_element_type=jnp.float32)

def norm_parts(values):
    centred = values - jnp.mean(values, axis=-1, keepdims=True)
    spread = jnp.mean(centred * centred, axis=-1, keepdims=True)
    return centred, lax.rsqrt(spread + EPSILON)

def token_rows(onehot, mod, k):
    images = mod.shape[0] // 6
    total = onehot[:, 0:1] * mod[k * images:k * images + 1]
    for i in range(1, images):
        total = total + onehot[:, i:i + 1] * mod[k * images + i:k * images + i + 1]
    return total

def head_window(h):
    start = jnp.minimum((h * HD) // 128 * 128, D - 256)
    start = pl.multiple_of(start, 128)
    lane = lax.broadcasted_iota(jnp.int32, (1, 256), 1) + start
    return start, (lane >= h * HD) & (lane < h * HD + HD)

def region(out, zs, y, x, c, off, w):
    return out.at[zs, y, x, c, :, pl.ds(off, w)]

def gather_program(n, ins, outs, sems, rounds):
    lsem, zs_sem, zr_sem, xs_sem, xr_sem, cs_sem, cr_sem = sems
    pc = Place(n)
    Z = pc.Z
    z, y, x, c = pc.z, pc.y, pc.x, pc.c
    allz = slice(None); lo = slice(0, Z // 2); hi = slice(Z // 2, Z)
    def plane(r): return rounds[r][4]
    def reg(r, zs, y_, x_):
        a, off, w = rounds[r][:3]
        return region(outs[a], zs, y_, x_, c, off, w)
    def own_in(r):
        a, off, w = rounds[r][:3]
        return ins[a].at[:, pl.ds(off, w)]
    def rcopy(src, dst, ss, rs, dev):
        return pltpu.make_async_remote_copy(src_ref=src, dst_ref=dst, send_sem=ss, recv_sem=rs, device_id=(dev,), device_id_type=MESH)
    def line_part(r, org):
        return reg(r, org, slice(None), slice(None)) if plane(r) else reg(r, org, y, x)
    def zcopy(r, side, s):
        org = z - s if side == 0 else z + s
        dst = line_part(r, org)
        src = own_in(r) if s == 0 and not plane(r) else dst
        return rcopy(src, dst, zs_sem.at[r, side, s], zr_sem.at[r, side, s], pc.me + (8 if side == 0 else -8))
    def zrecv(r, side, s):
        org = z - 1 - s if side == 0 else z + 1 + s
        d = line_part(r, org)
        rcopy(d, d, zs_sem.at[r, side, s], zr_sem.at[r, side, s], pc.me).wait_recv()
    def local(r):
        return pltpu.make_async_copy(own_in(r), reg(r, z, y, x), lsem.at[r])
    def xy(r, k):
        if plane(r):
            if k < 2:
                return rcopy(own_in(r), reg(r, z, y, x), xs_sem.at[r, k], xr_sem.at[r, k], pc.yp if k else pc.xp)
            d = reg(r, z, y, 1 - x) if r % 2 else reg(r, z, 1 - y, x)
            return rcopy(d, d, xs_sem.at[r, 2], xr_sem.at[r, 2], pc.yp if r % 2 else pc.xp)
        if k < 2: d = reg(r, allz, y, x)
        elif k == 2: d = reg(r, lo, y, 1 - x)
        else: d = reg(r, hi, 1 - y, x)
        return rcopy(d, d, xs_sem.at[r, k], xr_sem.at[r, k], pc.xp if k in (0, 3) else pc.yp)
    def core(r, k):
        if plane(r): d = reg(r, allz, slice(None), slice(None))
        else: d = reg(r, allz, y if k in (0, 1) else 1 - y, x if k in (0, 2) else 1 - x)
        return rcopy(d, d, cs_sem.at[r, k], cr_sem.at[r, k], pc.cp)
    def zstart(r, s):
        @pl.when((z - s >= 0) & (z < Z - 1))
        def _(): zcopy(r, 0, s).start()
        @pl.when((z + s <= Z - 1) & (z > 0))
        def _(): zcopy(r, 1, s).start()
    def zwait(r, s):
        @pl.when(z - 1 - s >= 0)
        def _(): zrecv(r, 0, s)
        @pl.when(z + 1 + s <= Z - 1)
        def _(): zrecv(r, 1, s)
    def stage(r, s):
        if plane(r):
            if s == 0:
                local(r).start()
                xy(r, 0).start(); xy(r, 1).start()
            elif s == 1:
                local(r).wait()
                xy(r, 0).wait_recv(); xy(r, 1).wait_recv()
                xy(r, 2).start()
            elif s == 2:
                xy(r, 2).wait_recv()
                zstart(r, 0)
            elif s < Z + 1:
                zwait(r, s - 3)
                zstart(r, s - 2)
            elif s == Z + 1:
                zwait(r, Z - 2)
                core(r, 0).start()
            else:
                core(r, 0).wait_recv()
            return
        if s == 0:
            local(r).start()
            zstart(r, 0)
        elif s < Z - 1:
            zwait(r, s - 1)
            zstart(r, s)
        elif s == Z - 1:
            zwait(r, s - 1)
            local(r).wait()
            xy(r, 0).start(); xy(r, 1).start(); core(r, 0).start()
        elif s == Z:
            xy(r, 0).wait_recv(); xy(r, 2).start(); core(r, 1).start()
            xy(r, 1).wait_recv(); xy(r, 3).start(); core(r, 2).start()
        elif s == Z + 1:
            xy(r, 2).wait_recv(); xy(r, 3).wait_recv(); core(r, 3).start()
        elif s == Z + 2:
            for k in range(4): core(r, k).wait_recv()
    def finish(r):
        for s in range(Z - 1):
            @pl.when((z - s >= 0) & (z < Z - 1))
            def _(): zcopy(r, 0, s).wait_send()
            @pl.when((z + s <= Z - 1) & (z > 0))
            def _(): zcopy(r, 1, s).wait_send()
        for k in range(3 if plane(r) else 4):
            xy(r, k).wait_send()
        for k in range(1 if plane(r) else 4):
            core(r, k).wait_send()
    return stage, finish, Z + 3

def weight_loads(chunk, full, slot, sem, top=0, bottom=None):
    a, off, w, stacks = chunk[:4]
    ref, cps = full[a], []
    rows, sw = ref.shape[4], w // stacks
    bottom = bottom or rows
    for j in range(4):
        for s in range(stacks):
            cps.append((ref.at[:, :, j // 2, j % 2, pl.ds(top, bottom - top), pl.ds(off + s * sw, sw)],
                        slot.at[j, :, :, pl.ds(s * rows + top, bottom - top), pl.ds(0, sw)]))
    return [pltpu.make_async_copy(s, d, sem.at[k]) for k, (s, d) in enumerate(cps)]

def chunk_weight(chunk, slot, rows, part):
    sw = chunk[2] // chunk[3]
    Z = slot.shape[1]
    return jnp.concatenate(
        [slot[j, zz, yy, part * rows:(part + 1) * rows, 0:sw] for zz in range(Z) for yy in range(2) for j in range(4)], axis=0)

def scatter_program(n, R, G, CR, XR, ZR, keep, sems, final):
    cs, cr, xs, xr, zs_, zr, credit = sems
    keep_g, keep_c, keep_x = keep
    pc = Place(n)
    Z = pc.Z; H = Z // 2
    z, y, x, c = pc.z, pc.y, pc.x, pc.c
    up_dev = jnp.minimum(pc.me + 8, n - 1)
    down_dev = jnp.maximum(pc.me - 8, 0)
    def rcopy(src, dst, ss, rs, dev):
        return pltpu.make_async_remote_copy(src_ref=src, dst_ref=dst, send_sem=ss, recv_sem=rs, device_id=(dev,), device_id_type=MESH)
    def signal(k, dev):
        pl.semaphore_signal(credit.at[k], inc=1, device_id=(dev,), device_id_type=MESH)
    def core(r): return rcopy(G(r).at[1 - c], CR(r), cs.at[r], cr.at[r], pc.cp)
    def xy(r, k):
        b, xb = G(r).at[c], XR(r)
        if k == 0: return rcopy(b.at[1 - x, 0:H, 1 - y], xb.at[0:H], xs.at[r, 0], xr.at[r, 0], pc.yp)
        if k == 1: return rcopy(b.at[1 - x, H:Z, 1 - y], xb.at[H:Z], xs.at[r, 1], xr.at[r, 1], pc.xp)
        if k == 2: return rcopy(b.at[1 - x, :, y], xb.at[Z:2 * Z], xs.at[r, 2], xr.at[r, 2], pc.xp)
        return rcopy(b.at[x, :, 1 - y], xb.at[2 * Z:3 * Z], xs.at[r, 3], xr.at[r, 3], pc.yp)
    def zc(r, side, d):
        return rcopy(XR(r).at[Z + d], ZR(r).at[side, d], zs_.at[r, side, d], zr.at[r, side, d], up_dev if side == 0 else down_dev)
    def waits_send(r):
        core(r).wait_send()
        for k in range(4): xy(r, k).wait_send()
    def zwaits_send(r):
        for d in range(Z):
            @pl.when(d > z)
            def _(): zc(r, 0, d).wait_send()
            @pl.when(d < z)
            def _(): zc(r, 1, d).wait_send()
    def zstep(r, s):
        for side in (0, 1):
            p = s if side == 0 else Z - 1 - s
            @pl.when(z == p)
            def _():
                if r >= keep_x and (p < Z - 1 if side == 0 else p > 0):
                    pl.semaphore_wait(credit.at[3 + side], 1)
                for d in range(Z):
                    if (d > p) if side == 0 else (d < p):
                        if s > 0:
                            zc(r, side, d).wait_recv()
                            XR(r)[Z + d] = XR(r)[Z + d] + ZR(r)[side, d]
                        zc(r, side, d).start()
    def before(r):
        if r >= keep_g:
            waits_send(r - keep_g)
    def stage(r, s):
        b = G(r).at[c]
        if s == 0:
            if r >= keep_c:
                pl.semaphore_wait(credit.at[0], 1)
            core(r).start()
        elif s == 1:
            core(r).wait_recv()
            def add(i, carry):
                xx, zz, yy = i // (2 * Z), (i // 2) % Z, i % 2
                b[xx, zz, yy] = b[xx, zz, yy] + CR(r)[xx, zz, yy]
                return carry
            lax.fori_loop(0, 4 * Z, add, 0)
            if r + keep_c < R:
                signal(0, pc.cp)
            if r >= keep_x:
                pl.semaphore_wait(credit.at[1], 1)
                pl.semaphore_wait(credit.at[2], 1)
            xy(r, 0).start(); xy(r, 1).start()
        elif s == 2:
            xy(r, 0).wait_recv()
            def add(i, carry):
                b[1 - x, i, y] = b[1 - x, i, y] + XR(r)[i]
                return carry
            lax.fori_loop(0, H, add, 0)
            xy(r, 2).start()
            xy(r, 1).wait_recv()
            def add(i, carry):
                b[x, i, 1 - y] = b[x, i, 1 - y] + XR(r)[i]
                return carry
            lax.fori_loop(H, Z, add, 0)
            xy(r, 3).start()
        elif s == 3:
            xy(r, 2).wait_recv(); xy(r, 3).wait_recv()
            def add(i, carry):
                XR(r)[Z + i] = b[x, i, y] + XR(r)[Z + i] + XR(r)[2 * Z + i]
                return carry
            lax.fori_loop(0, Z, add, 0)
            zstep(r, 0)
        elif s < Z + 2:
            zstep(r, s - 3)
        else:
            for d in range(Z):
                @pl.when(d == z)
                def _():
                    tot = XR(r)[Z + d].astype(jnp.float32)
                    if d > 0:
                        zc(r, 0, d).wait_recv()
                        tot = tot + ZR(r)[0, d].astype(jnp.float32)
                    if d < Z - 1:
                        zc(r, 1, d).wait_recv()
                        tot = tot + ZR(r)[1, d].astype(jnp.float32)
                    final(r, tot)
            zwaits_send(r)
            if r + keep_x < R:
                signal(1, pc.xp)
                signal(2, pc.yp)
                @pl.when(z < Z - 1)
                def _(): signal(4, up_dev)
                @pl.when(z > 0)
                def _(): signal(3, down_dev)
    def finish():
        for r in range(max(0, R - keep_g), R):
            waits_send(r)
    return before, stage, finish, Z + 3

def scatter_sems(R, Z):
    D_ = pltpu.SemaphoreType.DMA
    return [D_((R,)), D_((R,)), D_((R, 4)), D_((R, 4)), D_((R, 2, Z)), D_((R, 2, Z)), pltpu.SemaphoreType.REGULAR((5,))]

BIASES = (6 * D, 2 * D, 2 * D, FF, P_SIZE, P_SIZE, Z_OUT)

def forward_kernel(n, images, offs, *refs):
    rounds = CHUNKS
    qkv_w, attn_in, up_w, in_w, down_w, mid_w, out_w, ada_w, mail, tokens, onehot, same = refs[:12]
    refs = refs[12:]
    full, refs = refs[:6], refs[6:]
    (first_in, projected, heads, branch_attn, middle, second_in, up_pre, up_act, branch_mlp, mixed,
     first_pre, first_act, second_pre, second_act, features, mod, cond_mine) = refs[:17]
    refs = refs[17:]
    slots, attn_w, first_own, up_own, in_own, box, mod_own, mod_core, mod_xy, mod_line = refs[:10]
    bias_rows, refs = refs[10:17], refs[17:]
    load_sem, mail_send, mail_recv = refs[:3]
    ada_b, qv_b, tail_b, up_b, in_b, mid_b, out_b = bias_rows
    R, Z = len(rounds), n // 8
    pc = Place(n)
    stage, finish, S = gather_program(
        n, (first_own, up_own, down_w, in_own, mid_w, out_w), full, refs[3:10], rounds)
    per = D // n
    for s in range(4):
        first_own[s * per:(s + 1) * per] = qkv_w[:, s * D:(s + 1) * D] if s < 3 else attn_in[...]
        up_own[s * per:(s + 1) * per] = up_w[:, s * (FF // 4):(s + 1) * (FF // 4)]
        in_own[s * per:(s + 1) * per] = in_w[:, s * (P_SIZE // 4):(s + 1) * (P_SIZE // 4)]

    def mod_final(r, tot):
        for k in range(6):
            for i in range(images):
                row = k * images + i
                mod[row:row + 1] = tot[row:row + 1] + ada_b[:, k * D:(k + 1) * D]
    _, mod_stage, mod_finish, _ = scatter_program(
        n, 1, lambda r: mod_own, lambda r: mod_core, lambda r: mod_xy, lambda r: mod_line, (1, 1, 1), refs[10:], mod_final)

    def letter(k):
        dest = lax.rem(pc.me + k, n)
        return pltpu.make_async_remote_copy(
            src_ref=mail.at[dest], dst_ref=box.at[pc.me], send_sem=mail_send.at[k], recv_sem=mail_recv.at[k],
            device_id=(dest,), device_id_type=MESH)

    def send_mail():
        def go(k, carry):
            letter(k).start()
            return carry
        lax.fori_loop(1, n, go, 0)
        box[pc.me] = mail[pc.me]

    def read_mail():
        def wait(k, carry):
            letter(k).wait()
            return carry
        lax.fori_loop(1, n, wait, 0)
        cond_mine[...] = jnp.concatenate([box[d, 0:images, 0:per] for d in range(n)], axis=0)
        row = images
        for ref, width in zip(bias_rows, BIASES):
            part = width // n
            for at in range(0, part, 128):
                size = min(128, part - at)
                for d in range(n):
                    ref[:, d * part + at:d * part + at + size] = box[d, row:row + 1, 0:size].astype(jnp.float32)
                row += 1
        mod_own[...] = jnp.zeros_like(mod_own)
        for k in range(6):
            value = dot(cond_mine[...], ada_w[:, k * D:(k + 1) * D])
            for d in range(n):
                mod_own[d % 2, (d // 2) % 2, d // 8, (d // 4) % 2, k * images:(k + 1) * images] = value[d * images:(d + 1) * images]
    barrier(pc, n)
    last_of = {a: max(r for r in range(R) if rounds[r][0] == a) for a in range(6)}

    def loads(r):
        return weight_loads(rounds[r], full, slots.at[r % 2], load_sem.at[r % 2])

    def prepare():
        oh, md = onehot[...], mod
        values = tokens[...].astype(jnp.float32)
        centred, scale = norm_parts(values)
        first_in[...] = (centred * scale * (1.0 + token_rows(oh, md, 1)) + token_rows(oh, md, 0)).astype(jnp.bfloat16)

    def attention():
        def head(h, carry):
            start, inside = head_window(h)
            q = projected[:, pl.ds(start, 256)]
            k = projected[:, pl.ds(pl.multiple_of(start + D, 128), 256)]
            v = projected[:, pl.ds(pl.multiple_of(start + 2 * D, 128), 256)]
            q = jnp.where(inside, q, jnp.zeros_like(q))
            scores = jnp.where(same[...] > 0.0, dot_nt(q, k) * HD ** (-0.5), -1e30)
            e = jnp.exp(scores - jnp.max(scores, axis=-1, keepdims=True))
            p = (e / jnp.sum(e, axis=-1, keepdims=True)).astype(jnp.bfloat16)
            o = dot(p, v).astype(jnp.bfloat16)
            heads[:, pl.ds(start, 256)] = jnp.where(inside, o, heads[:, pl.ds(start, 256)])
            return carry
        heads[...] = jnp.zeros_like(heads)
        lax.fori_loop(0, HEADS, head, 0)
        for i in range(3):
            cols = slice(384 * i, 384 * (i + 1))
            branch_attn[:, cols] = dot(heads[...], attn_w[:, cols]) + tail_b[:, cols]
        oh, md = onehot[...], mod
        mid = tokens[...].astype(jnp.float32) + token_rows(oh, md, 2) * branch_attn[...]
        middle[...] = mid
        centred, scale = norm_parts(mid)
        second_in[...] = (centred * scale * (1.0 + token_rows(oh, md, 4)) + token_rows(oh, md, 3)).astype(jnp.bfloat16)

    def compute(r):
        a, off, w, stacks = rounds[r][:4]
        slot = slots.at[r % 2]
        sw = w // stacks
        def weight(part):
            return chunk_weight(rounds[r], slot, per if SLABBED[a] else slot_rows[a], part)
        if a == 0:
            for j in range(3):
                cols = slice(j * D + off, j * D + off + w)
                value = dot(first_in[...], weight(j))
                if j != 1:
                    at = (j // 2) * D + off
                    value = value + qv_b[:, at:at + w]
                projected[:, cols] = value.astype(jnp.bfloat16)
            attn_w[:, off:off + w] = weight(3)
            if r == last_of[0]:
                attention()
        elif a == 1:
            for j in range(4):
                cols = slice(j * (FF // 4) + off, j * (FF // 4) + off + w)
                pre = dot(second_in[...], weight(j)) + up_b[:, cols]
                up_pre[:, cols] = pre
                up_act[:, cols] = gelu_tanh(pre).astype(jnp.bfloat16)
        elif a == 2:
            branch_mlp[:, off:off + w] = dot(up_act[...], weight(0)) + tail_b[:, D + off:D + off + w]
            if r == last_of[2]:
                hidden = middle[...] + token_rows(onehot[...], mod, 5) * branch_mlp[...]
                mixed[...] = hidden.astype(jnp.bfloat16)
        elif a == 3:
            for j in range(4):
                cols = slice(j * (P_SIZE // 4) + off, j * (P_SIZE // 4) + off + w)
                pre = dot(mixed[...], weight(j)) + in_b[:, cols]
                first_pre[:, cols] = pre
                first_act[:, cols] = sigmoid_linear(pre).astype(jnp.bfloat16)
        else:
            for s in range(stacks):
                cols = slice(off + s * sw, off + (s + 1) * sw)
                if a == 4:
                    pre = dot(first_act[...], weight(s)) + mid_b[:, cols]
                    second_pre[:, cols] = pre
                    second_act[:, cols] = sigmoid_linear(pre).astype(jnp.bfloat16)
                else:
                    features[:, cols] = dot(second_act[...], weight(s)) + out_b[:, cols]
    slot_rows = {2: FF // n, 4: P_SIZE // n, 5: P_SIZE // n}

    offs_of = lambda r: offs[rounds[r][4]]
    ready = [max(r2 + offs_of(r2)[S - 1] for r2 in range(r + 1)) for r in range(R)]
    mod_at = 2
    t, computed, loaded, began = 0, 0, 0, []
    while computed < R:
        for s in reversed(range(S)):
            for r in range(R):
                if r + offs_of(r)[s] == t:
                    stage(r, s)
        if t == 0:
            send_mail()
        if t == mod_at:
            read_mail()
        if mod_at <= t < mod_at + Z + 3:
            mod_stage(0, t - mod_at)
        if t == mod_at + Z + 2:
            prepare()
        done_now = 0
        while True:
            while loaded < R and ready[loaded] <= t and loaded < computed + 2:
                for cp in loads(loaded): cp.start()
                loaded += 1
                began.append(t)
            if computed == loaded or t < mod_at + Z + 2 or (t < ready[-1] and (done_now == 2 or began[computed] == t)):
                break
            for cp in loads(computed): cp.wait()
            compute(computed)
            computed += 1
            done_now += 1
        t += 1
    for r in range(R):
        finish(r)
    mod_finish()

def forward(n, images, shards, small, offs, cid):
    Z, R = n // 8, len(CHUNKS)
    f32, bf = jnp.float32, jnp.bfloat16
    tok = small[2].shape[0]
    blocks = ((4 * D // n, D), (4 * D // n, FF // 4), (FF // n, D), (4 * D // n, P_SIZE // 4), (P_SIZE // n, P_SIZE), (P_SIZE // n, Z_OUT))
    shapes = [jax.ShapeDtypeStruct((Z, 2, 2, 2) + b, bf) for b in blocks]
    acts = [(D, bf), (3 * D, bf), (D, bf), (D, f32), (D, f32), (D, bf), (FF, f32), (FF, bf), (D, f32), (D, bf),
            (P_SIZE, f32), (P_SIZE, bf), (P_SIZE, f32), (P_SIZE, bf), (Z_OUT, f32)]
    shapes += [jax.ShapeDtypeStruct((tok, w), dt) for w, dt in acts]
    mod_dims = (-(-6 * images // 8) * 8, D)
    shapes.append(jax.ShapeDtypeStruct((6 * images, D), f32))
    shapes.append(jax.ShapeDtypeStruct((n * images, D // n), bf))
    D_, V = pltpu.SemaphoreType.DMA, pltpu.VMEM
    hbm, vmem = pl.BlockSpec(memory_space=pltpu.HBM), pl.BlockSpec(memory_space=pltpu.VMEM)
    return pl.pallas_call(
        functools.partial(forward_kernel, n, images, offs),
        out_shape=shapes,
        in_specs=[vmem] * 4 + [hbm] * 3 + [vmem] * len(small),
        out_specs=[hbm] * 6 + [vmem] * (len(acts) + 2),
        scratch_shapes=[
            V((2, 4, Z, 2, 144, 384), bf), V((D, D), bf), V(blocks[0], bf), V(blocks[1], bf), V(blocks[3], bf),
            V((n, 16, 128), bf),
            V((2, 2, Z, 2) + mod_dims, f32), V((2, Z, 2) + mod_dims, f32), V((3 * Z,) + mod_dims, f32), V((2, Z) + mod_dims, f32),
        ] + [V((1, w), f32) for w in BIASES] + [
            D_((2, 8)), D_((n,)), D_((n,)),
            D_((R,)), D_((R, 2, Z - 1)), D_((R, 2, Z - 1)), D_((R, 4)), D_((R, 4)), D_((R, 4)), D_((R, 4)),
        ] + scatter_sems(1, Z),
        compiler_params=pltpu.CompilerParams(collective_id=cid, has_side_effects=True, vmem_limit_bytes=58 * 2**20),
    )(*shards, *small)


BACK_CHUNKS = (
    ((5, 0, 768, 2),)
    + ((4, 0, 768, 2), (4, 768, 768, 2), (4, 1536, 512, 2))
    + ((3, 0, 384, 1), (3, 384, 128, 1))
    + tuple((2, 384 * i, 384, 1) for i in range(3))
    + tuple((1, 384 * i, 384, 1) for i in range(3))
    + tuple((0, 384 * i, 384, 1) for i in range(3))
)
CHAIN = BACK_CHUNKS[:12] + tuple((6, 384 * i, 384, 1) for i in range(3)) + BACK_CHUNKS[12:]

def dot_tn(a, b):
    return lax.dot_general(a, b, (((0,), (0,)), ((), ())), preferred_element_type=jnp.float32)

def norm_back(centred, scale, grad):
    normed = centred * scale
    inner = jnp.mean(grad * normed, axis=-1, keepdims=True)
    return scale * (grad - jnp.mean(grad, axis=-1, keepdims=True) - normed * inner)

def sigmoid_linear_slope(v):
    s = jax.nn.sigmoid(v)
    return s * (1.0 + v * (1.0 - s))

def gelu_slope(v):
    t = jnp.tanh(0.7978845608028654 * (v + 0.044715 * v * v * v))
    return 0.5 * (1.0 + t) + 0.5 * v * (1.0 - t * t) * 0.7978845608028654 * (1.0 + 3.0 * 0.044715 * v * v)

def backward_kernel(n, images, chain_per_tick, scatter_offs, mod_offs, *refs):
    Z = n // 8
    full, refs = refs[:6], refs[6:]
    (tokens, onehot, same, mod, targets, out_grad, first_in, projected, heads, branch_attn, middle, second_in,
     up_pre, up_act, branch_mlp, mixed, first_pre, first_act, second_pre, second_act, features) = refs[:21]
    refs = refs[21:]
    outs, refs = refs[:7], refs[7:]
    tokens_grad, qkv_sums, attn_sums, mlp_sums, up_sums, in_sums, mid_sums, out_sums, mod_all = refs[:9]
    refs = refs[9:]
    (slots, load_sem, G_, CR_, XR_, ZR_, feature_grad, second_back, first_back, hidden_grad, mlp_grad, up_grad,
     middle_grad, attn_grad, heads_grad, projected_grad, wide, narrow, mod_grad, mod_rows, mod_lines) = refs[:21]
    refs = refs[21:]
    rounds, R = BACK_CHUNKS, len(BACK_CHUNKS)
    per = D // n
    bf = jnp.bfloat16
    pc = Place(n)

    def dims(r):
        a, off, w, stacks = rounds[r]
        return (4 * per if a < 4 else stacks * (P_SIZE // n)), w // stacks
    keep = (G_.shape[0], CR_.shape[0], XR_.shape[0])
    def cut(ref, r):
        rows, w = dims(r)
        lead = (slice(None),) * (len(ref.shape) - 3)
        return ref.at[(r % ref.shape[0],) + lead + (slice(0, rows), slice(0, w))]
    def final(r, tot):
        a, off, w, stacks = rounds[r]
        rows, sw = dims(r)
        qkv_out, attn_out, up_out, down_out, in_out, mid_out, out_out = outs
        if SLABBED[a]:
            for s in range(4):
                part = tot[s * per:(s + 1) * per]
                if a == 0 and s == 3:
                    attn_out[:, off:off + w] = part
                else:
                    ref, q = {0: (qkv_out, D), 1: (up_out, FF // 4), 3: (in_out, P_SIZE // 4)}[a]
                    ref[:, s * q + off:s * q + off + w] = part
        else:
            rows = rows // stacks
            ref = {2: down_out, 4: mid_out, 5: out_out}[a]
            for s in range(stacks):
                ref[:, off + s * sw:off + (s + 1) * sw] = tot[s * rows:(s + 1) * rows]
    before, stage, finish, S = scatter_program(
        n, R, lambda r: cut(G_, r), lambda r: cut(CR_, r), lambda r: cut(XR_, r), lambda r: cut(ZR_, r), keep, refs[:7], final)
    mod_stage, mod_finish, _ = gather_program(n, [mod_rows], [mod_all], refs[7:], ((0, 0, 128, 1, 0),))
    barrier(pc)
    mod_lines[...] = jnp.zeros_like(mod_lines)

    def image_sums(k, value):
        cols = slice(k * D, (k + 1) * D)
        for i in range(images):
            mod_grad[i:i + 1, cols] = jnp.sum(value * onehot[:, i:i + 1], axis=0, keepdims=True)

    def sums(value):
        return jnp.sum(value.astype(jnp.float32), axis=0, keepdims=True)

    def start_chain():
        f, t = features[...], targets[...].astype(jnp.float32)
        f_norm = jnp.sqrt(jnp.sum(f * f, axis=1, keepdims=True) + EPSILON)
        t_norm = jnp.sqrt(jnp.sum(t * t, axis=1, keepdims=True) + EPSILON)
        inner = jnp.sum(f * t, axis=1, keepdims=True)
        grad = -0.5 * (t / (f_norm * t_norm) - f * (inner / (f_norm * f_norm * f_norm * t_norm)))
        feature_grad[...] = grad.astype(bf)
        out_sums[...] = sums(feature_grad[...])

    def attention_back():
        projected_grad[...] = jnp.zeros_like(projected_grad)
        def head(h, carry):
            start, inside = head_window(h)
            at_q, at_k, at_v = [pl.ds(pl.multiple_of(start + i * D, 128), 256) for i in range(3)]
            q, k, v = projected[:, at_q], projected[:, at_k], projected[:, at_v]
            q = jnp.where(inside, q, jnp.zeros_like(q))
            g = heads_grad[:, at_q]
            g = jnp.where(inside, g, jnp.zeros_like(g))
            scores = jnp.where(same[...] > 0.0, dot_nt(q, k) * HD ** (-0.5), -1e30)
            e = jnp.exp(scores - jnp.max(scores, axis=-1, keepdims=True))
            p = e / jnp.sum(e, axis=-1, keepdims=True)
            pg = dot_nt(g, v)
            sg = (p * (pg - jnp.sum(p * pg, axis=-1, keepdims=True))).astype(bf)
            for at, value in (
                (at_q, dot(sg, k) * HD ** (-0.5)),
                (at_k, dot_tn(sg, q) * HD ** (-0.5)),
                (at_v, dot_tn(p.astype(bf), g)),
            ):
                projected_grad[:, at] = jnp.where(inside, value.astype(bf), projected_grad[:, at])
            return carry
        lax.fori_loop(0, HEADS, head, 0)
        qkv_sums[...] = sums(projected_grad[...])

    C = len(CHAIN)
    last = {a: max(k for k in range(C) if CHAIN[k][0] == a) for a in range(7)}
    first = {a: min(k for k in range(C) if CHAIN[k][0] == a) for a in range(7)}

    def chain_loads(k):
        a, off, w, stacks = CHAIN[k]
        slot, sem = slots.at[k % 2], load_sem.at[k % 2]
        if a == 6:
            return weight_loads((0, off, w, stacks), full, slot, sem, 3 * per // 16 * 16)
        return weight_loads((a, off, w, stacks), full, slot, sem, 0, -(-3 * per // 16) * 16 if a == 0 else None)

    def accumulate(acc, cols, new, k, a):
        acc[:, cols] = new if k == first[a] else acc[:, cols] + new

    def chain(k):
        a, off, w, stacks = CHAIN[k]
        slot = slots.at[k % 2]
        sw = w // stacks
        if a in (4, 5):
            grad = second_back if a == 4 else feature_grad
            new = None
            for s in range(stacks):
                part = dot_nt(grad[:, off + s * sw:off + (s + 1) * sw], chunk_weight(CHAIN[k], slot, P_SIZE // n, s))
                new = part if new is None else new + part
            accumulate(wide, slice(0, P_SIZE), new, k, a)
            if k == last[a]:
                target, pre = (second_back, second_pre) if a == 5 else (first_back, first_pre)
                target[...] = (wide[:, 0:P_SIZE] * sigmoid_linear_slope(pre[...])).astype(bf)
                (mid_sums if a == 5 else in_sums)[...] = sums(target[...])
        elif a == 2:
            whole = chunk_weight(CHAIN[k], slot, FF // n, 0)
            for q in range(4):
                weight = whole[q * D:(q + 1) * D]
                accumulate(wide, slice(q * D, (q + 1) * D), dot_nt(mlp_grad[:, off:off + w], weight), k, a)
            if k == last[a]:
                for q in range(4):
                    cols = slice(q * D, (q + 1) * D)
                    up_grad[:, cols] = (wide[:, cols] * gelu_slope(up_pre[:, cols])).astype(bf)
                up_sums[...] = sums(up_grad[...])
        else:
            src, parts, width = {3: (first_back, range(4), P_SIZE // 4), 1: (up_grad, range(4), FF // 4),
                                 0: (projected_grad, range(3), D), 6: (attn_grad, range(3, 4), D)}[a]
            new = None
            for j in parts:
                col = off if a == 6 else j * width + off
                weight = chunk_weight(CHAIN[k], slot, per, j)
                part = dot_nt(src[:, col:col + w], weight)
                new = part if new is None else new + part
            accumulate(narrow, slice(0, D), new, k, a)
            if k == last[a]:
                oh = onehot[...]
                if a == 3:
                    hg = out_grad[...].astype(jnp.float32) + narrow[...]
                    hidden_grad[...] = hg
                    mlp_grad[...] = (hg * token_rows(oh, mod, 5)).astype(bf)
                    mlp_sums[...] = sums(mlp_grad[...])
                    image_sums(5, hg * branch_mlp[...])
                elif a == 1:
                    g = narrow[...]
                    centred, scale = norm_parts(middle[...])
                    image_sums(3, g)
                    image_sums(4, g * (centred * scale))
                    mg = hidden_grad[...] + norm_back(centred, scale, g * (1.0 + token_rows(oh, mod, 4)))
                    middle_grad[...] = mg
                    attn_grad[...] = (mg * token_rows(oh, mod, 2)).astype(bf)
                    attn_sums[...] = sums(attn_grad[...])
                    image_sums(2, mg * branch_attn[...])
                elif a == 6:
                    heads_grad[...] = narrow[...].astype(bf)
                    attention_back()
                else:
                    g = narrow[...]
                    centred, scale = norm_parts(tokens[...].astype(jnp.float32))
                    image_sums(0, g)
                    image_sums(1, g * (centred * scale))
                    tg = middle_grad[...] + norm_back(centred, scale, g * (1.0 + token_rows(oh, mod, 1)))
                    tokens_grad[...] = tg.astype(bf)
                    stacked = mod_grad[...]
                    rows = 6 * D // 128
                    for i in range(images):
                        for k in range(rows):
                            mod_lines[i * rows + k:i * rows + k + 1] = stacked[i:i + 1, 128 * k:128 * (k + 1)]
                    mod_rows[...] = mod_lines[...].astype(bf)

    def produce(r):
        a, off, w, stacks = rounds[r]
        before(r)
        left, right = {5: (second_act, feature_grad), 4: (first_act, second_back), 3: (mixed, first_back), 2: (up_act, mlp_grad),
                       1: (second_in, up_grad), 0: (first_in, projected_grad)}[a]
        rows, sw = dims(r)
        g = cut(G_, r)
        def put(d, at, value):
            g[d % 2, (d // 2) % 2, d // 8, (d // 4) % 2, at:at + value.shape[0]] = value
        if SLABBED[a]:
            for s in range(4):
                if a == 0 and s == 3:
                    value = dot_tn(heads[...], attn_grad[:, off:off + w])
                else:
                    at = {3: P_SIZE // 4, 1: FF // 4, 0: D}[a] * s + off
                    value = dot_tn(left[...], right[:, at:at + w])
                value = value.astype(bf)
                for d in range(n):
                    put(d, s * per, value[d * per:(d + 1) * per])
        else:
            rows = rows // stacks
            piece = 1152 if a == 2 else 1024
            for s in range(stacks):
                for part in range(left.shape[1] // piece):
                    at = off + s * sw
                    value = dot_tn(left[:, part * piece:(part + 1) * piece], right[:, at:at + sw]).astype(bf)
                    for i in range(piece // rows):
                        put(part * (piece // rows) + i, s * rows, value[i * rows:(i + 1) * rows])

    need = {5: 0, 4: first[4], 3: first[3], 2: first[2], 1: first[1], 0: first[0]}
    done = 0
    mod_start = None
    for cp in chain_loads(0): cp.start()
    start_chain()
    t = 0
    while True:
        busy = False
        for s in reversed(range(1, S)):
            r = t - scatter_offs[s]
            if 0 <= r < R:
                stage(r, s); busy = True
        if t < R:
            busy = True
            while done < need[rounds[t][0]]:
                done = advance(done, chain_loads, chain, C)
            produce(t)
            stage(t, 0)
        for _ in range(chain_per_tick):
            if done < C:
                done = advance(done, chain_loads, chain, C)
        if done == C and mod_start is None:
            mod_start = t
        if mod_start is not None:
            for s in reversed(range(Z + 3)):
                if t - mod_start == mod_offs[s]:
                    mod_stage(0, s)
            busy = busy or t - mod_start < mod_offs[-1]
        if not busy:
            break
        t += 1
    finish()
    mod_finish(0)

def advance(k, chain_loads, chain, total):
    if k + 1 < total:
        for cp in chain_loads(k + 1): cp.start()
    for cp in chain_loads(k): cp.wait()
    chain(k)
    return k + 1

def backward(n, images, weights, acts, mod_height, plan, cid):
    Z, R = n // 8, len(BACK_CHUNKS)
    f32, bf = jnp.float32, jnp.bfloat16
    tok = acts[0].shape[0]
    chain_per_tick, scatter_offs, mod_offs, keep = plan
    shapes = [jax.ShapeDtypeStruct((k // n, w), f32) for k, w in (
        (D, 3 * D), (D, D), (D, FF), (FF, D), (D, P_SIZE), (P_SIZE, P_SIZE), (P_SIZE, Z_OUT))]
    shapes.append(jax.ShapeDtypeStruct((tok, D), bf))
    shapes += [jax.ShapeDtypeStruct((1, w), f32) for w in (3 * D, D, D, FF, P_SIZE, P_SIZE, Z_OUT)]
    hbm, vmem = pl.BlockSpec(memory_space=pltpu.HBM), pl.BlockSpec(memory_space=pltpu.VMEM)
    shapes.append(jax.ShapeDtypeStruct((Z, 2, 2, 2, mod_height, 128), bf))
    D_ = pltpu.SemaphoreType.DMA
    V = pltpu.VMEM
    return pl.pallas_call(
        functools.partial(backward_kernel, n, images, chain_per_tick, scatter_offs, mod_offs),
        out_shape=shapes,
        in_specs=[hbm] * 6 + [vmem] * len(acts),
        out_specs=[vmem] * 15 + [hbm],
        scratch_shapes=[
            V((2, 4, Z, 2, 144, 384), bf),
            D_((2, 8)),
            V((keep[0], 2, 2, Z, 2, 144, 384), bf),
            V((keep[1], 2, Z, 2, 144, 384), bf),
            V((keep[2], 3 * Z, 144, 384), bf),
            V((keep[2], 2, Z, 144, 384), bf),
            V((tok, Z_OUT), bf), V((tok, P_SIZE), bf), V((tok, P_SIZE), bf), V((tok, D), f32), V((tok, D), bf), V((tok, FF), bf),
            V((tok, D), f32), V((tok, D), bf), V((tok, D), bf), V((tok, 3 * D), bf), V((tok, FF), f32), V((tok, D), f32),
            V((images, 6 * D), f32), V((mod_height, 128), bf), V((mod_height, 128), f32),
        ] + scatter_sems(R, Z)
        + [D_((1,)), D_((1, 2, Z - 1)), D_((1, 2, Z - 1)), D_((1, 4)), D_((1, 4)), D_((1, 4)), D_((1, 4))],
        compiler_params=pltpu.CompilerParams(collective_id=cid, has_side_effects=True, vmem_limit_bytes=61 * 2**20),
    )(*weights, *acts)


def per_device(
    tokens,
    cond,
    image_lengths,
    ada_weight,
    ada_bias,
    qkv_weight,
    qv_bias,
    attn_weight,
    tail_bias,
    up_weight,
    up_bias,
    down_weight,
    projector_in,
    projector_in_bias,
    projector_mid,
    projector_mid_bias,
    projector_out,
    projector_out_bias,
    targets,
    out_grad,
):
    owners = lax.axis_size("fsdp")
    mix_gathered = (
        lax.all_gather(ada_weight, "fsdp", axis=0, tiled=True),
        lax.all_gather(ada_bias, "fsdp", axis=0, tiled=True),
        lax.all_gather(qkv_weight, "fsdp", axis=0, tiled=True),
        lax.all_gather(qv_bias, "fsdp", axis=0, tiled=True),
        lax.all_gather(attn_weight, "fsdp", axis=0, tiled=True),
        lax.all_gather(tail_bias, "fsdp", axis=0, tiled=True),
    )
    mix_full = unpack_mix(mix_gathered)
    ada_full, ada_bias_full, qkv_full, qv_full, attn_full, tail_full = mix_full
    row_count = tokens.shape[0]
    cond_values = cond.astype(jnp.float32)
    cond_low = lowered(sigmoid_linear(cond_values))
    modulation = matmul(cond_low, ada_full) + ada_bias_full
    image_of, onehot = image_onehot(image_lengths[0], row_count)
    per_token = jnp.dot(onehot, modulation, precision=PRECISE)
    shift_one, scale_one, gate_one, shift_two, scale_two, gate_two = jnp.split(per_token, 6, axis=1)
    inputs = tokens.astype(jnp.float32)
    normed_one = layer_norm(inputs)
    first_in = lowered(normed_one * (1.0 + scale_one) + shift_one)
    key_zero = jnp.zeros((D,), jnp.float32)
    bias_full = jnp.concatenate([qv_full[:D], key_zero, qv_full[D:]])
    projected = lowered(matmul(first_in, qkv_full) + bias_full)
    queries = projected[:, :D].reshape(row_count, HEADS, HD)
    keys_all = projected[:, D : 2 * D].reshape(row_count, HEADS, HD)
    values_all = projected[:, 2 * D :].reshape(row_count, HEADS, HD)
    same_image = (image_of[:, None] == image_of[None, :])[None]
    score_scale = HD ** (-0.5)

    def masked_scores():
        raw_scores = (
            jnp.einsum("qhd,khd->hqk", queries, keys_all, preferred_element_type=jnp.float32)
            * score_scale
        )
        return jnp.where(same_image, raw_scores, -1e30)

    masked = masked_scores()
    row_max = jnp.max(masked, axis=-1, keepdims=True)
    exp_scores = jnp.exp(masked - row_max)
    row_total = jnp.sum(exp_scores, axis=-1, keepdims=True)
    attn_probs = exp_scores / row_total
    head_out = jnp.einsum(
        "hqk,khd->qhd", lowered(attn_probs), values_all, preferred_element_type=jnp.float32
    )
    heads_low = lowered(head_out.reshape(row_count, D))
    branch_attn = matmul(heads_low, attn_full) + tail_full[:D]
    middle = inputs + gate_one * branch_attn
    normed_two = layer_norm(middle)
    second_in = lowered(normed_two * (1.0 + scale_two) + shift_two)
    dense_gathered = (
        lax.all_gather(up_weight, "fsdp", axis=0, tiled=True),
        lax.all_gather(up_bias, "fsdp", axis=0, tiled=True),
        lax.all_gather(down_weight, "fsdp", axis=0, tiled=True),
        lax.all_gather(projector_in, "fsdp", axis=0, tiled=True),
        lax.all_gather(projector_in_bias, "fsdp", axis=0, tiled=True),
        lax.all_gather(projector_mid, "fsdp", axis=0, tiled=True),
        lax.all_gather(projector_mid_bias, "fsdp", axis=0, tiled=True),
        lax.all_gather(projector_out, "fsdp", axis=0, tiled=True),
        lax.all_gather(projector_out_bias, "fsdp", axis=0, tiled=True),
    )
    dense_full = unpack_dense(dense_gathered)
    (
        up_full,
        up_bias_full,
        down_full,
        proj_in_full,
        proj_in_bias_full,
        proj_mid_full,
        proj_mid_bias_full,
        proj_out_full,
        proj_out_bias_full,
    ) = dense_full
    up_pre = matmul(second_in, up_full) + up_bias_full
    up_act = lowered(gelu_tanh(up_pre))
    branch_mlp = matmul(up_act, down_full) + tail_full[D:]
    hidden = middle + gate_two * branch_mlp
    mixed = lowered(hidden)
    first_pre = matmul(mixed, proj_in_full) + proj_in_bias_full
    first_act = lowered(sigmoid_linear(first_pre))
    second_pre = matmul(first_act, proj_mid_full) + proj_mid_bias_full
    second_act = lowered(sigmoid_linear(second_pre))
    features = matmul(second_act, proj_out_full) + proj_out_bias_full
    target_values = targets.astype(jnp.float32)

    def cosine_loss(values):
        value_norm = jnp.sqrt(jnp.sum(values * values, axis=1) + EPSILON)
        target_norm = jnp.sqrt(jnp.sum(target_values * target_values, axis=1) + EPSILON)
        return -0.5 * jnp.sum(jnp.sum(values * target_values, axis=1) / (value_norm * target_norm))

    feature_grad = lowered(jax.grad(cosine_loss)(features))
    dense_again = (
        lax.all_gather(up_weight, "fsdp", axis=0, tiled=True),
        lax.all_gather(up_bias, "fsdp", axis=0, tiled=True),
        lax.all_gather(down_weight, "fsdp", axis=0, tiled=True),
        lax.all_gather(projector_in, "fsdp", axis=0, tiled=True),
        lax.all_gather(projector_in_bias, "fsdp", axis=0, tiled=True),
        lax.all_gather(projector_mid, "fsdp", axis=0, tiled=True),
        lax.all_gather(projector_mid_bias, "fsdp", axis=0, tiled=True),
        lax.all_gather(projector_out, "fsdp", axis=0, tiled=True),
        lax.all_gather(projector_out_bias, "fsdp", axis=0, tiled=True),
    )
    dense_back = unpack_dense(dense_again)
    up_back = dense_back[0]
    down_back = dense_back[2]
    proj_in_back = dense_back[3]
    proj_mid_back = dense_back[5]
    proj_out_back = dense_back[7]
    grad_proj_out = transposed_left(second_act, feature_grad)
    second_back = lowered(
        pull_back(sigmoid_linear, second_pre, transposed_right(feature_grad, proj_out_back))
    )
    grad_proj_mid = transposed_left(first_act, second_back)
    first_back = lowered(
        pull_back(sigmoid_linear, first_pre, transposed_right(second_back, proj_mid_back))
    )
    grad_proj_in = transposed_left(mixed, first_back)
    hidden_grad = out_grad.astype(jnp.float32) + transposed_right(first_back, proj_in_back)
    gate_two_grad = hidden_grad * branch_mlp
    branch_mlp_grad = lowered(hidden_grad * gate_two)
    grad_down = transposed_left(up_act, branch_mlp_grad)
    up_grad = lowered(pull_back(gelu_tanh, up_pre, transposed_right(branch_mlp_grad, down_back)))
    grad_up = transposed_left(second_in, up_grad)
    second_in_grad = transposed_right(up_grad, up_back)
    middle_grad = hidden_grad + pull_back(layer_norm, middle, second_in_grad * (1.0 + scale_two))
    up_rows = by_owner(grad_up, owners)
    up_bias_rows = by_owner(column_sums(up_grad), owners)
    down_rows = by_owner(grad_down, owners)
    proj_in_rows = by_owner(grad_proj_in, owners)
    proj_in_sums = by_owner(column_sums(first_back), owners)
    proj_mid_rows = by_owner(grad_proj_mid, owners)
    proj_mid_sums = by_owner(column_sums(second_back), owners)
    proj_out_rows = by_owner(grad_proj_out, owners)
    proj_out_sums = by_owner(column_sums(feature_grad), owners)
    dense_grads = flatten_all(
        (
            lax.psum_scatter(up_rows, "fsdp", scatter_dimension=0, tiled=True),
            lax.psum_scatter(up_bias_rows, "fsdp", scatter_dimension=0, tiled=True),
            lax.psum_scatter(down_rows, "fsdp", scatter_dimension=0, tiled=True),
            lax.psum_scatter(proj_in_rows, "fsdp", scatter_dimension=0, tiled=True),
            lax.psum_scatter(proj_in_sums, "fsdp", scatter_dimension=0, tiled=True),
            lax.psum_scatter(proj_mid_rows, "fsdp", scatter_dimension=0, tiled=True),
            lax.psum_scatter(proj_mid_sums, "fsdp", scatter_dimension=0, tiled=True),
            lax.psum_scatter(proj_out_rows, "fsdp", scatter_dimension=0, tiled=True),
            lax.psum_scatter(proj_out_sums, "fsdp", scatter_dimension=0, tiled=True),
        )
    )
    mix_again = (
        lax.all_gather(ada_weight, "fsdp", axis=0, tiled=True),
        lax.all_gather(ada_bias, "fsdp", axis=0, tiled=True),
        lax.all_gather(qkv_weight, "fsdp", axis=0, tiled=True),
        lax.all_gather(qv_bias, "fsdp", axis=0, tiled=True),
        lax.all_gather(attn_weight, "fsdp", axis=0, tiled=True),
        lax.all_gather(tail_bias, "fsdp", axis=0, tiled=True),
    )
    mix_back = unpack_mix(mix_again)
    ada_back = mix_back[0]
    qkv_back = mix_back[2]
    attn_back = mix_back[4]
    gate_one_grad = middle_grad * branch_attn
    branch_attn_grad = lowered(middle_grad * gate_one)
    grad_attn = transposed_left(heads_low, branch_attn_grad)
    heads_grad = lowered(transposed_right(branch_attn_grad, attn_back)).reshape(
        row_count, HEADS, HD
    )
    again_probs = jnp.exp(masked_scores() - row_max) / row_total
    prob_grad = jnp.einsum(
        "qhd,khd->hqk", heads_grad, values_all, preferred_element_type=jnp.float32
    )
    value_grad = jnp.einsum(
        "hqk,qhd->khd", lowered(again_probs), heads_grad, preferred_element_type=jnp.float32
    )
    score_grad = lowered(
        again_probs * (prob_grad - jnp.sum(again_probs * prob_grad, axis=-1, keepdims=True))
    )
    query_grad = (
        jnp.einsum("hqk,khd->qhd", score_grad, keys_all, preferred_element_type=jnp.float32)
        * score_scale
    )
    key_grad = (
        jnp.einsum("hqk,qhd->khd", score_grad, queries, preferred_element_type=jnp.float32)
        * score_scale
    )
    projected_grad = lowered(
        jnp.concatenate(
            [
                query_grad.reshape(row_count, D),
                key_grad.reshape(row_count, D),
                value_grad.reshape(row_count, D),
            ],
            axis=1,
        )
    )
    grad_qkv = transposed_left(first_in, projected_grad)
    projected_sums = column_sums(projected_grad)
    grad_qv_bias = jnp.concatenate([projected_sums[:D], projected_sums[2 * D :]])
    first_in_grad = transposed_right(projected_grad, qkv_back)
    input_grad = middle_grad + pull_back(layer_norm, inputs, first_in_grad * (1.0 + scale_one))
    token_mod_grad = jnp.concatenate(
        [
            first_in_grad,
            first_in_grad * normed_one,
            gate_one_grad,
            second_in_grad,
            second_in_grad * normed_two,
            gate_two_grad,
        ],
        axis=1,
    )
    modulation_grad = lowered(
        lax.dot_general(onehot, token_mod_grad, (((0,), (0,)), ((), ())), precision=PRECISE)
    )
    grad_ada = transposed_left(cond_low, modulation_grad)
    cond_grad = pull_back(
        sigmoid_linear, cond_values, transposed_right(modulation_grad, ada_back)
    ).astype(jnp.bfloat16)
    grad_tail = jnp.concatenate([column_sums(branch_attn_grad), column_sums(branch_mlp_grad)])
    ada_rows = by_owner(grad_ada, owners)
    ada_sums = by_owner(column_sums(modulation_grad), owners)
    qkv_rows = by_owner(grad_qkv, owners)
    qv_rows = by_owner(grad_qv_bias, owners)
    attn_rows = by_owner(grad_attn, owners)
    tail_rows = by_owner(grad_tail, owners)
    mix_grads = flatten_all(
        (
            lax.psum_scatter(ada_rows, "fsdp", scatter_dimension=0, tiled=True),
            lax.psum_scatter(ada_sums, "fsdp", scatter_dimension=0, tiled=True),
            lax.psum_scatter(qkv_rows, "fsdp", scatter_dimension=0, tiled=True),
            lax.psum_scatter(qv_rows, "fsdp", scatter_dimension=0, tiled=True),
            lax.psum_scatter(attn_rows, "fsdp", scatter_dimension=0, tiled=True),
            lax.psum_scatter(tail_rows, "fsdp", scatter_dimension=0, tiled=True),
        )
    )
    return (
        mixed,
        input_grad.astype(jnp.bfloat16),
        cond_grad,
        mix_grads[0],
        mix_grads[1],
        mix_grads[2],
        mix_grads[3],
        mix_grads[4],
        mix_grads[5],
        dense_grads[0],
        dense_grads[1],
        dense_grads[2],
        dense_grads[3],
        dense_grads[4],
        dense_grads[5],
        dense_grads[6],
        dense_grads[7],
        dense_grads[8],
    )


def per_device_kernels(
    tokens,
    cond,
    image_lengths,
    ada_weight,
    ada_bias,
    qkv_weight,
    qv_bias,
    attn_weight,
    tail_bias,
    up_weight,
    up_bias,
    down_weight,
    projector_in,
    projector_in_bias,
    projector_mid,
    projector_mid_bias,
    projector_out,
    projector_out_bias,
    targets,
    out_grad,
):
    owners = lax.axis_size("fsdp")
    me = lax.axis_index("fsdp")
    row_count = tokens.shape[0]
    rows = D // owners
    images = cond.shape[0]
    cond_values = cond.astype(jnp.float32)
    cond_low = lowered(sigmoid_linear(cond_values))
    letters = [jnp.pad(cond_low.reshape(images, owners, rows).transpose(1, 0, 2), ((0, 0), (0, 0), (0, 128 - rows)))]
    biases = (ada_bias, qv_bias, tail_bias, up_bias, projector_in_bias, projector_mid_bias, projector_out_bias)
    for bias in biases:
        height = -(-bias.shape[0] // 128)
        lines = jnp.pad(bias, (0, height * 128 - bias.shape[0])).reshape(1, height, 128)
        letters.append(jnp.broadcast_to(lines, (owners, height, 128)))
    letters = jnp.concatenate(letters, axis=1)
    letters = jnp.pad(letters, ((0, 0), (0, 16 - letters.shape[1]), (0, 0)))
    ada_mine = ada_weight.reshape(rows, 6 * D)
    used = images * 6 * D // 128
    mod_height = -(-used // 16) * 16
    widths = (6 * D, 2 * D, 2 * D, FF, P_SIZE, P_SIZE, Z)
    image_of, onehot = image_onehot(image_lengths[0], row_count)
    same_image = (image_of[:, None] == image_of[None, :]).astype(jnp.float32)
    onehot = jnp.pad(onehot, ((0, 0), (0, 128 - onehot.shape[1])))
    results = forward(
        owners,
        images,
        (
            qkv_weight.reshape(rows, 3 * D),
            attn_weight.reshape(rows, D),
            up_weight.reshape(rows, FF),
            projector_in.reshape(rows, P_SIZE),
            down_weight.reshape(-1, D),
            projector_mid.reshape(-1, P_SIZE),
            projector_out.reshape(-1, Z),
        ),
        (ada_mine, letters, tokens, onehot, same_image),
        ((0, 1, 2, 3, 5, 7, 8), (0, 1, 2, 4, 6, 8, 9)),
        1,
    )
    mixed = results[15]
    modulation, cond_mine = results[21:]
    sums = backward(
        owners,
        images,
        results[:6],
        (tokens, onehot, same_image, modulation, targets, out_grad) + tuple(results[6:21]),
        mod_height,
        (2, (0, 1, 2, 3, 4, 5, 6), (0, 1, 2, 3, 4, 5, 6), (3, 2, 6)),
        2,
    )
    qkv_sum, attn_sum, up_sum, down_sum, in_sum, mid_sum, out_sum, tokens_grad = sums[:8]
    qkv_cols, attn_cols, mlp_cols, up_cols, in_cols, mid_cols, out_cols = [part[0] for part in sums[8:15]]
    modulation_all = sums[15].reshape(owners, mod_height, 128)[:, :used].reshape(owners * images, 6 * D)
    grad_ada = transposed_left(cond_mine, modulation_all)
    cond_back = transposed_right(modulation_all, ada_mine).reshape(owners, images * rows)
    bias_parts = [
        by_owner(part, owners)
        for part in (
            jnp.concatenate([qkv_cols[:D], qkv_cols[2 * D :]]),
            jnp.concatenate([attn_cols, mlp_cols]),
            up_cols,
            in_cols,
            mid_cols,
            out_cols,
        )
    ]
    received = lax.all_to_all(jnp.concatenate([cond_back] + bias_parts, axis=1), "fsdp", 0, 0, tiled=True)
    cond_back = received[:, : images * rows].reshape(owners, images, rows).transpose(1, 0, 2).reshape(images, D)
    cond_grad = pull_back(sigmoid_linear, cond_values, cond_back).astype(jnp.bfloat16)
    small = jnp.sum(received[:, images * rows :], axis=0)
    grad_ada_bias = lax.dynamic_slice(
        column_sums(modulation_all), (me * (6 * D // owners),), (6 * D // owners,)
    )
    small_parts, at = [], 0
    for width in widths[1:]:
        small_parts.append(small[at : at + width // owners])
        at += width // owners
    qv_small, tail_small, up_small, in_small, mid_small, out_small = small_parts
    return (
        mixed,
        tokens_grad,
        cond_grad,
        grad_ada.reshape(-1),
        grad_ada_bias,
        qkv_sum.reshape(-1),
        qv_small,
        attn_sum.reshape(-1),
        tail_small,
        up_sum.reshape(-1),
        up_small,
        down_sum.reshape(-1),
        in_sum.reshape(-1),
        in_small,
        mid_sum.reshape(-1),
        mid_small,
        out_sum.reshape(-1),
        out_small,
    )


def solution(mesh):
    in_specs = (
        P("fsdp", None),
        P("fsdp", None),
        P("fsdp", None),
        P("fsdp"),
        P("fsdp"),
        P("fsdp"),
        P("fsdp"),
        P("fsdp"),
        P("fsdp"),
        P("fsdp"),
        P("fsdp"),
        P("fsdp"),
        P("fsdp"),
        P("fsdp"),
        P("fsdp"),
        P("fsdp"),
        P("fsdp"),
        P("fsdp"),
        P("fsdp", None),
        P("fsdp", None),
    )
    out_specs = (
        P("fsdp", None),
        P("fsdp", None),
        P("fsdp", None),
        P("fsdp"),
        P("fsdp"),
        P("fsdp"),
        P("fsdp"),
        P("fsdp"),
        P("fsdp"),
        P("fsdp"),
        P("fsdp"),
        P("fsdp"),
        P("fsdp"),
        P("fsdp"),
        P("fsdp"),
        P("fsdp"),
        P("fsdp"),
        P("fsdp"),
    )
    owners = mesh.shape["fsdp"]
    program = per_device_kernels if owners % 16 == 0 and D % owners == 0 else per_device
    return jax.shard_map(
        program, mesh=mesh, in_specs=in_specs, out_specs=out_specs, check_vma=False
    )
```

```python
import functools

import jax
import jax.numpy as jnp
from jax import lax
from jax.experimental import pallas as pl
from jax.experimental.pallas import tpu as pltpu
from jax.sharding import PartitionSpec as P

D = 1152
HEADS = 16
HD = 72
FF = 4608
P_SIZE = 2048
Z = 768
Z_OUT = Z


EPSILON = 1e-06
PRECISE = lax.Precision.HIGHEST


def layer_norm(values):
    centred = values - jnp.mean(values, axis=-1, keepdims=True)
    spread = jnp.mean(centred * centred, axis=-1, keepdims=True)
    return centred * lax.rsqrt(spread + EPSILON)


def sigmoid_linear(values):
    return values * jax.nn.sigmoid(values)


def gelu_tanh(values):
    inner = 0.7978845608028654 * (values + 0.044715 * values * values * values)
    return 0.5 * values * (1.0 + jnp.tanh(inner))


def image_onehot(lengths, row_count):
    ends = jnp.cumsum(lengths)
    position = jnp.arange(row_count, dtype=jnp.int32)
    image_of = jnp.sum((position[:, None] >= ends[None, :]).astype(jnp.int32), axis=1)
    images = jnp.arange(lengths.shape[0], dtype=jnp.int32)
    return (image_of, (image_of[:, None] == images[None, :]).astype(jnp.float32))


def pull_back(function, point, cotangent):
    return jax.vjp(function, point)[1](cotangent)[0]


def lowered(values):
    return values.astype(jnp.bfloat16)


def matmul(left, right):
    return jnp.dot(left, right, preferred_element_type=jnp.float32)


def transposed_left(left, right):
    return lax.dot_general(
        left, right, (((0,), (0,)), ((), ())), preferred_element_type=jnp.float32
    )


def transposed_right(left, right):
    return lax.dot_general(
        left, right, (((1,), (1,)), ((), ())), preferred_element_type=jnp.float32
    )


def column_sums(values):
    return jnp.sum(values.astype(jnp.float32), axis=0)


def by_owner(values, owners):
    return values.reshape(owners, -1)


def flatten_all(pieces):
    return tuple((piece.reshape(-1) for piece in pieces))


def unpack_mix(gathered):
    return (
        gathered[0].reshape(D, 6 * D),
        gathered[1].astype(jnp.float32),
        gathered[2].reshape(D, 3 * D),
        gathered[3].astype(jnp.float32),
        gathered[4].reshape(D, D),
        gathered[5].astype(jnp.float32),
    )


def unpack_dense(gathered):
    return (
        gathered[0].reshape(D, FF),
        gathered[1].astype(jnp.float32),
        gathered[2].reshape(FF, D),
        gathered[3].reshape(D, P_SIZE),
        gathered[4].astype(jnp.float32),
        gathered[5].reshape(P_SIZE, P_SIZE),
        gathered[6].astype(jnp.float32),
        gathered[7].reshape(P_SIZE, Z),
        gathered[8].astype(jnp.float32),
    )


MESH = pl.DeviceIdType.MESH

class Place:
    def __init__(self, n):
        self.me = me = lax.axis_index("fsdp")
        self.Z = n // 8
        self.z, self.y, self.x, self.c = me // 8, (me // 4) % 2, (me // 2) % 2, me % 2
        self.xp = me + 2 - 4 * self.x
        self.yp = me + 4 - 8 * self.y
        self.cp = me + 1 - 2 * self.c

def barrier(pc, everyone=0):
    sem = pltpu.get_barrier_semaphore()
    if everyone:
        def greet(k, carry):
            pl.semaphore_signal(sem, inc=1, device_id=(lax.rem(pc.me + k, everyone),), device_id_type=MESH)
            return carry
        lax.fori_loop(1, everyone, greet, 0)
        pl.semaphore_wait(sem, everyone - 1)
        return
    for q in (pc.xp, pc.yp, pc.cp):
        pl.semaphore_signal(sem, inc=1, device_id=(q,), device_id_type=MESH)
    @pl.when(pc.z > 0)
    def _():
        pl.semaphore_signal(sem, inc=1, device_id=(pc.me - 8,), device_id_type=MESH)
    @pl.when(pc.z < pc.Z - 1)
    def _():
        pl.semaphore_signal(sem, inc=1, device_id=(pc.me + 8,), device_id_type=MESH)
    ends = (pc.z == 0).astype(jnp.int32) + (pc.z == pc.Z - 1).astype(jnp.int32)
    pl.semaphore_wait(sem, 5 - ends)


SLABBED = (True, True, False, True, False, False)

CHUNKS = tuple(
    (a, off, w, stacks, 1 if k in (1, 5, 9) else 0)
    for k, (a, off, w, stacks) in enumerate(
        tuple((a, off, 384, 1) for a in range(3) for off in (0, 384, 768))
        + ((3, 0, 384, 1), (3, 384, 128, 1), (4, 0, 768, 2), (4, 768, 768, 2), (4, 1536, 512, 2), (5, 0, 512, 2), (5, 512, 256, 2))
    )
)

def dot(a, b):
    return jnp.dot(a, b, preferred_element_type=jnp.float32)

def dot_nt(a, b):
    return lax.dot_general(a, b, (((1,), (1,)), ((), ())), preferred_element_type=jnp.float32)

def norm_parts(values):
    centred = values - jnp.mean(values, axis=-1, keepdims=True)
    spread = jnp.mean(centred * centred, axis=-1, keepdims=True)
    return centred, lax.rsqrt(spread + EPSILON)

def token_rows(onehot, mod, k):
    images = mod.shape[0] // 6
    total = onehot[:, 0:1] * mod[k * images:k * images + 1]
    for i in range(1, images):
        total = total + onehot[:, i:i + 1] * mod[k * images + i:k * images + i + 1]
    return total

def head_window(h):
    start = jnp.minimum((h * HD) // 128 * 128, D - 256)
    start = pl.multiple_of(start, 128)
    lane = lax.broadcasted_iota(jnp.int32, (1, 256), 1) + start
    return start, (lane >= h * HD) & (lane < h * HD + HD)

def region(out, zs, y, x, c, off, w):
    return out.at[zs, y, x, c, :, pl.ds(off, w)]

def gather_program(n, ins, outs, sems, rounds):
    lsem, zs_sem, zr_sem, xs_sem, xr_sem, cs_sem, cr_sem = sems
    pc = Place(n)
    Z = pc.Z
    z, y, x, c = pc.z, pc.y, pc.x, pc.c
    allz = slice(None); lo = slice(0, Z // 2); hi = slice(Z // 2, Z)
    def plane(r): return rounds[r][4]
    def reg(r, zs, y_, x_):
        a, off, w = rounds[r][:3]
        return region(outs[a], zs, y_, x_, c, off, w)
    def own_in(r):
        a, off, w = rounds[r][:3]
        return ins[a].at[:, pl.ds(off, w)]
    def rcopy(src, dst, ss, rs, dev):
        return pltpu.make_async_remote_copy(src_ref=src, dst_ref=dst, send_sem=ss, recv_sem=rs, device_id=(dev,), device_id_type=MESH)
    def line_part(r, org):
        return reg(r, org, slice(None), slice(None)) if plane(r) else reg(r, org, y, x)
    def zcopy(r, side, s):
        org = z - s if side == 0 else z + s
        dst = line_part(r, org)
        src = own_in(r) if s == 0 and not plane(r) else dst
        return rcopy(src, dst, zs_sem.at[r, side, s], zr_sem.at[r, side, s], pc.me + (8 if side == 0 else -8))
    def zrecv(r, side, s):
        org = z - 1 - s if side == 0 else z + 1 + s
        d = line_part(r, org)
        rcopy(d, d, zs_sem.at[r, side, s], zr_sem.at[r, side, s], pc.me).wait_recv()
    def local(r):
        return pltpu.make_async_copy(own_in(r), reg(r, z, y, x), lsem.at[r])
    def xy(r, k):
        if plane(r):
            if k < 2:
                return rcopy(own_in(r), reg(r, z, y, x), xs_sem.at[r, k], xr_sem.at[r, k], pc.yp if k else pc.xp)
            d = reg(r, z, y, 1 - x) if r % 2 else reg(r, z, 1 - y, x)
            return rcopy(d, d, xs_sem.at[r, 2], xr_sem.at[r, 2], pc.yp if r % 2 else pc.xp)
        if k < 2: d = reg(r, allz, y, x)
        elif k == 2: d = reg(r, lo, y, 1 - x)
        else: d = reg(r, hi, 1 - y, x)
        return rcopy(d, d, xs_sem.at[r, k], xr_sem.at[r, k], pc.xp if k in (0, 3) else pc.yp)
    def core(r, k):
        if plane(r): d = reg(r, allz, slice(None), slice(None))
        else: d = reg(r, allz, y if k in (0, 1) else 1 - y, x if k in (0, 2) else 1 - x)
        return rcopy(d, d, cs_sem.at[r, k], cr_sem.at[r, k], pc.cp)
    def zstart(r, s):
        @pl.when((z - s >= 0) & (z < Z - 1))
        def _(): zcopy(r, 0, s).start()
        @pl.when((z + s <= Z - 1) & (z > 0))
        def _(): zcopy(r, 1, s).start()
    def zwait(r, s):
        @pl.when(z - 1 - s >= 0)
        def _(): zrecv(r, 0, s)
        @pl.when(z + 1 + s <= Z - 1)
        def _(): zrecv(r, 1, s)
    def stage(r, s):
        if plane(r):
            if s == 0:
                local(r).start()
                xy(r, 0).start(); xy(r, 1).start()
            elif s == 1:
                local(r).wait()
                xy(r, 0).wait_recv(); xy(r, 1).wait_recv()
                xy(r, 2).start()
            elif s == 2:
                xy(r, 2).wait_recv()
                zstart(r, 0)
            elif s < Z + 1:
                zwait(r, s - 3)
                zstart(r, s - 2)
            elif s == Z + 1:
                zwait(r, Z - 2)
                core(r, 0).start()
            else:
                core(r, 0).wait_recv()
            return
        if s == 0:
            local(r).start()
            zstart(r, 0)
        elif s < Z - 1:
            zwait(r, s - 1)
            zstart(r, s)
        elif s == Z - 1:
            zwait(r, s - 1)
            local(r).wait()
            xy(r, 0).start(); xy(r, 1).start(); core(r, 0).start()
        elif s == Z:
            xy(r, 0).wait_recv(); xy(r, 2).start(); core(r, 1).start()
            xy(r, 1).wait_recv(); xy(r, 3).start(); core(r, 2).start()
        elif s == Z + 1:
            xy(r, 2).wait_recv(); xy(r, 3).wait_recv(); core(r, 3).start()
        elif s == Z + 2:
            for k in range(4): core(r, k).wait_recv()
    def finish(r):
        for s in range(Z - 1):
            @pl.when((z - s >= 0) & (z < Z - 1))
            def _(): zcopy(r, 0, s).wait_send()
            @pl.when((z + s <= Z - 1) & (z > 0))
            def _(): zcopy(r, 1, s).wait_send()
        for k in range(3 if plane(r) else 4):
            xy(r, k).wait_send()
        for k in range(1 if plane(r) else 4):
            core(r, k).wait_send()
    return stage, finish, Z + 3

def weight_loads(chunk, full, slot, sem, top=0, bottom=None):
    a, off, w, stacks = chunk[:4]
    ref, cps = full[a], []
    rows, sw = ref.shape[4], w // stacks
    bottom = bottom or rows
    for j in range(4):
        for s in range(stacks):
            cps.append((ref.at[:, :, j // 2, j % 2, pl.ds(top, bottom - top), pl.ds(off + s * sw, sw)],
                        slot.at[j, :, :, pl.ds(s * rows + top, bottom - top), pl.ds(0, sw)]))
    return [pltpu.make_async_copy(s, d, sem.at[k]) for k, (s, d) in enumerate(cps)]

def chunk_weight(chunk, slot, rows, part):
    sw = chunk[2] // chunk[3]
    Z = slot.shape[1]
    return jnp.concatenate(
        [slot[j, zz, yy, part * rows:(part + 1) * rows, 0:sw] for zz in range(Z) for yy in range(2) for j in range(4)], axis=0)

def scatter_program(n, R, G, CR, OWN, XR, ZR, keep, sems, final, late=(), P=None):
    cs, cr, xs, xr, zs_, zr, credit = sems
    keep_g, keep_c, keep_o, keep_x, keep_p = keep
    pc = Place(n)
    Z = pc.Z; H = Z // 2
    z, y, x, c = pc.z, pc.y, pc.x, pc.c
    up_dev = jnp.minimum(pc.me + 8, n - 1)
    down_dev = jnp.maximum(pc.me - 8, 0)
    early = [r for r in range(R) if r not in late]
    def turn(r): return (late if r in late else early).index(r)
    def first_use(r): return turn(r) < (keep_p if r in late else keep_x)
    def last_use(r): return turn(r) + (keep_p if r in late else keep_x) >= len(late if r in late else early)
    def base(r): return 5 if r in late else 1
    def rcopy(src, dst, ss, rs, dev):
        return pltpu.make_async_remote_copy(src_ref=src, dst_ref=dst, send_sem=ss, recv_sem=rs, device_id=(dev,), device_id_type=MESH)
    def signal(k, dev):
        pl.semaphore_signal(credit.at[k], inc=1, device_id=(dev,), device_id_type=MESH)
    def spend(k):
        pl.semaphore_wait(credit.at[k], 1)
    def core(r): return rcopy(G(r).at[1 - c], CR(r), cs.at[r], cr.at[r], pc.cp)
    def xy(r, k):
        if r in late:
            own, _, px = P(r)
            dev = (pc.yp if r % 2 else pc.xp, pc.xp, pc.yp)[k]
            src = own.at[x if k == 2 else 1 - x, z, y if k == 1 else 1 - y]
            return rcopy(src, px.at[k], xs.at[r, k], xr.at[r, k], dev)
        b, xb = OWN(r), XR(r)
        if k == 0: return rcopy(b.at[1 - x, 0:H, 1 - y], xb.at[0:H], xs.at[r, 0], xr.at[r, 0], pc.yp)
        if k == 1: return rcopy(b.at[1 - x, H:Z, 1 - y], xb.at[H:Z], xs.at[r, 1], xr.at[r, 1], pc.xp)
        if k == 2: return rcopy(b.at[1 - x, :, y], xb.at[Z:2 * Z], xs.at[r, 2], xr.at[r, 2], pc.xp)
        return rcopy(b.at[x, :, 1 - y], xb.at[2 * Z:3 * Z], xs.at[r, 3], xr.at[r, 3], pc.yp)
    def line_refs(r, d):
        if r in late:
            own, pz, _ = P(r)
            return own.at[:, d], pz
        return XR(r).at[Z + d], ZR(r)
    def zc(r, side, d):
        src, dst = line_refs(r, d)
        at = d - z - 1 if side == 0 else Z - z + 1 + d
        return rcopy(src, dst.at[at], zs_.at[r, side, d], zr.at[r, side, d], up_dev if side == 0 else down_dev)
    def zgot(r, side, d):
        src, dst = line_refs(r, d)
        at = d - z if side == 0 else Z - z + d
        rcopy(src, dst.at[at], zs_.at[r, side, d], zr.at[r, side, d], up_dev if side == 0 else down_dev).wait_recv()
    def plane_sent(o):
        for k in range(4): xy(early[o], k).wait_send()
    def zwaits_send(r):
        for d in range(Z):
            @pl.when(d > z)
            def _(): zc(r, 0, d).wait_send()
            @pl.when(d < z)
            def _(): zc(r, 1, d).wait_send()
    def add_line(r, side, d, at):
        if r in late:
            own, pz, _ = P(r)
            for xx in range(2):
                for yy in range(2):
                    own[xx, d, yy] = own[xx, d, yy] + pz[at, xx, yy]
        else:
            XR(r)[Z + d] = XR(r)[Z + d] + ZR(r)[at]
    def zstep(r, s):
        for side in (0, 1):
            p = s if side == 0 else Z - 1 - s
            @pl.when(z == p)
            def _():
                if not first_use(r) and (p < Z - 1 if side == 0 else p > 0):
                    spend(base(r) + 2 + side)
                for d in range(Z):
                    if (d > p) if side == 0 else (d < p):
                        if s > 0:
                            zgot(r, side, d)
                            add_line(r, side, d, d - p if side == 0 else Z - p + d)
                        zc(r, side, d).start()
    def give_back(r):
        if not last_use(r):
            signal(base(r), pc.xp)
            signal(base(r) + 1, pc.yp)
            @pl.when(z < Z - 1)
            def _(): signal(base(r) + 3, up_dev)
            @pl.when(z > 0)
            def _(): signal(base(r) + 2, down_dev)
    def before(r):
        if r >= keep_g:
            core(r - keep_g).wait_send()
    def core_sum(r, out):
        b = G(r).at[c]
        core(r).wait_recv()
        def add(i, carry):
            xx, zz, yy = i // (2 * Z), (i // 2) % Z, i % 2
            out[xx, zz, yy] = b[xx, zz, yy] + CR(r)[xx, zz, yy]
            return carry
        lax.fori_loop(0, 4 * Z, add, 0)
        if r + keep_c < R:
            signal(0, pc.cp)
    def late_stage(r, s):
        own, pz, px = P(r)
        if s == 1:
            core_sum(r, own)
            zstep(r, 0)
        elif s < Z:
            zstep(r, s - 1)
        elif s == Z:
            for d in range(Z):
                @pl.when(d == z)
                def _():
                    if d > 0:
                        zgot(r, 0, d)
                        add_line(r, 0, d, 0)
                    if d < Z - 1:
                        zgot(r, 1, d)
                        add_line(r, 1, d, Z)
            if not first_use(r):
                spend(base(r))
                spend(base(r) + 1)
            xy(r, 0).start()
            xy(r, 2 if r % 2 else 1).start()
        elif s == Z + 1:
            xy(r, 0).wait_recv()
            if r % 2:
                own[1 - x, z, y] = own[1 - x, z, y] + px[0]
            else:
                own[x, z, 1 - y] = own[x, z, 1 - y] + px[0]
            xy(r, 1 if r % 2 else 2).start()
        else:
            xy(r, 1).wait_recv()
            xy(r, 2).wait_recv()
            final(r, own[x, z, y].astype(jnp.float32) + px[1].astype(jnp.float32) + px[2].astype(jnp.float32))
            for k in range(3): xy(r, k).wait_send()
            zwaits_send(r)
            give_back(r)
    def stage(r, s):
        b = None if r in late else OWN(r)
        if s == 0:
            if r >= keep_c:
                spend(0)
            core(r).start()
        elif r in late:
            late_stage(r, s)
        elif s == 1:
            if turn(r) >= keep_o:
                plane_sent(turn(r) - keep_o)
            core_sum(r, b)
            if not first_use(r):
                spend(base(r))
                spend(base(r) + 1)
            xy(r, 0).start(); xy(r, 1).start()
        elif s == 2:
            xy(r, 0).wait_recv()
            def add(i, carry):
                b[1 - x, i, y] = b[1 - x, i, y] + XR(r)[i]
                return carry
            lax.fori_loop(0, H, add, 0)
            xy(r, 2).start()
            xy(r, 1).wait_recv()
            def add(i, carry):
                b[x, i, 1 - y] = b[x, i, 1 - y] + XR(r)[i]
                return carry
            lax.fori_loop(H, Z, add, 0)
            xy(r, 3).start()
        elif s == 3:
            xy(r, 2).wait_recv(); xy(r, 3).wait_recv()
            def add(i, carry):
                XR(r)[Z + i] = b[x, i, y] + XR(r)[Z + i] + XR(r)[2 * Z + i]
                return carry
            lax.fori_loop(0, Z, add, 0)
            zstep(r, 0)
        elif s < Z + 2:
            zstep(r, s - 3)
        else:
            for d in range(Z):
                @pl.when(d == z)
                def _():
                    tot = XR(r)[Z + d].astype(jnp.float32)
                    if d > 0:
                        zgot(r, 0, d)
                        tot = tot + ZR(r)[0].astype(jnp.float32)
                    if d < Z - 1:
                        zgot(r, 1, d)
                        tot = tot + ZR(r)[Z].astype(jnp.float32)
                    final(r, tot)
            zwaits_send(r)
            give_back(r)
    def finish():
        for r in range(max(0, R - keep_g), R):
            core(r).wait_send()
        for o in range(max(0, len(early) - keep_o), len(early)):
            plane_sent(o)
    return before, stage, finish, Z + 3

def scatter_sems(R, Z):
    D_ = pltpu.SemaphoreType.DMA
    return [D_((R,)), D_((R,)), D_((R, 4)), D_((R, 4)), D_((R, 2, Z)), D_((R, 2, Z)), pltpu.SemaphoreType.REGULAR((9,))]

BIASES = (6 * D, 2 * D, 2 * D, FF, P_SIZE, P_SIZE, Z_OUT)

def forward_kernel(n, images, offs, *refs):
    rounds = CHUNKS
    qkv_w, attn_in, up_w, in_w, down_w, mid_w, out_w, ada_w, mail, tokens, onehot, same = refs[:12]
    refs = refs[12:]
    full, refs = refs[:6], refs[6:]
    act_outs, (mod, cond_mine) = refs[:15], refs[15:17]
    refs = refs[17:]
    acts, refs = refs[:15], refs[15:]
    (first_in, projected, heads, branch_attn, middle, second_in, up_pre, up_act, branch_mlp, mixed,
     first_pre, first_act, second_pre, second_act, features) = acts
    act_sem, refs = refs[0], refs[1:]
    def leave(*which):
        return [pltpu.make_async_copy(acts[k], act_outs[k], act_sem.at[k]) for k in which]
    slots, attn_w, first_own, up_own, in_own, box, mod_own, mod_core, mod_xy, mod_line = refs[:10]
    bias_rows, refs = refs[10:17], refs[17:]
    load_sem, mail_send, mail_recv = refs[:3]
    ada_b, qv_b, tail_b, up_b, in_b, mid_b, out_b = bias_rows
    R, Z = len(rounds), n // 8
    pc = Place(n)
    stage, finish, S = gather_program(
        n, (first_own, up_own, down_w, in_own, mid_w, out_w), full, refs[3:10], rounds)
    per = D // n
    for s in range(4):
        first_own[s * per:(s + 1) * per] = qkv_w[:, s * D:(s + 1) * D] if s < 3 else attn_in[...]
        up_own[s * per:(s + 1) * per] = up_w[:, s * (FF // 4):(s + 1) * (FF // 4)]
        in_own[s * per:(s + 1) * per] = in_w[:, s * (P_SIZE // 4):(s + 1) * (P_SIZE // 4)]

    def mod_final(r, tot):
        for k in range(6):
            for i in range(images):
                row = k * images + i
                mod[row:row + 1] = tot[row:row + 1] + ada_b[:, k * D:(k + 1) * D]
    _, mod_stage, mod_finish, _ = scatter_program(
        n, 1, lambda r: mod_own, lambda r: mod_core, lambda r: mod_own.at[pc.c], lambda r: mod_xy, lambda r: mod_line, (1, 1, 1, 1, 1), refs[10:], mod_final)

    def letter(k):
        dest = lax.rem(pc.me + k, n)
        return pltpu.make_async_remote_copy(
            src_ref=mail.at[dest], dst_ref=box.at[pc.me], send_sem=mail_send.at[k], recv_sem=mail_recv.at[k],
            device_id=(dest,), device_id_type=MESH)

    def send_mail():
        def go(k, carry):
            letter(k).start()
            return carry
        lax.fori_loop(1, n, go, 0)
        box[pc.me] = mail[pc.me]

    def read_mail():
        def wait(k, carry):
            letter(k).wait()
            return carry
        lax.fori_loop(1, n, wait, 0)
        cond_mine[...] = jnp.concatenate([box[d, 0:images, 0:per] for d in range(n)], axis=0)
        row = images
        for ref, width in zip(bias_rows, BIASES):
            part = width // n
            for at in range(0, part, 128):
                size = min(128, part - at)
                for d in range(n):
                    ref[:, d * part + at:d * part + at + size] = box[d, row:row + 1, 0:size].astype(jnp.float32)
                row += 1
        mod_own[...] = jnp.zeros_like(mod_own)
        for k in range(6):
            value = dot(cond_mine[...], ada_w[:, k * D:(k + 1) * D])
            for d in range(n):
                mod_own[d % 2, (d // 2) % 2, d // 8, (d // 4) % 2, k * images:(k + 1) * images] = value[d * images:(d + 1) * images]
    barrier(pc, n)
    last_of = {a: max(r for r in range(R) if rounds[r][0] == a) for a in range(6)}

    def loads(r):
        return weight_loads(rounds[r], full, slots.at[r % 2], load_sem.at[r % 2])

    def prepare():
        oh, md = onehot[...], mod
        values = tokens[...].astype(jnp.float32)
        centred, scale = norm_parts(values)
        first_in[...] = (centred * scale * (1.0 + token_rows(oh, md, 1)) + token_rows(oh, md, 0)).astype(jnp.bfloat16)

    def attention():
        def head(h, carry):
            start, inside = head_window(h)
            q = projected[:, pl.ds(start, 256)]
            k = projected[:, pl.ds(pl.multiple_of(start + D, 128), 256)]
            v = projected[:, pl.ds(pl.multiple_of(start + 2 * D, 128), 256)]
            q = jnp.where(inside, q, jnp.zeros_like(q))
            scores = jnp.where(same[...] > 0.0, dot_nt(q, k) * HD ** (-0.5), -1e30)
            e = jnp.exp(scores - jnp.max(scores, axis=-1, keepdims=True))
            p = (e / jnp.sum(e, axis=-1, keepdims=True)).astype(jnp.bfloat16)
            o = dot(p, v).astype(jnp.bfloat16)
            heads[:, pl.ds(start, 256)] = jnp.where(inside, o, heads[:, pl.ds(start, 256)])
            return carry
        heads[...] = jnp.zeros_like(heads)
        lax.fori_loop(0, HEADS, head, 0)
        for i in range(3):
            cols = slice(384 * i, 384 * (i + 1))
            branch_attn[:, cols] = dot(heads[...], attn_w[:, cols]) + tail_b[:, cols]
        oh, md = onehot[...], mod
        mid = tokens[...].astype(jnp.float32) + token_rows(oh, md, 2) * branch_attn[...]
        middle[...] = mid
        centred, scale = norm_parts(mid)
        second_in[...] = (centred * scale * (1.0 + token_rows(oh, md, 4)) + token_rows(oh, md, 3)).astype(jnp.bfloat16)

    def compute(r):
        a, off, w, stacks = rounds[r][:4]
        slot = slots.at[r % 2]
        sw = w // stacks
        def weight(part):
            return chunk_weight(rounds[r], slot, per if SLABBED[a] else slot_rows[a], part)
        if a == 0:
            for j in range(3):
                cols = slice(j * D + off, j * D + off + w)
                value = dot(first_in[...], weight(j))
                if j != 1:
                    at = (j // 2) * D + off
                    value = value + qv_b[:, at:at + w]
                projected[:, cols] = value.astype(jnp.bfloat16)
            attn_w[:, off:off + w] = weight(3)
            if r == last_of[0]:
                attention()
        elif a == 1:
            for j in range(4):
                cols = slice(j * (FF // 4) + off, j * (FF // 4) + off + w)
                pre = dot(second_in[...], weight(j)) + up_b[:, cols]
                up_pre[:, cols] = pre
                up_act[:, cols] = gelu_tanh(pre).astype(jnp.bfloat16)
        elif a == 2:
            branch_mlp[:, off:off + w] = dot(up_act[...], weight(0)) + tail_b[:, D + off:D + off + w]
            if r == last_of[2]:
                hidden = middle[...] + token_rows(onehot[...], mod, 5) * branch_mlp[...]
                mixed[...] = hidden.astype(jnp.bfloat16)
        elif a == 3:
            for j in range(4):
                cols = slice(j * (P_SIZE // 4) + off, j * (P_SIZE // 4) + off + w)
                pre = dot(mixed[...], weight(j)) + in_b[:, cols]
                first_pre[:, cols] = pre
                first_act[:, cols] = sigmoid_linear(pre).astype(jnp.bfloat16)
        else:
            for s in range(stacks):
                cols = slice(off + s * sw, off + (s + 1) * sw)
                if a == 4:
                    pre = dot(first_act[...], weight(s)) + mid_b[:, cols]
                    second_pre[:, cols] = pre
                    second_act[:, cols] = sigmoid_linear(pre).astype(jnp.bfloat16)
                else:
                    features[:, cols] = dot(second_act[...], weight(s)) + out_b[:, cols]
        if r == last_of[a]:
            for cp in leave(*left_by[a]): cp.start()
    slot_rows = {2: FF // n, 4: P_SIZE // n, 5: P_SIZE // n}
    left_by = {0: (0, 1, 2, 3, 4, 5), 1: (6, 7), 2: (8, 9), 3: (10, 11), 4: (12, 13), 5: (14,)}

    offs_of = lambda r: offs[rounds[r][4]]
    ready = [max(r2 + offs_of(r2)[S - 1] for r2 in range(r + 1)) for r in range(R)]
    mod_at = 2
    t, computed, loaded, began = 0, 0, 0, []
    while computed < R:
        for s in reversed(range(S)):
            for r in range(R):
                if r + offs_of(r)[s] == t:
                    stage(r, s)
        if t == 0:
            send_mail()
        if t == mod_at:
            read_mail()
        if mod_at <= t < mod_at + Z + 3:
            mod_stage(0, t - mod_at)
        if t == mod_at + Z + 2:
            prepare()
        done_now = 0
        while True:
            while loaded < R and ready[loaded] <= t and loaded < computed + 2:
                for cp in loads(loaded): cp.start()
                loaded += 1
                began.append(t)
            if computed == loaded or t < mod_at + Z + 2 or (t < ready[-1] and (done_now == 2 or began[computed] == t)):
                break
            for cp in loads(computed): cp.wait()
            compute(computed)
            computed += 1
            done_now += 1
        t += 1
    for cp in leave(*range(15)): cp.wait()
    for r in range(R):
        finish(r)
    mod_finish()

def forward(n, images, shards, small, offs, cid):
    Z, R = n // 8, len(CHUNKS)
    f32, bf = jnp.float32, jnp.bfloat16
    tok = small[2].shape[0]
    blocks = ((4 * D // n, D), (4 * D // n, FF // 4), (FF // n, D), (4 * D // n, P_SIZE // 4), (P_SIZE // n, P_SIZE), (P_SIZE // n, Z_OUT))
    shapes = [jax.ShapeDtypeStruct((Z, 2, 2, 2) + b, bf) for b in blocks]
    acts = [(D, bf), (3 * D, bf), (D, bf), (D, f32), (D, f32), (D, bf), (FF, f32), (FF, bf), (D, f32), (D, bf),
            (P_SIZE, f32), (P_SIZE, bf), (P_SIZE, f32), (P_SIZE, bf), (Z_OUT, f32)]
    shapes += [jax.ShapeDtypeStruct((tok, w), dt) for w, dt in acts]
    mod_dims = (-(-6 * images // 8) * 8, D)
    shapes.append(jax.ShapeDtypeStruct((6 * images, D), f32))
    shapes.append(jax.ShapeDtypeStruct((n * images, D // n), bf))
    D_, V = pltpu.SemaphoreType.DMA, pltpu.VMEM
    hbm, vmem = pl.BlockSpec(memory_space=pltpu.HBM), pl.BlockSpec(memory_space=pltpu.VMEM)
    return pl.pallas_call(
        functools.partial(forward_kernel, n, images, offs),
        out_shape=shapes,
        in_specs=[vmem] * 4 + [hbm] * 3 + [vmem] * len(small),
        out_specs=[hbm] * (6 + len(acts)) + [vmem] * 2,
        scratch_shapes=[V((tok, w), dt) for w, dt in acts] + [D_((len(acts),))] + [
            V((2, 4, Z, 2, 144, 384), bf), V((D, D), bf), V(blocks[0], bf), V(blocks[1], bf), V(blocks[3], bf),
            V((n, 16, 128), bf),
            V((2, 2, Z, 2) + mod_dims, f32), V((2, Z, 2) + mod_dims, f32), V((3 * Z,) + mod_dims, f32), V((Z + 1,) + mod_dims, f32),
        ] + [V((1, w), f32) for w in BIASES] + [
            D_((2, 8)), D_((n,)), D_((n,)),
            D_((R,)), D_((R, 2, Z - 1)), D_((R, 2, Z - 1)), D_((R, 4)), D_((R, 4)), D_((R, 4)), D_((R, 4)),
        ] + scatter_sems(1, Z),
        compiler_params=pltpu.CompilerParams(collective_id=cid, has_side_effects=True, vmem_limit_bytes=58 * 2**20),
    )(*shards, *small)


def back_rounds(order):
    out = []
    for a, total, width, stacks in order:
        out += [(a, off, min(width, total - off), stacks) for off in range(0, total, width)]
    return tuple(out)

BACK_CHUNKS = back_rounds(((5, 768, 512, 2), (4, P_SIZE, 512, 2), (3, P_SIZE // 4, 256, 1), (2, D, 256, 1), (1, FF // 4, 256, 1), (0, D, 256, 1)))
LATE = (3, 8, 12, 16)
CHAIN = back_rounds(((5, 768, 768, 2), (4, P_SIZE, 768, 2), (3, P_SIZE // 4, 384, 1), (2, D, 384, 1), (1, FF // 4, 384, 1), (6, D, 384, 1), (0, D, 384, 1)))

def dot_tn(a, b):
    return lax.dot_general(a, b, (((0,), (0,)), ((), ())), preferred_element_type=jnp.float32)

def norm_back(centred, scale, grad):
    normed = centred * scale
    inner = jnp.mean(grad * normed, axis=-1, keepdims=True)
    return scale * (grad - jnp.mean(grad, axis=-1, keepdims=True) - normed * inner)

def sigmoid_linear_slope(v):
    s = jax.nn.sigmoid(v)
    return s * (1.0 + v * (1.0 - s))

def gelu_slope(v):
    t = jnp.tanh(0.7978845608028654 * (v + 0.044715 * v * v * v))
    return 0.5 * (1.0 + t) + 0.5 * v * (1.0 - t * t) * 0.7978845608028654 * (1.0 + 3.0 * 0.044715 * v * v)

def backward_kernel(n, images, chain_per_tick, scatter_offs, mod_offs, *refs):
    Z = n // 8
    full, refs = refs[:6], refs[6:]
    (tokens, onehot, same, mod, targets, out_grad), act_ins, refs = refs[:6], refs[6:21], refs[21:]
    outs, refs = refs[:7], refs[7:]
    tokens_grad, qkv_sums, attn_sums, mlp_sums, up_sums, in_sums, mid_sums, out_sums, mod_all = refs[:9]
    refs = refs[9:]
    acts, act_sem, refs = refs[:15], refs[15], refs[16:]
    (first_in, projected, heads, branch_attn, middle, second_in, up_pre, up_act, branch_mlp, mixed,
     first_pre, first_act, second_pre, second_act, features) = acts
    def bring(which):
        return [pltpu.make_async_copy(act_ins[k], acts[k], act_sem.at[k]) for k in which]
    soon, later = (14, 12, 13, 11, 10), (9, 8, 6, 7, 5, 4, 3, 2, 1, 0)
    for cp in bring(soon + later): cp.start()
    (slots, load_sem, G_, CR_, OWN_, XR_, ZR_, PB_, PZ_, PX_, feature_grad, second_back, first_back, hidden_grad, mlp_grad, up_grad,
     middle_grad, attn_grad, heads_grad, projected_grad, wide, narrow, mod_grad, mod_rows, mod_lines) = refs[:25]
    refs = refs[25:]
    rounds, R = BACK_CHUNKS, len(BACK_CHUNKS)
    per = D // n
    bf = jnp.bfloat16
    pc = Place(n)

    def dims(r):
        a, off, w, stacks = rounds[r]
        return (4 * per if a < 4 else stacks * (P_SIZE // n)), w // stacks
    keep = (G_.shape[0], CR_.shape[0], OWN_.shape[0], XR_.shape[0], PB_.shape[0])
    early = [r for r in range(R) if r not in LATE]
    def cut(ref, r, at):
        rows, w = dims(r)
        lead = (slice(None),) * (len(ref.shape) - 3)
        return ref.at[(at % ref.shape[0],) + lead + (slice(0, rows), slice(0, w))]
    def final(r, tot):
        a, off, w, stacks = rounds[r]
        rows, sw = dims(r)
        qkv_out, attn_out, up_out, down_out, in_out, mid_out, out_out = outs
        if SLABBED[a]:
            for s in range(4):
                part = tot[s * per:(s + 1) * per]
                if a == 0 and s == 3:
                    attn_out[:, off:off + w] = part
                else:
                    ref, q = {0: (qkv_out, D), 1: (up_out, FF // 4), 3: (in_out, P_SIZE // 4)}[a]
                    ref[:, s * q + off:s * q + off + w] = part
        else:
            rows = rows // stacks
            ref = {2: down_out, 4: mid_out, 5: out_out}[a]
            for s in range(stacks):
                ref[:, off + s * sw:off + (s + 1) * sw] = tot[s * rows:(s + 1) * rows]
    before, stage, finish, S = scatter_program(
        n, R, lambda r: cut(G_, r, r), lambda r: cut(CR_, r, r),
        lambda r: cut(OWN_, r, early.index(r)), lambda r: cut(XR_, r, early.index(r)), lambda r: cut(ZR_, r, early.index(r)), keep, refs[:7], final, LATE,
        lambda r: tuple(cut(ref, r, LATE.index(r)) for ref in (PB_, PZ_, PX_)))
    mod_stage, mod_finish, _ = gather_program(n, [mod_rows], [mod_all], refs[7:], ((0, 0, 128, 1, 0),))
    barrier(pc)
    mod_lines[...] = jnp.zeros_like(mod_lines)

    def image_sums(k, value):
        cols = slice(k * D, (k + 1) * D)
        for i in range(images):
            mod_grad[i:i + 1, cols] = jnp.sum(value * onehot[:, i:i + 1], axis=0, keepdims=True)

    def sums(value):
        return jnp.sum(value.astype(jnp.float32), axis=0, keepdims=True)

    def start_chain():
        f, t = features[...], targets[...].astype(jnp.float32)
        f_norm = jnp.sqrt(jnp.sum(f * f, axis=1, keepdims=True) + EPSILON)
        t_norm = jnp.sqrt(jnp.sum(t * t, axis=1, keepdims=True) + EPSILON)
        inner = jnp.sum(f * t, axis=1, keepdims=True)
        grad = -0.5 * (t / (f_norm * t_norm) - f * (inner / (f_norm * f_norm * f_norm * t_norm)))
        feature_grad[...] = grad.astype(bf)
        out_sums[...] = sums(feature_grad[...])

    def attention_back():
        projected_grad[...] = jnp.zeros_like(projected_grad)
        def head(h, carry):
            start, inside = head_window(h)
            at_q, at_k, at_v = [pl.ds(pl.multiple_of(start + i * D, 128), 256) for i in range(3)]
            q, k, v = projected[:, at_q], projected[:, at_k], projected[:, at_v]
            q = jnp.where(inside, q, jnp.zeros_like(q))
            g = heads_grad[:, at_q]
            g = jnp.where(inside, g, jnp.zeros_like(g))
            scores = jnp.where(same[...] > 0.0, dot_nt(q, k) * HD ** (-0.5), -1e30)
            e = jnp.exp(scores - jnp.max(scores, axis=-1, keepdims=True))
            p = e / jnp.sum(e, axis=-1, keepdims=True)
            pg = dot_nt(g, v)
            sg = (p * (pg - jnp.sum(p * pg, axis=-1, keepdims=True))).astype(bf)
            for at, value in (
                (at_q, dot(sg, k) * HD ** (-0.5)),
                (at_k, dot_tn(sg, q) * HD ** (-0.5)),
                (at_v, dot_tn(p.astype(bf), g)),
            ):
                projected_grad[:, at] = jnp.where(inside, value.astype(bf), projected_grad[:, at])
            return carry
        lax.fori_loop(0, HEADS, head, 0)
        qkv_sums[...] = sums(projected_grad[...])

    C = len(CHAIN)
    last = {a: max(k for k in range(C) if CHAIN[k][0] == a) for a in range(7)}
    first = {a: min(k for k in range(C) if CHAIN[k][0] == a) for a in range(7)}

    def chain_loads(k):
        a, off, w, stacks = CHAIN[k]
        slot, sem = slots.at[k % 2], load_sem.at[k % 2]
        if a == 6:
            return weight_loads((0, off, w, stacks), full, slot, sem, 3 * per // 16 * 16)
        return weight_loads((a, off, w, stacks), full, slot, sem, 0, -(-3 * per // 16) * 16 if a == 0 else None)

    def accumulate(acc, cols, new, k, a):
        acc[:, cols] = new if k == first[a] else acc[:, cols] + new

    def chain(k):
        a, off, w, stacks = CHAIN[k]
        if k == first[3]:
            for cp in bring(later): cp.wait()
        slot = slots.at[k % 2]
        sw = w // stacks
        if a in (4, 5):
            grad = second_back if a == 4 else feature_grad
            new = None
            for s in range(stacks):
                part = dot_nt(grad[:, off + s * sw:off + (s + 1) * sw], chunk_weight(CHAIN[k], slot, P_SIZE // n, s))
                new = part if new is None else new + part
            accumulate(wide, slice(0, P_SIZE), new, k, a)
            if k == last[a]:
                target, pre = (second_back, second_pre) if a == 5 else (first_back, first_pre)
                target[...] = (wide[:, 0:P_SIZE] * sigmoid_linear_slope(pre[...])).astype(bf)
                (mid_sums if a == 5 else in_sums)[...] = sums(target[...])
        elif a == 2:
            whole = chunk_weight(CHAIN[k], slot, FF // n, 0)
            for q in range(4):
                weight = whole[q * D:(q + 1) * D]
                accumulate(wide, slice(q * D, (q + 1) * D), dot_nt(mlp_grad[:, off:off + w], weight), k, a)
            if k == last[a]:
                for q in range(4):
                    cols = slice(q * D, (q + 1) * D)
                    up_grad[:, cols] = (wide[:, cols] * gelu_slope(up_pre[:, cols])).astype(bf)
                up_sums[...] = sums(up_grad[...])
        else:
            src, parts, width = {3: (first_back, range(4), P_SIZE // 4), 1: (up_grad, range(4), FF // 4),
                                 0: (projected_grad, range(3), D), 6: (attn_grad, range(3, 4), D)}[a]
            new = None
            for j in parts:
                col = off if a == 6 else j * width + off
                weight = chunk_weight(CHAIN[k], slot, per, j)
                part = dot_nt(src[:, col:col + w], weight)
                new = part if new is None else new + part
            accumulate(narrow, slice(0, D), new, k, a)
            if k == last[a]:
                oh = onehot[...]
                if a == 3:
                    hg = out_grad[...].astype(jnp.float32) + narrow[...]
                    hidden_grad[...] = hg
                    mlp_grad[...] = (hg * token_rows(oh, mod, 5)).astype(bf)
                    mlp_sums[...] = sums(mlp_grad[...])
                    image_sums(5, hg * branch_mlp[...])
                elif a == 1:
                    g = narrow[...]
                    centred, scale = norm_parts(middle[...])
                    image_sums(3, g)
                    image_sums(4, g * (centred * scale))
                    mg = hidden_grad[...] + norm_back(centred, scale, g * (1.0 + token_rows(oh, mod, 4)))
                    middle_grad[...] = mg
                    attn_grad[...] = (mg * token_rows(oh, mod, 2)).astype(bf)
                    attn_sums[...] = sums(attn_grad[...])
                    image_sums(2, mg * branch_attn[...])
                elif a == 6:
                    heads_grad[...] = narrow[...].astype(bf)
                    attention_back()
                else:
                    g = narrow[...]
                    centred, scale = norm_parts(tokens[...].astype(jnp.float32))
                    image_sums(0, g)
                    image_sums(1, g * (centred * scale))
                    tg = middle_grad[...] + norm_back(centred, scale, g * (1.0 + token_rows(oh, mod, 1)))
                    tokens_grad[...] = tg.astype(bf)
                    stacked = mod_grad[...]
                    rows = 6 * D // 128
                    for i in range(images):
                        for k in range(rows):
                            mod_lines[i * rows + k:i * rows + k + 1] = stacked[i:i + 1, 128 * k:128 * (k + 1)]
                    mod_rows[...] = mod_lines[...].astype(bf)

    def produce(r):
        a, off, w, stacks = rounds[r]
        before(r)
        left, right = {5: (second_act, feature_grad), 4: (first_act, second_back), 3: (mixed, first_back), 2: (up_act, mlp_grad),
                       1: (second_in, up_grad), 0: (first_in, projected_grad)}[a]
        rows, sw = dims(r)
        g = cut(G_, r, r)
        def put(d, at, value):
            g[d % 2, (d // 2) % 2, d // 8, (d // 4) % 2, at:at + value.shape[0]] = value
        if SLABBED[a]:
            for s in range(4):
                if a == 0 and s == 3:
                    value = dot_tn(heads[...], attn_grad[:, off:off + w])
                else:
                    at = {3: P_SIZE // 4, 1: FF // 4, 0: D}[a] * s + off
                    value = dot_tn(left[...], right[:, at:at + w])
                value = value.astype(bf)
                for d in range(n):
                    put(d, s * per, value[d * per:(d + 1) * per])
        else:
            rows = rows // stacks
            piece = 1152 if a == 2 else 1024
            for s in range(stacks):
                for part in range(left.shape[1] // piece):
                    at = off + s * sw
                    value = dot_tn(left[:, part * piece:(part + 1) * piece], right[:, at:at + sw]).astype(bf)
                    for i in range(piece // rows):
                        put(part * (piece // rows) + i, s * rows, value[i * rows:(i + 1) * rows])

    need = {5: 0, 4: first[4], 3: first[3], 2: first[2], 1: first[1], 0: first[0]}
    done = 0
    mod_start = None
    for cp in chain_loads(0): cp.start()
    for cp in bring(soon): cp.wait()
    start_chain()
    t = 0
    while True:
        for s in reversed(range(1, S)):
            for r in range(R):
                if r + scatter_offs[r in LATE][s] == t:
                    stage(r, s)
        busy = any(r + scatter_offs[r in LATE][S - 1] >= t for r in range(R))
        if t < R:
            busy = True
            while done < need[rounds[t][0]]:
                done = advance(done, chain_loads, chain, C)
            produce(t)
            stage(t, 0)
        for _ in range(chain_per_tick):
            if done < C:
                done = advance(done, chain_loads, chain, C)
        if done == C and mod_start is None:
            mod_start = t
        if mod_start is not None:
            for s in reversed(range(Z + 3)):
                if t - mod_start == mod_offs[s]:
                    mod_stage(0, s)
            busy = busy or t - mod_start < mod_offs[-1]
        if not busy:
            break
        t += 1
    finish()
    mod_finish(0)

def advance(k, chain_loads, chain, total):
    if k + 1 < total:
        for cp in chain_loads(k + 1): cp.start()
    for cp in chain_loads(k): cp.wait()
    chain(k)
    return k + 1

def backward(n, images, weights, acts, mod_height, plan, cid):
    Z, R = n // 8, len(BACK_CHUNKS)
    f32, bf = jnp.float32, jnp.bfloat16
    tok = acts[0].shape[0]
    chain_per_tick, scatter_offs, mod_offs, keep = plan
    most = (144, max(c[2] // c[3] for c in BACK_CHUNKS))
    late = most if LATE else (16, 128)
    shapes = [jax.ShapeDtypeStruct((k // n, w), f32) for k, w in (
        (D, 3 * D), (D, D), (D, FF), (FF, D), (D, P_SIZE), (P_SIZE, P_SIZE), (P_SIZE, Z_OUT))]
    shapes.append(jax.ShapeDtypeStruct((tok, D), bf))
    shapes += [jax.ShapeDtypeStruct((1, w), f32) for w in (3 * D, D, D, FF, P_SIZE, P_SIZE, Z_OUT)]
    hbm, vmem = pl.BlockSpec(memory_space=pltpu.HBM), pl.BlockSpec(memory_space=pltpu.VMEM)
    shapes.append(jax.ShapeDtypeStruct((Z, 2, 2, 2, mod_height, 128), bf))
    D_ = pltpu.SemaphoreType.DMA
    V = pltpu.VMEM
    return pl.pallas_call(
        functools.partial(backward_kernel, n, images, chain_per_tick, scatter_offs, mod_offs),
        out_shape=shapes,
        in_specs=[hbm] * 6 + [vmem] * 6 + [hbm] * (len(acts) - 6),
        out_specs=[vmem] * 15 + [hbm],
        scratch_shapes=[V(a.shape, a.dtype) for a in acts[6:]] + [D_((len(acts) - 6,))] + [
            V((2, 4, Z, 2, 144, 384), bf),
            D_((2, 8)),
            V((keep[0], 2, 2, Z, 2) + most, bf),
            V((keep[1], 2, Z, 2) + most, bf),
            V((keep[2], 2, Z, 2) + most, bf),
            V((keep[3], 3 * Z) + most, bf),
            V((keep[3], Z + 1) + most, bf),
            V((keep[4], 2, Z, 2) + late, bf), V((keep[4], Z + 1, 2, 2) + late, bf), V((keep[4], 3) + late, bf),
            V((tok, Z_OUT), bf), V((tok, P_SIZE), bf), V((tok, P_SIZE), bf), V((tok, D), f32), V((tok, D), bf), V((tok, FF), bf),
            V((tok, D), f32), V((tok, D), bf), V((tok, D), bf), V((tok, 3 * D), bf), V((tok, FF), f32), V((tok, D), f32),
            V((images, 6 * D), f32), V((mod_height, 128), bf), V((mod_height, 128), f32),
        ] + scatter_sems(R, Z)
        + [D_((1,)), D_((1, 2, Z - 1)), D_((1, 2, Z - 1)), D_((1, 4)), D_((1, 4)), D_((1, 4)), D_((1, 4))],
        compiler_params=pltpu.CompilerParams(collective_id=cid, has_side_effects=True, vmem_limit_bytes=63 * 2**20),
    )(*weights, *acts)


def per_device(
    tokens,
    cond,
    image_lengths,
    ada_weight,
    ada_bias,
    qkv_weight,
    qv_bias,
    attn_weight,
    tail_bias,
    up_weight,
    up_bias,
    down_weight,
    projector_in,
    projector_in_bias,
    projector_mid,
    projector_mid_bias,
    projector_out,
    projector_out_bias,
    targets,
    out_grad,
):
    owners = lax.axis_size("fsdp")
    mix_gathered = (
        lax.all_gather(ada_weight, "fsdp", axis=0, tiled=True),
        lax.all_gather(ada_bias, "fsdp", axis=0, tiled=True),
        lax.all_gather(qkv_weight, "fsdp", axis=0, tiled=True),
        lax.all_gather(qv_bias, "fsdp", axis=0, tiled=True),
        lax.all_gather(attn_weight, "fsdp", axis=0, tiled=True),
        lax.all_gather(tail_bias, "fsdp", axis=0, tiled=True),
    )
    mix_full = unpack_mix(mix_gathered)
    ada_full, ada_bias_full, qkv_full, qv_full, attn_full, tail_full = mix_full
    row_count = tokens.shape[0]
    cond_values = cond.astype(jnp.float32)
    cond_low = lowered(sigmoid_linear(cond_values))
    modulation = matmul(cond_low, ada_full) + ada_bias_full
    image_of, onehot = image_onehot(image_lengths[0], row_count)
    per_token = jnp.dot(onehot, modulation, precision=PRECISE)
    shift_one, scale_one, gate_one, shift_two, scale_two, gate_two = jnp.split(per_token, 6, axis=1)
    inputs = tokens.astype(jnp.float32)
    normed_one = layer_norm(inputs)
    first_in = lowered(normed_one * (1.0 + scale_one) + shift_one)
    key_zero = jnp.zeros((D,), jnp.float32)
    bias_full = jnp.concatenate([qv_full[:D], key_zero, qv_full[D:]])
    projected = lowered(matmul(first_in, qkv_full) + bias_full)
    queries = projected[:, :D].reshape(row_count, HEADS, HD)
    keys_all = projected[:, D : 2 * D].reshape(row_count, HEADS, HD)
    values_all = projected[:, 2 * D :].reshape(row_count, HEADS, HD)
    same_image = (image_of[:, None] == image_of[None, :])[None]
    score_scale = HD ** (-0.5)

    def masked_scores():
        raw_scores = (
            jnp.einsum("qhd,khd->hqk", queries, keys_all, preferred_element_type=jnp.float32)
            * score_scale
        )
        return jnp.where(same_image, raw_scores, -1e30)

    masked = masked_scores()
    row_max = jnp.max(masked, axis=-1, keepdims=True)
    exp_scores = jnp.exp(masked - row_max)
    row_total = jnp.sum(exp_scores, axis=-1, keepdims=True)
    attn_probs = exp_scores / row_total
    head_out = jnp.einsum(
        "hqk,khd->qhd", lowered(attn_probs), values_all, preferred_element_type=jnp.float32
    )
    heads_low = lowered(head_out.reshape(row_count, D))
    branch_attn = matmul(heads_low, attn_full) + tail_full[:D]
    middle = inputs + gate_one * branch_attn
    normed_two = layer_norm(middle)
    second_in = lowered(normed_two * (1.0 + scale_two) + shift_two)
    dense_gathered = (
        lax.all_gather(up_weight, "fsdp", axis=0, tiled=True),
        lax.all_gather(up_bias, "fsdp", axis=0, tiled=True),
        lax.all_gather(down_weight, "fsdp", axis=0, tiled=True),
        lax.all_gather(projector_in, "fsdp", axis=0, tiled=True),
        lax.all_gather(projector_in_bias, "fsdp", axis=0, tiled=True),
        lax.all_gather(projector_mid, "fsdp", axis=0, tiled=True),
        lax.all_gather(projector_mid_bias, "fsdp", axis=0, tiled=True),
        lax.all_gather(projector_out, "fsdp", axis=0, tiled=True),
        lax.all_gather(projector_out_bias, "fsdp", axis=0, tiled=True),
    )
    dense_full = unpack_dense(dense_gathered)
    (
        up_full,
        up_bias_full,
        down_full,
        proj_in_full,
        proj_in_bias_full,
        proj_mid_full,
        proj_mid_bias_full,
        proj_out_full,
        proj_out_bias_full,
    ) = dense_full
    up_pre = matmul(second_in, up_full) + up_bias_full
    up_act = lowered(gelu_tanh(up_pre))
    branch_mlp = matmul(up_act, down_full) + tail_full[D:]
    hidden = middle + gate_two * branch_mlp
    mixed = lowered(hidden)
    first_pre = matmul(mixed, proj_in_full) + proj_in_bias_full
    first_act = lowered(sigmoid_linear(first_pre))
    second_pre = matmul(first_act, proj_mid_full) + proj_mid_bias_full
    second_act = lowered(sigmoid_linear(second_pre))
    features = matmul(second_act, proj_out_full) + proj_out_bias_full
    target_values = targets.astype(jnp.float32)

    def cosine_loss(values):
        value_norm = jnp.sqrt(jnp.sum(values * values, axis=1) + EPSILON)
        target_norm = jnp.sqrt(jnp.sum(target_values * target_values, axis=1) + EPSILON)
        return -0.5 * jnp.sum(jnp.sum(values * target_values, axis=1) / (value_norm * target_norm))

    feature_grad = lowered(jax.grad(cosine_loss)(features))
    dense_again = (
        lax.all_gather(up_weight, "fsdp", axis=0, tiled=True),
        lax.all_gather(up_bias, "fsdp", axis=0, tiled=True),
        lax.all_gather(down_weight, "fsdp", axis=0, tiled=True),
        lax.all_gather(projector_in, "fsdp", axis=0, tiled=True),
        lax.all_gather(projector_in_bias, "fsdp", axis=0, tiled=True),
        lax.all_gather(projector_mid, "fsdp", axis=0, tiled=True),
        lax.all_gather(projector_mid_bias, "fsdp", axis=0, tiled=True),
        lax.all_gather(projector_out, "fsdp", axis=0, tiled=True),
        lax.all_gather(projector_out_bias, "fsdp", axis=0, tiled=True),
    )
    dense_back = unpack_dense(dense_again)
    up_back = dense_back[0]
    down_back = dense_back[2]
    proj_in_back = dense_back[3]
    proj_mid_back = dense_back[5]
    proj_out_back = dense_back[7]
    grad_proj_out = transposed_left(second_act, feature_grad)
    second_back = lowered(
        pull_back(sigmoid_linear, second_pre, transposed_right(feature_grad, proj_out_back))
    )
    grad_proj_mid = transposed_left(first_act, second_back)
    first_back = lowered(
        pull_back(sigmoid_linear, first_pre, transposed_right(second_back, proj_mid_back))
    )
    grad_proj_in = transposed_left(mixed, first_back)
    hidden_grad = out_grad.astype(jnp.float32) + transposed_right(first_back, proj_in_back)
    gate_two_grad = hidden_grad * branch_mlp
    branch_mlp_grad = lowered(hidden_grad * gate_two)
    grad_down = transposed_left(up_act, branch_mlp_grad)
    up_grad = lowered(pull_back(gelu_tanh, up_pre, transposed_right(branch_mlp_grad, down_back)))
    grad_up = transposed_left(second_in, up_grad)
    second_in_grad = transposed_right(up_grad, up_back)
    middle_grad = hidden_grad + pull_back(layer_norm, middle, second_in_grad * (1.0 + scale_two))
    up_rows = by_owner(grad_up, owners)
    up_bias_rows = by_owner(column_sums(up_grad), owners)
    down_rows = by_owner(grad_down, owners)
    proj_in_rows = by_owner(grad_proj_in, owners)
    proj_in_sums = by_owner(column_sums(first_back), owners)
    proj_mid_rows = by_owner(grad_proj_mid, owners)
    proj_mid_sums = by_owner(column_sums(second_back), owners)
    proj_out_rows = by_owner(grad_proj_out, owners)
    proj_out_sums = by_owner(column_sums(feature_grad), owners)
    dense_grads = flatten_all(
        (
            lax.psum_scatter(up_rows, "fsdp", scatter_dimension=0, tiled=True),
            lax.psum_scatter(up_bias_rows, "fsdp", scatter_dimension=0, tiled=True),
            lax.psum_scatter(down_rows, "fsdp", scatter_dimension=0, tiled=True),
            lax.psum_scatter(proj_in_rows, "fsdp", scatter_dimension=0, tiled=True),
            lax.psum_scatter(proj_in_sums, "fsdp", scatter_dimension=0, tiled=True),
            lax.psum_scatter(proj_mid_rows, "fsdp", scatter_dimension=0, tiled=True),
            lax.psum_scatter(proj_mid_sums, "fsdp", scatter_dimension=0, tiled=True),
            lax.psum_scatter(proj_out_rows, "fsdp", scatter_dimension=0, tiled=True),
            lax.psum_scatter(proj_out_sums, "fsdp", scatter_dimension=0, tiled=True),
        )
    )
    mix_again = (
        lax.all_gather(ada_weight, "fsdp", axis=0, tiled=True),
        lax.all_gather(ada_bias, "fsdp", axis=0, tiled=True),
        lax.all_gather(qkv_weight, "fsdp", axis=0, tiled=True),
        lax.all_gather(qv_bias, "fsdp", axis=0, tiled=True),
        lax.all_gather(attn_weight, "fsdp", axis=0, tiled=True),
        lax.all_gather(tail_bias, "fsdp", axis=0, tiled=True),
    )
    mix_back = unpack_mix(mix_again)
    ada_back = mix_back[0]
    qkv_back = mix_back[2]
    attn_back = mix_back[4]
    gate_one_grad = middle_grad * branch_attn
    branch_attn_grad = lowered(middle_grad * gate_one)
    grad_attn = transposed_left(heads_low, branch_attn_grad)
    heads_grad = lowered(transposed_right(branch_attn_grad, attn_back)).reshape(
        row_count, HEADS, HD
    )
    again_probs = jnp.exp(masked_scores() - row_max) / row_total
    prob_grad = jnp.einsum(
        "qhd,khd->hqk", heads_grad, values_all, preferred_element_type=jnp.float32
    )
    value_grad = jnp.einsum(
        "hqk,qhd->khd", lowered(again_probs), heads_grad, preferred_element_type=jnp.float32
    )
    score_grad = lowered(
        again_probs * (prob_grad - jnp.sum(again_probs * prob_grad, axis=-1, keepdims=True))
    )
    query_grad = (
        jnp.einsum("hqk,khd->qhd", score_grad, keys_all, preferred_element_type=jnp.float32)
        * score_scale
    )
    key_grad = (
        jnp.einsum("hqk,qhd->khd", score_grad, queries, preferred_element_type=jnp.float32)
        * score_scale
    )
    projected_grad = lowered(
        jnp.concatenate(
            [
                query_grad.reshape(row_count, D),
                key_grad.reshape(row_count, D),
                value_grad.reshape(row_count, D),
            ],
            axis=1,
        )
    )
    grad_qkv = transposed_left(first_in, projected_grad)
    projected_sums = column_sums(projected_grad)
    grad_qv_bias = jnp.concatenate([projected_sums[:D], projected_sums[2 * D :]])
    first_in_grad = transposed_right(projected_grad, qkv_back)
    input_grad = middle_grad + pull_back(layer_norm, inputs, first_in_grad * (1.0 + scale_one))
    token_mod_grad = jnp.concatenate(
        [
            first_in_grad,
            first_in_grad * normed_one,
            gate_one_grad,
            second_in_grad,
            second_in_grad * normed_two,
            gate_two_grad,
        ],
        axis=1,
    )
    modulation_grad = lowered(
        lax.dot_general(onehot, token_mod_grad, (((0,), (0,)), ((), ())), precision=PRECISE)
    )
    grad_ada = transposed_left(cond_low, modulation_grad)
    cond_grad = pull_back(
        sigmoid_linear, cond_values, transposed_right(modulation_grad, ada_back)
    ).astype(jnp.bfloat16)
    grad_tail = jnp.concatenate([column_sums(branch_attn_grad), column_sums(branch_mlp_grad)])
    ada_rows = by_owner(grad_ada, owners)
    ada_sums = by_owner(column_sums(modulation_grad), owners)
    qkv_rows = by_owner(grad_qkv, owners)
    qv_rows = by_owner(grad_qv_bias, owners)
    attn_rows = by_owner(grad_attn, owners)
    tail_rows = by_owner(grad_tail, owners)
    mix_grads = flatten_all(
        (
            lax.psum_scatter(ada_rows, "fsdp", scatter_dimension=0, tiled=True),
            lax.psum_scatter(ada_sums, "fsdp", scatter_dimension=0, tiled=True),
            lax.psum_scatter(qkv_rows, "fsdp", scatter_dimension=0, tiled=True),
            lax.psum_scatter(qv_rows, "fsdp", scatter_dimension=0, tiled=True),
            lax.psum_scatter(attn_rows, "fsdp", scatter_dimension=0, tiled=True),
            lax.psum_scatter(tail_rows, "fsdp", scatter_dimension=0, tiled=True),
        )
    )
    return (
        mixed,
        input_grad.astype(jnp.bfloat16),
        cond_grad,
        mix_grads[0],
        mix_grads[1],
        mix_grads[2],
        mix_grads[3],
        mix_grads[4],
        mix_grads[5],
        dense_grads[0],
        dense_grads[1],
        dense_grads[2],
        dense_grads[3],
        dense_grads[4],
        dense_grads[5],
        dense_grads[6],
        dense_grads[7],
        dense_grads[8],
    )


def per_device_kernels(
    tokens,
    cond,
    image_lengths,
    ada_weight,
    ada_bias,
    qkv_weight,
    qv_bias,
    attn_weight,
    tail_bias,
    up_weight,
    up_bias,
    down_weight,
    projector_in,
    projector_in_bias,
    projector_mid,
    projector_mid_bias,
    projector_out,
    projector_out_bias,
    targets,
    out_grad,
):
    owners = lax.axis_size("fsdp")
    me = lax.axis_index("fsdp")
    row_count = tokens.shape[0]
    rows = D // owners
    images = cond.shape[0]
    cond_values = cond.astype(jnp.float32)
    cond_low = lowered(sigmoid_linear(cond_values))
    letters = [jnp.pad(cond_low.reshape(images, owners, rows).transpose(1, 0, 2), ((0, 0), (0, 0), (0, 128 - rows)))]
    biases = (ada_bias, qv_bias, tail_bias, up_bias, projector_in_bias, projector_mid_bias, projector_out_bias)
    for bias in biases:
        height = -(-bias.shape[0] // 128)
        lines = jnp.pad(bias, (0, height * 128 - bias.shape[0])).reshape(1, height, 128)
        letters.append(jnp.broadcast_to(lines, (owners, height, 128)))
    letters = jnp.concatenate(letters, axis=1)
    letters = jnp.pad(letters, ((0, 0), (0, 16 - letters.shape[1]), (0, 0)))
    ada_mine = ada_weight.reshape(rows, 6 * D)
    used = images * 6 * D // 128
    mod_height = -(-used // 16) * 16
    widths = (6 * D, 2 * D, 2 * D, FF, P_SIZE, P_SIZE, Z)
    image_of, onehot = image_onehot(image_lengths[0], row_count)
    same_image = (image_of[:, None] == image_of[None, :]).astype(jnp.float32)
    onehot = jnp.pad(onehot, ((0, 0), (0, 128 - onehot.shape[1])))
    results = forward(
        owners,
        images,
        (
            qkv_weight.reshape(rows, 3 * D),
            attn_weight.reshape(rows, D),
            up_weight.reshape(rows, FF),
            projector_in.reshape(rows, P_SIZE),
            down_weight.reshape(-1, D),
            projector_mid.reshape(-1, P_SIZE),
            projector_out.reshape(-1, Z),
        ),
        (ada_mine, letters, tokens, onehot, same_image),
        ((0, 1, 2, 3, 5, 7, 8), (0, 1, 2, 4, 6, 8, 9)),
        1,
    )
    mixed = results[15]
    modulation, cond_mine = results[21:]
    sums = backward(
        owners,
        images,
        results[:6],
        (tokens, onehot, same_image, modulation, targets, out_grad) + tuple(results[6:21]),
        mod_height,
        (1, ((0, 1, 3, 5, 6, 7, 8), (0, 1, 4, 6, 8, 9, 10)), (0, 1, 2, 3, 4, 5, 6), (2, 2, 5, 8, 3)),
        2,
    )
    qkv_sum, attn_sum, up_sum, down_sum, in_sum, mid_sum, out_sum, tokens_grad = sums[:8]
    qkv_cols, attn_cols, mlp_cols, up_cols, in_cols, mid_cols, out_cols = [part[0] for part in sums[8:15]]
    modulation_all = sums[15].reshape(owners, mod_height, 128)[:, :used].reshape(owners * images, 6 * D)
    grad_ada = transposed_left(cond_mine, modulation_all)
    cond_back = transposed_right(modulation_all, ada_mine).reshape(owners, images * rows)
    bias_parts = [
        by_owner(part, owners)
        for part in (
            jnp.concatenate([qkv_cols[:D], qkv_cols[2 * D :]]),
            jnp.concatenate([attn_cols, mlp_cols]),
            up_cols,
            in_cols,
            mid_cols,
            out_cols,
        )
    ]
    received = lax.all_to_all(jnp.concatenate([cond_back] + bias_parts, axis=1), "fsdp", 0, 0, tiled=True)
    cond_back = received[:, : images * rows].reshape(owners, images, rows).transpose(1, 0, 2).reshape(images, D)
    cond_grad = pull_back(sigmoid_linear, cond_values, cond_back).astype(jnp.bfloat16)
    small = jnp.sum(received[:, images * rows :], axis=0)
    grad_ada_bias = lax.dynamic_slice(
        column_sums(modulation_all), (me * (6 * D // owners),), (6 * D // owners,)
    )
    small_parts, at = [], 0
    for width in widths[1:]:
        small_parts.append(small[at : at + width // owners])
        at += width // owners
    qv_small, tail_small, up_small, in_small, mid_small, out_small = small_parts
    return (
        mixed,
        tokens_grad,
        cond_grad,
        grad_ada.reshape(-1),
        grad_ada_bias,
        qkv_sum.reshape(-1),
        qv_small,
        attn_sum.reshape(-1),
        tail_small,
        up_sum.reshape(-1),
        up_small,
        down_sum.reshape(-1),
        in_sum.reshape(-1),
        in_small,
        mid_sum.reshape(-1),
        mid_small,
        out_sum.reshape(-1),
        out_small,
    )


def solution(mesh):
    in_specs = (
        P("fsdp", None),
        P("fsdp", None),
        P("fsdp", None),
        P("fsdp"),
        P("fsdp"),
        P("fsdp"),
        P("fsdp"),
        P("fsdp"),
        P("fsdp"),
        P("fsdp"),
        P("fsdp"),
        P("fsdp"),
        P("fsdp"),
        P("fsdp"),
        P("fsdp"),
        P("fsdp"),
        P("fsdp"),
        P("fsdp"),
        P("fsdp", None),
        P("fsdp", None),
    )
    out_specs = (
        P("fsdp", None),
        P("fsdp", None),
        P("fsdp", None),
        P("fsdp"),
        P("fsdp"),
        P("fsdp"),
        P("fsdp"),
        P("fsdp"),
        P("fsdp"),
        P("fsdp"),
        P("fsdp"),
        P("fsdp"),
        P("fsdp"),
        P("fsdp"),
        P("fsdp"),
        P("fsdp"),
        P("fsdp"),
        P("fsdp"),
    )
    owners = mesh.shape["fsdp"]
    program = per_device_kernels if owners % 16 == 0 and D % owners == 0 else per_device
    return jax.shard_map(
        program, mesh=mesh, in_specs=in_specs, out_specs=out_specs, check_vma=False
    )
```

```python
import functools

import jax
import jax.numpy as jnp
from jax import lax
from jax.experimental import pallas as pl
from jax.experimental.pallas import tpu as pltpu
from jax.sharding import PartitionSpec as P

D = 1152
HEADS = 16
HD = 72
FF = 4608
P_SIZE = 2048
Z = 768
Z_OUT = Z


EPSILON = 1e-06
PRECISE = lax.Precision.HIGHEST


def layer_norm(values):
    centred = values - jnp.mean(values, axis=-1, keepdims=True)
    spread = jnp.mean(centred * centred, axis=-1, keepdims=True)
    return centred * lax.rsqrt(spread + EPSILON)


def sigmoid_linear(values):
    return values * jax.nn.sigmoid(values)


def gelu_tanh(values):
    inner = 0.7978845608028654 * (values + 0.044715 * values * values * values)
    return 0.5 * values * (1.0 + jnp.tanh(inner))


def image_onehot(lengths, row_count):
    ends = jnp.cumsum(lengths)
    position = jnp.arange(row_count, dtype=jnp.int32)
    image_of = jnp.sum((position[:, None] >= ends[None, :]).astype(jnp.int32), axis=1)
    images = jnp.arange(lengths.shape[0], dtype=jnp.int32)
    return (image_of, (image_of[:, None] == images[None, :]).astype(jnp.float32))


def pull_back(function, point, cotangent):
    return jax.vjp(function, point)[1](cotangent)[0]


def lowered(values):
    return values.astype(jnp.bfloat16)


def matmul(left, right):
    return jnp.dot(left, right, preferred_element_type=jnp.float32)


def transposed_left(left, right):
    return lax.dot_general(
        left, right, (((0,), (0,)), ((), ())), preferred_element_type=jnp.float32
    )


def transposed_right(left, right):
    return lax.dot_general(
        left, right, (((1,), (1,)), ((), ())), preferred_element_type=jnp.float32
    )


def column_sums(values):
    return jnp.sum(values.astype(jnp.float32), axis=0)


def by_owner(values, owners):
    return values.reshape(owners, -1)


def flatten_all(pieces):
    return tuple((piece.reshape(-1) for piece in pieces))


def unpack_mix(gathered):
    return (
        gathered[0].reshape(D, 6 * D),
        gathered[1].astype(jnp.float32),
        gathered[2].reshape(D, 3 * D),
        gathered[3].astype(jnp.float32),
        gathered[4].reshape(D, D),
        gathered[5].astype(jnp.float32),
    )


def unpack_dense(gathered):
    return (
        gathered[0].reshape(D, FF),
        gathered[1].astype(jnp.float32),
        gathered[2].reshape(FF, D),
        gathered[3].reshape(D, P_SIZE),
        gathered[4].astype(jnp.float32),
        gathered[5].reshape(P_SIZE, P_SIZE),
        gathered[6].astype(jnp.float32),
        gathered[7].reshape(P_SIZE, Z),
        gathered[8].astype(jnp.float32),
    )


MESH = pl.DeviceIdType.MESH

class Place:
    def __init__(self, n):
        self.me = me = lax.axis_index("fsdp")
        self.Z = n // 8
        self.z, self.y, self.x, self.c = me // 8, (me // 4) % 2, (me // 2) % 2, me % 2
        self.xp = me + 2 - 4 * self.x
        self.yp = me + 4 - 8 * self.y
        self.cp = me + 1 - 2 * self.c

def barrier(pc, everyone=0):
    sem = pltpu.get_barrier_semaphore()
    if everyone:
        def greet(k, carry):
            pl.semaphore_signal(sem, inc=1, device_id=(lax.rem(pc.me + k, everyone),), device_id_type=MESH)
            return carry
        lax.fori_loop(1, everyone, greet, 0)
        pl.semaphore_wait(sem, everyone - 1)
        return
    for q in (pc.xp, pc.yp, pc.cp):
        pl.semaphore_signal(sem, inc=1, device_id=(q,), device_id_type=MESH)
    @pl.when(pc.z > 0)
    def _():
        pl.semaphore_signal(sem, inc=1, device_id=(pc.me - 8,), device_id_type=MESH)
    @pl.when(pc.z < pc.Z - 1)
    def _():
        pl.semaphore_signal(sem, inc=1, device_id=(pc.me + 8,), device_id_type=MESH)
    ends = (pc.z == 0).astype(jnp.int32) + (pc.z == pc.Z - 1).astype(jnp.int32)
    pl.semaphore_wait(sem, 5 - ends)


SLABBED = (True, True, False, True, False, False)

CHUNKS = tuple(
    (a, off, w, stacks, 1 if k in (1, 5, 9) else 0)
    for k, (a, off, w, stacks) in enumerate(
        tuple((a, off, 384, 1) for a in range(3) for off in (0, 384, 768))
        + ((3, 0, 384, 1), (3, 384, 128, 1), (4, 0, 768, 2), (4, 768, 768, 2), (4, 1536, 512, 2), (5, 0, 512, 2), (5, 512, 256, 2))
    )
)

def dot(a, b):
    return jnp.dot(a, b, preferred_element_type=jnp.float32)

def dot_nt(a, b):
    return lax.dot_general(a, b, (((1,), (1,)), ((), ())), preferred_element_type=jnp.float32)

def norm_parts(values):
    centred = values - jnp.mean(values, axis=-1, keepdims=True)
    spread = jnp.mean(centred * centred, axis=-1, keepdims=True)
    return centred, lax.rsqrt(spread + EPSILON)

def token_rows(onehot, mod, k):
    images = mod.shape[0] // 6
    total = onehot[:, 0:1] * mod[k * images:k * images + 1]
    for i in range(1, images):
        total = total + onehot[:, i:i + 1] * mod[k * images + i:k * images + i + 1]
    return total

def head_window(h):
    start = jnp.minimum((h * HD) // 128 * 128, D - 256)
    start = pl.multiple_of(start, 128)
    lane = lax.broadcasted_iota(jnp.int32, (1, 256), 1) + start
    return start, (lane >= h * HD) & (lane < h * HD + HD)

def region(out, zs, y, x, c, off, w):
    return out.at[zs, y, x, c, :, pl.ds(off, w)]

def gather_program(n, ins, outs, sems, rounds):
    lsem, zs_sem, zr_sem, xs_sem, xr_sem, cs_sem, cr_sem = sems
    pc = Place(n)
    Z = pc.Z
    z, y, x, c = pc.z, pc.y, pc.x, pc.c
    allz = slice(None); lo = slice(0, Z // 2); hi = slice(Z // 2, Z)
    def plane(r): return rounds[r][4]
    def reg(r, zs, y_, x_):
        a, off, w = rounds[r][:3]
        return region(outs[a], zs, y_, x_, c, off, w)
    def own_in(r):
        a, off, w = rounds[r][:3]
        return ins[a].at[:, pl.ds(off, w)]
    def rcopy(src, dst, ss, rs, dev):
        return pltpu.make_async_remote_copy(src_ref=src, dst_ref=dst, send_sem=ss, recv_sem=rs, device_id=(dev,), device_id_type=MESH)
    def line_part(r, org):
        return reg(r, org, slice(None), slice(None)) if plane(r) else reg(r, org, y, x)
    def zcopy(r, side, s):
        org = z - s if side == 0 else z + s
        dst = line_part(r, org)
        src = own_in(r) if s == 0 and not plane(r) else dst
        return rcopy(src, dst, zs_sem.at[r, side, s], zr_sem.at[r, side, s], pc.me + (8 if side == 0 else -8))
    def zrecv(r, side, s):
        org = z - 1 - s if side == 0 else z + 1 + s
        d = line_part(r, org)
        rcopy(d, d, zs_sem.at[r, side, s], zr_sem.at[r, side, s], pc.me).wait_recv()
    def local(r):
        return pltpu.make_async_copy(own_in(r), reg(r, z, y, x), lsem.at[r])
    def xy(r, k):
        if plane(r):
            if k < 2:
                return rcopy(own_in(r), reg(r, z, y, x), xs_sem.at[r, k], xr_sem.at[r, k], pc.yp if k else pc.xp)
            d = reg(r, z, y, 1 - x) if r % 2 else reg(r, z, 1 - y, x)
            return rcopy(d, d, xs_sem.at[r, 2], xr_sem.at[r, 2], pc.yp if r % 2 else pc.xp)
        if k < 2: d = reg(r, allz, y, x)
        elif k == 2: d = reg(r, lo, y, 1 - x)
        else: d = reg(r, hi, 1 - y, x)
        return rcopy(d, d, xs_sem.at[r, k], xr_sem.at[r, k], pc.xp if k in (0, 3) else pc.yp)
    def core(r, k):
        if plane(r): d = reg(r, allz, slice(None), slice(None))
        else: d = reg(r, allz, y if k in (0, 1) else 1 - y, x if k in (0, 2) else 1 - x)
        return rcopy(d, d, cs_sem.at[r, k], cr_sem.at[r, k], pc.cp)
    def zstart(r, s):
        @pl.when((z - s >= 0) & (z < Z - 1))
        def _(): zcopy(r, 0, s).start()
        @pl.when((z + s <= Z - 1) & (z > 0))
        def _(): zcopy(r, 1, s).start()
    def zwait(r, s):
        @pl.when(z - 1 - s >= 0)
        def _(): zrecv(r, 0, s)
        @pl.when(z + 1 + s <= Z - 1)
        def _(): zrecv(r, 1, s)
    def stage(r, s):
        if plane(r):
            if s == 0:
                local(r).start()
                xy(r, 0).start(); xy(r, 1).start()
            elif s == 1:
                local(r).wait()
                xy(r, 0).wait_recv(); xy(r, 1).wait_recv()
                xy(r, 2).start()
            elif s == 2:
                xy(r, 2).wait_recv()
                zstart(r, 0)
            elif s < Z + 1:
                zwait(r, s - 3)
                zstart(r, s - 2)
            elif s == Z + 1:
                zwait(r, Z - 2)
                core(r, 0).start()
            else:
                core(r, 0).wait_recv()
            return
        if s == 0:
            local(r).start()
            zstart(r, 0)
        elif s < Z - 1:
            zwait(r, s - 1)
            zstart(r, s)
        elif s == Z - 1:
            zwait(r, s - 1)
            local(r).wait()
            xy(r, 0).start(); xy(r, 1).start(); core(r, 0).start()
        elif s == Z:
            xy(r, 0).wait_recv(); xy(r, 2).start(); core(r, 1).start()
            xy(r, 1).wait_recv(); xy(r, 3).start(); core(r, 2).start()
        elif s == Z + 1:
            xy(r, 2).wait_recv(); xy(r, 3).wait_recv(); core(r, 3).start()
        elif s == Z + 2:
            for k in range(4): core(r, k).wait_recv()
    def finish(r):
        for s in range(Z - 1):
            @pl.when((z - s >= 0) & (z < Z - 1))
            def _(): zcopy(r, 0, s).wait_send()
            @pl.when((z + s <= Z - 1) & (z > 0))
            def _(): zcopy(r, 1, s).wait_send()
        for k in range(3 if plane(r) else 4):
            xy(r, k).wait_send()
        for k in range(1 if plane(r) else 4):
            core(r, k).wait_send()
    return stage, finish, Z + 3

def weight_loads(chunk, full, slot, sem, top=0, bottom=None):
    a, off, w, stacks = chunk[:4]
    ref, cps = full[a], []
    rows, sw = ref.shape[4], w // stacks
    bottom = bottom or rows
    for j in range(4):
        for s in range(stacks):
            cps.append((ref.at[:, :, j // 2, j % 2, pl.ds(top, bottom - top), pl.ds(off + s * sw, sw)],
                        slot.at[j, :, :, pl.ds(s * rows + top, bottom - top), pl.ds(0, sw)]))
    return [pltpu.make_async_copy(s, d, sem.at[k]) for k, (s, d) in enumerate(cps)]

def chunk_weight(chunk, slot, rows, part):
    sw = chunk[2] // chunk[3]
    Z = slot.shape[1]
    return jnp.concatenate(
        [slot[j, zz, yy, part * rows:(part + 1) * rows, 0:sw] for zz in range(Z) for yy in range(2) for j in range(4)], axis=0)

def scatter_program(n, R, G, CR, OWN, XR, ZR, keep, sems, final, late=(), P=None):
    cs, cr, xs, xr, zs_, zr, credit = sems
    keep_g, keep_c, keep_o, keep_x, keep_p = keep
    pc = Place(n)
    Z = pc.Z; H = Z // 2
    z, y, x, c = pc.z, pc.y, pc.x, pc.c
    up_dev = jnp.minimum(pc.me + 8, n - 1)
    down_dev = jnp.maximum(pc.me - 8, 0)
    early = [r for r in range(R) if r not in late]
    def turn(r): return (late if r in late else early).index(r)
    def first_use(r): return turn(r) < (keep_p if r in late else keep_x)
    def last_use(r): return turn(r) + (keep_p if r in late else keep_x) >= len(late if r in late else early)
    def base(r): return 5 if r in late else 1
    def rcopy(src, dst, ss, rs, dev):
        return pltpu.make_async_remote_copy(src_ref=src, dst_ref=dst, send_sem=ss, recv_sem=rs, device_id=(dev,), device_id_type=MESH)
    def signal(k, dev):
        pl.semaphore_signal(credit.at[k], inc=1, device_id=(dev,), device_id_type=MESH)
    def spend(k):
        pl.semaphore_wait(credit.at[k], 1)
    def core(r): return rcopy(G(r).at[1 - c], CR(r), cs.at[r], cr.at[r], pc.cp)
    def xy(r, k):
        if r in late:
            own, _, px = P(r)
            dev = (pc.yp if r % 2 else pc.xp, pc.xp, pc.yp)[k]
            src = own.at[x if k == 2 else 1 - x, z, y if k == 1 else 1 - y]
            return rcopy(src, px.at[k], xs.at[r, k], xr.at[r, k], dev)
        b, xb = OWN(r), XR(r)
        if k == 0: return rcopy(b.at[1 - x, 0:H, 1 - y], xb.at[0:H], xs.at[r, 0], xr.at[r, 0], pc.yp)
        if k == 1: return rcopy(b.at[1 - x, H:Z, 1 - y], xb.at[H:Z], xs.at[r, 1], xr.at[r, 1], pc.xp)
        if k == 2: return rcopy(b.at[1 - x, :, y], xb.at[Z:2 * Z], xs.at[r, 2], xr.at[r, 2], pc.xp)
        return rcopy(b.at[x, :, 1 - y], xb.at[2 * Z:3 * Z], xs.at[r, 3], xr.at[r, 3], pc.yp)
    def line_refs(r, d):
        if r in late:
            own, pz, _ = P(r)
            return own.at[:, d], pz
        return XR(r).at[Z + d], ZR(r)
    def zc(r, side, d):
        src, dst = line_refs(r, d)
        at = d - z - 1 if side == 0 else Z - z + 1 + d
        return rcopy(src, dst.at[at], zs_.at[r, side, d], zr.at[r, side, d], up_dev if side == 0 else down_dev)
    def zgot(r, side, d):
        src, dst = line_refs(r, d)
        at = d - z if side == 0 else Z - z + d
        rcopy(src, dst.at[at], zs_.at[r, side, d], zr.at[r, side, d], up_dev if side == 0 else down_dev).wait_recv()
    def plane_sent(o):
        for k in range(4): xy(early[o], k).wait_send()
    def zwaits_send(r):
        for d in range(Z):
            @pl.when(d > z)
            def _(): zc(r, 0, d).wait_send()
            @pl.when(d < z)
            def _(): zc(r, 1, d).wait_send()
    def add_line(r, side, d, at):
        if r in late:
            own, pz, _ = P(r)
            for xx in range(2):
                for yy in range(2):
                    own[xx, d, yy] = own[xx, d, yy] + pz[at, xx, yy]
        else:
            XR(r)[Z + d] = XR(r)[Z + d] + ZR(r)[at]
    def zstep(r, s):
        for side in (0, 1):
            p = s if side == 0 else Z - 1 - s
            @pl.when(z == p)
            def _():
                if not first_use(r) and (p < Z - 1 if side == 0 else p > 0):
                    spend(base(r) + 2 + side)
                for d in range(Z):
                    if (d > p) if side == 0 else (d < p):
                        if s > 0:
                            zgot(r, side, d)
                            add_line(r, side, d, d - p if side == 0 else Z - p + d)
                        zc(r, side, d).start()
    def give_back(r):
        if not last_use(r):
            signal(base(r), pc.xp)
            signal(base(r) + 1, pc.yp)
            @pl.when(z < Z - 1)
            def _(): signal(base(r) + 3, up_dev)
            @pl.when(z > 0)
            def _(): signal(base(r) + 2, down_dev)
    def before(r):
        if r >= keep_g:
            core(r - keep_g).wait_send()
    def core_sum(r, out):
        b = G(r).at[c]
        core(r).wait_recv()
        def add(i, carry):
            xx, zz, yy = i // (2 * Z), (i // 2) % Z, i % 2
            out[xx, zz, yy] = b[xx, zz, yy] + CR(r)[xx, zz, yy]
            return carry
        lax.fori_loop(0, 4 * Z, add, 0)
        if r + keep_c < R:
            signal(0, pc.cp)
    def late_stage(r, s):
        own, pz, px = P(r)
        if s == 1:
            core_sum(r, own)
            zstep(r, 0)
        elif s < Z:
            zstep(r, s - 1)
        elif s == Z:
            for d in range(Z):
                @pl.when(d == z)
                def _():
                    if d > 0:
                        zgot(r, 0, d)
                        add_line(r, 0, d, 0)
                    if d < Z - 1:
                        zgot(r, 1, d)
                        add_line(r, 1, d, Z)
            if not first_use(r):
                spend(base(r))
                spend(base(r) + 1)
            xy(r, 0).start()
            xy(r, 2 if r % 2 else 1).start()
        elif s == Z + 1:
            xy(r, 0).wait_recv()
            if r % 2:
                own[1 - x, z, y] = own[1 - x, z, y] + px[0]
            else:
                own[x, z, 1 - y] = own[x, z, 1 - y] + px[0]
            xy(r, 1 if r % 2 else 2).start()
        else:
            xy(r, 1).wait_recv()
            xy(r, 2).wait_recv()
            final(r, own[x, z, y].astype(jnp.float32) + px[1].astype(jnp.float32) + px[2].astype(jnp.float32))
            for k in range(3): xy(r, k).wait_send()
            zwaits_send(r)
            give_back(r)
    def stage(r, s):
        b = None if r in late else OWN(r)
        if s == 0:
            if r >= keep_c:
                spend(0)
            core(r).start()
        elif r in late:
            late_stage(r, s)
        elif s == 1:
            if turn(r) >= keep_o:
                plane_sent(turn(r) - keep_o)
            core_sum(r, b)
            if not first_use(r):
                spend(base(r))
                spend(base(r) + 1)
            xy(r, 0).start(); xy(r, 1).start()
        elif s == 2:
            xy(r, 0).wait_recv()
            def add(i, carry):
                b[1 - x, i, y] = b[1 - x, i, y] + XR(r)[i]
                return carry
            lax.fori_loop(0, H, add, 0)
            xy(r, 2).start()
            xy(r, 1).wait_recv()
            def add(i, carry):
                b[x, i, 1 - y] = b[x, i, 1 - y] + XR(r)[i]
                return carry
            lax.fori_loop(H, Z, add, 0)
            xy(r, 3).start()
        elif s == 3:
            xy(r, 2).wait_recv(); xy(r, 3).wait_recv()
            def add(i, carry):
                XR(r)[Z + i] = b[x, i, y] + XR(r)[Z + i] + XR(r)[2 * Z + i]
                return carry
            lax.fori_loop(0, Z, add, 0)
            zstep(r, 0)
        elif s < Z + 2:
            zstep(r, s - 3)
        else:
            for d in range(Z):
                @pl.when(d == z)
                def _():
                    tot = XR(r)[Z + d].astype(jnp.float32)
                    if d > 0:
                        zgot(r, 0, d)
                        tot = tot + ZR(r)[0].astype(jnp.float32)
                    if d < Z - 1:
                        zgot(r, 1, d)
                        tot = tot + ZR(r)[Z].astype(jnp.float32)
                    final(r, tot)
            zwaits_send(r)
            give_back(r)
    def finish():
        for r in range(max(0, R - keep_g), R):
            core(r).wait_send()
        for o in range(max(0, len(early) - keep_o), len(early)):
            plane_sent(o)
    return before, stage, finish, Z + 3

def scatter_sems(R, Z):
    D_ = pltpu.SemaphoreType.DMA
    return [D_((R,)), D_((R,)), D_((R, 4)), D_((R, 4)), D_((R, 2, Z)), D_((R, 2, Z)), pltpu.SemaphoreType.REGULAR((9,))]

BIASES = (6 * D, 2 * D, 2 * D, FF, P_SIZE, P_SIZE, Z_OUT)

def forward_kernel(n, images, offs, *refs):
    rounds = CHUNKS
    qkv_w, attn_in, up_w, in_w, down_w, mid_w, out_w, ada_w, mail, tokens, onehot, same = refs[:12]
    refs = refs[12:]
    full, refs = refs[:6], refs[6:]
    act_outs, (mod, cond_mine) = refs[:15], refs[15:17]
    refs = refs[17:]
    acts, refs = refs[:15], refs[15:]
    (first_in, projected, heads, branch_attn, middle, second_in, up_pre, up_act, branch_mlp, mixed,
     first_pre, first_act, second_pre, second_act, features) = acts
    act_sem, refs = refs[0], refs[1:]
    def leave(*which):
        return [pltpu.make_async_copy(acts[k], act_outs[k], act_sem.at[k]) for k in which]
    slots, attn_w, first_own, up_own, in_own, box, mod_own, mod_core, mod_xy, mod_line = refs[:10]
    bias_rows, refs = refs[10:17], refs[17:]
    load_sem, mail_send, mail_recv = refs[:3]
    ada_b, qv_b, tail_b, up_b, in_b, mid_b, out_b = bias_rows
    R, Z = len(rounds), n // 8
    pc = Place(n)
    stage, finish, S = gather_program(
        n, (first_own, up_own, down_w, in_own, mid_w, out_w), full, refs[3:10], rounds)
    per = D // n
    for s in range(4):
        first_own[s * per:(s + 1) * per] = qkv_w[:, s * D:(s + 1) * D] if s < 3 else attn_in[...]
        up_own[s * per:(s + 1) * per] = up_w[:, s * (FF // 4):(s + 1) * (FF // 4)]
        in_own[s * per:(s + 1) * per] = in_w[:, s * (P_SIZE // 4):(s + 1) * (P_SIZE // 4)]

    def mod_final(r, tot):
        for k in range(6):
            for i in range(images):
                row = k * images + i
                mod[row:row + 1] = tot[row:row + 1] + ada_b[:, k * D:(k + 1) * D]
    _, mod_stage, mod_finish, _ = scatter_program(
        n, 1, lambda r: mod_own, lambda r: mod_core, lambda r: mod_own.at[pc.c], lambda r: mod_xy, lambda r: mod_line, (1, 1, 1, 1, 1), refs[10:], mod_final)

    def letter(k):
        dest = lax.rem(pc.me + k, n)
        return pltpu.make_async_remote_copy(
            src_ref=mail.at[dest], dst_ref=box.at[pc.me], send_sem=mail_send.at[k], recv_sem=mail_recv.at[k],
            device_id=(dest,), device_id_type=MESH)

    def send_mail():
        def go(k, carry):
            letter(k).start()
            return carry
        lax.fori_loop(1, n, go, 0)
        box[pc.me] = mail[pc.me]

    def read_mail():
        def wait(k, carry):
            letter(k).wait()
            return carry
        lax.fori_loop(1, n, wait, 0)
        cond_mine[...] = jnp.concatenate([box[d, 0:images, 0:per] for d in range(n)], axis=0)
        row = images
        for ref, width in zip(bias_rows, BIASES):
            part = width // n
            for at in range(0, part, 128):
                size = min(128, part - at)
                for d in range(n):
                    ref[:, d * part + at:d * part + at + size] = box[d, row:row + 1, 0:size].astype(jnp.float32)
                row += 1
        mod_own[...] = jnp.zeros_like(mod_own)
        for k in range(6):
            value = dot(cond_mine[...], ada_w[:, k * D:(k + 1) * D])
            for d in range(n):
                mod_own[d % 2, (d // 2) % 2, d // 8, (d // 4) % 2, k * images:(k + 1) * images] = value[d * images:(d + 1) * images]
    barrier(pc, n)
    last_of = {a: max(r for r in range(R) if rounds[r][0] == a) for a in range(6)}

    def loads(r):
        return weight_loads(rounds[r], full, slots.at[r % 2], load_sem.at[r % 2])

    def prepare():
        oh, md = onehot[...], mod
        values = tokens[...].astype(jnp.float32)
        centred, scale = norm_parts(values)
        first_in[...] = (centred * scale * (1.0 + token_rows(oh, md, 1)) + token_rows(oh, md, 0)).astype(jnp.bfloat16)

    def attention():
        def head(h, carry):
            start, inside = head_window(h)
            q = projected[:, pl.ds(start, 256)]
            k = projected[:, pl.ds(pl.multiple_of(start + D, 128), 256)]
            v = projected[:, pl.ds(pl.multiple_of(start + 2 * D, 128), 256)]
            q = jnp.where(inside, q, jnp.zeros_like(q))
            scores = jnp.where(same[...] > 0.0, dot_nt(q, k) * HD ** (-0.5), -1e30)
            e = jnp.exp(scores - jnp.max(scores, axis=-1, keepdims=True))
            p = (e / jnp.sum(e, axis=-1, keepdims=True)).astype(jnp.bfloat16)
            o = dot(p, v).astype(jnp.bfloat16)
            heads[:, pl.ds(start, 256)] = jnp.where(inside, o, heads[:, pl.ds(start, 256)])
            return carry
        heads[...] = jnp.zeros_like(heads)
        lax.fori_loop(0, HEADS, head, 0)
        for i in range(3):
            cols = slice(384 * i, 384 * (i + 1))
            branch_attn[:, cols] = dot(heads[...], attn_w[:, cols]) + tail_b[:, cols]
        oh, md = onehot[...], mod
        mid = tokens[...].astype(jnp.float32) + token_rows(oh, md, 2) * branch_attn[...]
        middle[...] = mid
        centred, scale = norm_parts(mid)
        second_in[...] = (centred * scale * (1.0 + token_rows(oh, md, 4)) + token_rows(oh, md, 3)).astype(jnp.bfloat16)

    def compute(r):
        a, off, w, stacks = rounds[r][:4]
        slot = slots.at[r % 2]
        sw = w // stacks
        def weight(part):
            return chunk_weight(rounds[r], slot, per if SLABBED[a] else slot_rows[a], part)
        if a == 0:
            for j in range(3):
                cols = slice(j * D + off, j * D + off + w)
                value = dot(first_in[...], weight(j))
                if j != 1:
                    at = (j // 2) * D + off
                    value = value + qv_b[:, at:at + w]
                projected[:, cols] = value.astype(jnp.bfloat16)
            attn_w[:, off:off + w] = weight(3)
            if r == last_of[0]:
                attention()
        elif a == 1:
            for j in range(4):
                cols = slice(j * (FF // 4) + off, j * (FF // 4) + off + w)
                pre = dot(second_in[...], weight(j)) + up_b[:, cols]
                up_pre[:, cols] = pre
                up_act[:, cols] = gelu_tanh(pre).astype(jnp.bfloat16)
        elif a == 2:
            branch_mlp[:, off:off + w] = dot(up_act[...], weight(0)) + tail_b[:, D + off:D + off + w]
            if r == last_of[2]:
                hidden = middle[...] + token_rows(onehot[...], mod, 5) * branch_mlp[...]
                mixed[...] = hidden.astype(jnp.bfloat16)
        elif a == 3:
            for j in range(4):
                cols = slice(j * (P_SIZE // 4) + off, j * (P_SIZE // 4) + off + w)
                pre = dot(mixed[...], weight(j)) + in_b[:, cols]
                first_pre[:, cols] = pre
                first_act[:, cols] = sigmoid_linear(pre).astype(jnp.bfloat16)
        else:
            for s in range(stacks):
                cols = slice(off + s * sw, off + (s + 1) * sw)
                if a == 4:
                    pre = dot(first_act[...], weight(s)) + mid_b[:, cols]
                    second_pre[:, cols] = pre
                    second_act[:, cols] = sigmoid_linear(pre).astype(jnp.bfloat16)
                else:
                    features[:, cols] = dot(second_act[...], weight(s)) + out_b[:, cols]
        if r == last_of[a]:
            for cp in leave(*left_by[a]): cp.start()
    slot_rows = {2: FF // n, 4: P_SIZE // n, 5: P_SIZE // n}
    left_by = {0: (0, 1, 2, 3, 4, 5), 1: (6, 7), 2: (8, 9), 3: (10, 11), 4: (12, 13), 5: (14,)}

    offs_of = lambda r: offs[rounds[r][4]]
    ready = [max(r2 + offs_of(r2)[S - 1] for r2 in range(r + 1)) for r in range(R)]
    mod_at = 2
    t, computed, loaded, began = 0, 0, 0, []
    while computed < R:
        for s in reversed(range(S)):
            for r in range(R):
                if r + offs_of(r)[s] == t:
                    stage(r, s)
        if t == 0:
            send_mail()
        if t == mod_at:
            read_mail()
        if mod_at <= t < mod_at + Z + 3:
            mod_stage(0, t - mod_at)
        if t == mod_at + Z + 2:
            prepare()
        done_now = 0
        while True:
            while loaded < R and ready[loaded] <= t and loaded < computed + 2:
                for cp in loads(loaded): cp.start()
                loaded += 1
                began.append(t)
            if computed == loaded or t < mod_at + Z + 2 or (t < ready[-1] and (done_now == 2 or began[computed] == t)):
                break
            for cp in loads(computed): cp.wait()
            compute(computed)
            computed += 1
            done_now += 1
        t += 1
    for cp in leave(*range(15)): cp.wait()
    for r in range(R):
        finish(r)
    mod_finish()

def forward(n, images, shards, small, offs, cid):
    Z, R = n // 8, len(CHUNKS)
    f32, bf = jnp.float32, jnp.bfloat16
    tok = small[2].shape[0]
    blocks = ((4 * D // n, D), (4 * D // n, FF // 4), (FF // n, D), (4 * D // n, P_SIZE // 4), (P_SIZE // n, P_SIZE), (P_SIZE // n, Z_OUT))
    shapes = [jax.ShapeDtypeStruct((Z, 2, 2, 2) + b, bf) for b in blocks]
    acts = [(D, bf), (3 * D, bf), (D, bf), (D, f32), (D, f32), (D, bf), (FF, f32), (FF, bf), (D, f32), (D, bf),
            (P_SIZE, f32), (P_SIZE, bf), (P_SIZE, f32), (P_SIZE, bf), (Z_OUT, f32)]
    shapes += [jax.ShapeDtypeStruct((tok, w), dt) for w, dt in acts]
    mod_dims = (-(-6 * images // 8) * 8, D)
    shapes.append(jax.ShapeDtypeStruct((6 * images, D), f32))
    shapes.append(jax.ShapeDtypeStruct((n * images, D // n), bf))
    D_, V = pltpu.SemaphoreType.DMA, pltpu.VMEM
    hbm, vmem = pl.BlockSpec(memory_space=pltpu.HBM), pl.BlockSpec(memory_space=pltpu.VMEM)
    return pl.pallas_call(
        functools.partial(forward_kernel, n, images, offs),
        out_shape=shapes,
        in_specs=[vmem] * 4 + [hbm] * 3 + [vmem] * len(small),
        out_specs=[hbm] * (6 + len(acts)) + [vmem] * 2,
        scratch_shapes=[V((tok, w), dt) for w, dt in acts] + [D_((len(acts),))] + [
            V((2, 4, Z, 2, 144, 384), bf), V((D, D), bf), V(blocks[0], bf), V(blocks[1], bf), V(blocks[3], bf),
            V((n, 16, 128), bf),
            V((2, 2, Z, 2) + mod_dims, f32), V((2, Z, 2) + mod_dims, f32), V((3 * Z,) + mod_dims, f32), V((Z + 1,) + mod_dims, f32),
        ] + [V((1, w), f32) for w in BIASES] + [
            D_((2, 8)), D_((n,)), D_((n,)),
            D_((R,)), D_((R, 2, Z - 1)), D_((R, 2, Z - 1)), D_((R, 4)), D_((R, 4)), D_((R, 4)), D_((R, 4)),
        ] + scatter_sems(1, Z),
        compiler_params=pltpu.CompilerParams(collective_id=cid, has_side_effects=True, vmem_limit_bytes=58 * 2**20),
    )(*shards, *small)


def back_rounds(order):
    out = []
    for a, total, width, stacks in order:
        out += [(a, off, min(width, total - off), stacks) for off in range(0, total, width)]
    return tuple(out)

BACK_CHUNKS = back_rounds(((5, 768, 512, 2), (4, P_SIZE, 512, 2), (3, P_SIZE // 4, 256, 1), (2, D, 256, 1), (1, FF // 4, 256, 1), (0, D, 256, 1)))
LATE = (3, 8, 12, 16)
CHAIN = back_rounds(((5, 768, 768, 2), (4, P_SIZE, 768, 2), (3, P_SIZE // 4, 384, 1), (2, D, 384, 1), (1, FF // 4, 384, 1), (6, D, 384, 1))) + tuple(
    (7, 4 * i, 4, 1) for i in range(HEADS // 4)
) + back_rounds(((0, D, 384, 1),))

def dot_tn(a, b):
    return lax.dot_general(a, b, (((0,), (0,)), ((), ())), preferred_element_type=jnp.float32)

def norm_back(centred, scale, grad):
    normed = centred * scale
    inner = jnp.mean(grad * normed, axis=-1, keepdims=True)
    return scale * (grad - jnp.mean(grad, axis=-1, keepdims=True) - normed * inner)

def sigmoid_linear_slope(v):
    s = jax.nn.sigmoid(v)
    return s * (1.0 + v * (1.0 - s))

def gelu_slope(v):
    t = jnp.tanh(0.7978845608028654 * (v + 0.044715 * v * v * v))
    return 0.5 * (1.0 + t) + 0.5 * v * (1.0 - t * t) * 0.7978845608028654 * (1.0 + 3.0 * 0.044715 * v * v)

def backward_kernel(n, images, chain_per_tick, scatter_offs, mod_offs, *refs):
    Z = n // 8
    full, refs = refs[:6], refs[6:]
    (tokens, onehot, same, mod, targets, out_grad), act_ins, refs = refs[:6], refs[6:21], refs[21:]
    outs, refs = refs[:7], refs[7:]
    tokens_grad, qkv_sums, attn_sums, mlp_sums, up_sums, in_sums, mid_sums, out_sums, mod_all = refs[:9]
    refs = refs[9:]
    acts, act_sem, refs = refs[:15], refs[15], refs[16:]
    (first_in, projected, heads, branch_attn, middle, second_in, up_pre, up_act, branch_mlp, mixed,
     first_pre, first_act, second_pre, second_act, features) = acts
    def bring(which):
        return [pltpu.make_async_copy(act_ins[k], acts[k], act_sem.at[k]) for k in which]
    soon, later = (14, 12, 13, 11, 10), (9, 8, 6, 7, 5, 4, 3, 2, 1, 0)
    for cp in bring(soon + later): cp.start()
    (slots, load_sem, G_, CR_, OWN_, XR_, ZR_, PB_, PZ_, PX_, feature_grad, second_back, first_back, hidden_grad, mlp_grad, up_grad,
     middle_grad, attn_grad, heads_grad, projected_grad, wide, narrow, mod_grad, mod_rows, mod_lines) = refs[:25]
    refs = refs[25:]
    rounds, R = BACK_CHUNKS, len(BACK_CHUNKS)
    per = D // n
    bf = jnp.bfloat16
    pc = Place(n)

    def dims(r):
        a, off, w, stacks = rounds[r]
        return (4 * per if a < 4 else stacks * (P_SIZE // n)), w // stacks
    keep = (G_.shape[0], CR_.shape[0], OWN_.shape[0], XR_.shape[0], PB_.shape[0])
    early = [r for r in range(R) if r not in LATE]
    def cut(ref, r, at):
        rows, w = dims(r)
        lead = (slice(None),) * (len(ref.shape) - 3)
        return ref.at[(at % ref.shape[0],) + lead + (slice(0, rows), slice(0, w))]
    def final(r, tot):
        a, off, w, stacks = rounds[r]
        rows, sw = dims(r)
        qkv_out, attn_out, up_out, down_out, in_out, mid_out, out_out = outs
        if SLABBED[a]:
            for s in range(4):
                part = tot[s * per:(s + 1) * per]
                if a == 0 and s == 3:
                    attn_out[:, off:off + w] = part
                else:
                    ref, q = {0: (qkv_out, D), 1: (up_out, FF // 4), 3: (in_out, P_SIZE // 4)}[a]
                    ref[:, s * q + off:s * q + off + w] = part
        else:
            rows = rows // stacks
            ref = {2: down_out, 4: mid_out, 5: out_out}[a]
            for s in range(stacks):
                ref[:, off + s * sw:off + (s + 1) * sw] = tot[s * rows:(s + 1) * rows]
    before, stage, finish, S = scatter_program(
        n, R, lambda r: cut(G_, r, r), lambda r: cut(CR_, r, r),
        lambda r: cut(OWN_, r, early.index(r)), lambda r: cut(XR_, r, early.index(r)), lambda r: cut(ZR_, r, early.index(r)), keep, refs[:7], final, LATE,
        lambda r: tuple(cut(ref, r, LATE.index(r)) for ref in (PB_, PZ_, PX_)))
    mod_stage, mod_finish, _ = gather_program(n, [mod_rows], [mod_all], refs[7:], ((0, 0, 128, 1, 0),))
    barrier(pc)
    mod_lines[...] = jnp.zeros_like(mod_lines)

    def image_sums(k, value):
        cols = slice(k * D, (k + 1) * D)
        for i in range(images):
            mod_grad[i:i + 1, cols] = jnp.sum(value * onehot[:, i:i + 1], axis=0, keepdims=True)

    def sums(value):
        return jnp.sum(value.astype(jnp.float32), axis=0, keepdims=True)

    def start_chain():
        f, t = features[...], targets[...].astype(jnp.float32)
        f_norm = jnp.sqrt(jnp.sum(f * f, axis=1, keepdims=True) + EPSILON)
        t_norm = jnp.sqrt(jnp.sum(t * t, axis=1, keepdims=True) + EPSILON)
        inner = jnp.sum(f * t, axis=1, keepdims=True)
        grad = -0.5 * (t / (f_norm * t_norm) - f * (inner / (f_norm * f_norm * f_norm * t_norm)))
        feature_grad[...] = grad.astype(bf)
        out_sums[...] = sums(feature_grad[...])

    def attention_back(begin, count):
        if begin == 0:
            projected_grad[...] = jnp.zeros_like(projected_grad)
        def head(h, carry):
            start, inside = head_window(h)
            at_q, at_k, at_v = [pl.ds(pl.multiple_of(start + i * D, 128), 256) for i in range(3)]
            q, k, v = projected[:, at_q], projected[:, at_k], projected[:, at_v]
            q = jnp.where(inside, q, jnp.zeros_like(q))
            g = heads_grad[:, at_q]
            g = jnp.where(inside, g, jnp.zeros_like(g))
            scores = jnp.where(same[...] > 0.0, dot_nt(q, k) * HD ** (-0.5), -1e30)
            e = jnp.exp(scores - jnp.max(scores, axis=-1, keepdims=True))
            p = e / jnp.sum(e, axis=-1, keepdims=True)
            pg = dot_nt(g, v)
            sg = (p * (pg - jnp.sum(p * pg, axis=-1, keepdims=True))).astype(bf)
            for at, value in (
                (at_q, dot(sg, k) * HD ** (-0.5)),
                (at_k, dot_tn(sg, q) * HD ** (-0.5)),
                (at_v, dot_tn(p.astype(bf), g)),
            ):
                projected_grad[:, at] = jnp.where(inside, value.astype(bf), projected_grad[:, at])
            return carry
        lax.fori_loop(begin, begin + count, head, 0)
        if begin + count == HEADS:
            qkv_sums[...] = sums(projected_grad[...])

    C = len(CHAIN)
    last = {a: max(k for k in range(C) if CHAIN[k][0] == a) for a in range(8)}
    first = {a: min(k for k in range(C) if CHAIN[k][0] == a) for a in range(8)}

    def chain_loads(k):
        a, off, w, stacks = CHAIN[k]
        slot, sem = slots.at[k % 2], load_sem.at[k % 2]
        if a == 7:
            return []
        if a == 6:
            return weight_loads((0, off, w, stacks), full, slot, sem, 3 * per // 16 * 16)
        return weight_loads((a, off, w, stacks), full, slot, sem, 0, -(-3 * per // 16) * 16 if a == 0 else None)

    def accumulate(acc, cols, new, k, a):
        acc[:, cols] = new if k == first[a] else acc[:, cols] + new

    def chain(k):
        a, off, w, stacks = CHAIN[k]
        if a == 7:
            attention_back(off, w)
            return
        if k == first[3]:
            for cp in bring(later): cp.wait()
        slot = slots.at[k % 2]
        sw = w // stacks
        if a in (4, 5):
            grad = second_back if a == 4 else feature_grad
            new = None
            for s in range(stacks):
                part = dot_nt(grad[:, off + s * sw:off + (s + 1) * sw], chunk_weight(CHAIN[k], slot, P_SIZE // n, s))
                new = part if new is None else new + part
            accumulate(wide, slice(0, P_SIZE), new, k, a)
            if k == last[a]:
                target, pre = (second_back, second_pre) if a == 5 else (first_back, first_pre)
                target[...] = (wide[:, 0:P_SIZE] * sigmoid_linear_slope(pre[...])).astype(bf)
                (mid_sums if a == 5 else in_sums)[...] = sums(target[...])
        elif a == 2:
            whole = chunk_weight(CHAIN[k], slot, FF // n, 0)
            for q in range(4):
                weight = whole[q * D:(q + 1) * D]
                accumulate(wide, slice(q * D, (q + 1) * D), dot_nt(mlp_grad[:, off:off + w], weight), k, a)
            if k == last[a]:
                for q in range(4):
                    cols = slice(q * D, (q + 1) * D)
                    up_grad[:, cols] = (wide[:, cols] * gelu_slope(up_pre[:, cols])).astype(bf)
                up_sums[...] = sums(up_grad[...])
        else:
            src, parts, width = {3: (first_back, range(4), P_SIZE // 4), 1: (up_grad, range(4), FF // 4),
                                 0: (projected_grad, range(3), D), 6: (attn_grad, range(3, 4), D)}[a]
            new = None
            for j in parts:
                col = off if a == 6 else j * width + off
                weight = chunk_weight(CHAIN[k], slot, per, j)
                part = dot_nt(src[:, col:col + w], weight)
                new = part if new is None else new + part
            accumulate(narrow, slice(0, D), new, k, a)
            if k == last[a]:
                oh = onehot[...]
                if a == 3:
                    hg = out_grad[...].astype(jnp.float32) + narrow[...]
                    hidden_grad[...] = hg
                    mlp_grad[...] = (hg * token_rows(oh, mod, 5)).astype(bf)
                    mlp_sums[...] = sums(mlp_grad[...])
                    image_sums(5, hg * branch_mlp[...])
                elif a == 1:
                    g = narrow[...]
                    centred, scale = norm_parts(middle[...])
                    image_sums(3, g)
                    image_sums(4, g * (centred * scale))
                    mg = hidden_grad[...] + norm_back(centred, scale, g * (1.0 + token_rows(oh, mod, 4)))
                    middle_grad[...] = mg
                    attn_grad[...] = (mg * token_rows(oh, mod, 2)).astype(bf)
                    attn_sums[...] = sums(attn_grad[...])
                    image_sums(2, mg * branch_attn[...])
                elif a == 6:
                    heads_grad[...] = narrow[...].astype(bf)
                else:
                    g = narrow[...]
                    centred, scale = norm_parts(tokens[...].astype(jnp.float32))
                    image_sums(0, g)
                    image_sums(1, g * (centred * scale))
                    tg = middle_grad[...] + norm_back(centred, scale, g * (1.0 + token_rows(oh, mod, 1)))
                    tokens_grad[...] = tg.astype(bf)
                    stacked = mod_grad[...]
                    rows = 6 * D // 128
                    for i in range(images):
                        for k in range(rows):
                            mod_lines[i * rows + k:i * rows + k + 1] = stacked[i:i + 1, 128 * k:128 * (k + 1)]
                    mod_rows[...] = mod_lines[...].astype(bf)

    def produce(r):
        a, off, w, stacks = rounds[r]
        before(r)
        left, right = {5: (second_act, feature_grad), 4: (first_act, second_back), 3: (mixed, first_back), 2: (up_act, mlp_grad),
                       1: (second_in, up_grad), 0: (first_in, projected_grad)}[a]
        rows, sw = dims(r)
        g = cut(G_, r, r)
        def put(d, at, value):
            g[d % 2, (d // 2) % 2, d // 8, (d // 4) % 2, at:at + value.shape[0]] = value
        if SLABBED[a]:
            for s in range(4):
                if a == 0 and s == 3:
                    value = dot_tn(heads[...], attn_grad[:, off:off + w])
                else:
                    at = {3: P_SIZE // 4, 1: FF // 4, 0: D}[a] * s + off
                    value = dot_tn(left[...], right[:, at:at + w])
                value = value.astype(bf)
                for d in range(n):
                    put(d, s * per, value[d * per:(d + 1) * per])
        else:
            rows = rows // stacks
            piece = 1152 if a == 2 else 1024
            for s in range(stacks):
                for part in range(left.shape[1] // piece):
                    at = off + s * sw
                    value = dot_tn(left[:, part * piece:(part + 1) * piece], right[:, at:at + sw]).astype(bf)
                    for i in range(piece // rows):
                        put(part * (piece // rows) + i, s * rows, value[i * rows:(i + 1) * rows])

    need = {5: 0, 4: first[4], 3: first[3], 2: first[2], 1: first[1], 0: first[0]}
    done = 0
    mod_start = None
    for cp in chain_loads(0): cp.start()
    for cp in bring(soon): cp.wait()
    start_chain()
    t = 0
    while True:
        for s in reversed(range(1, S)):
            for r in range(R):
                if r + scatter_offs[r in LATE][s] == t:
                    stage(r, s)
        busy = any(r + scatter_offs[r in LATE][S - 1] >= t for r in range(R))
        if t < R:
            busy = True
            while done < need[rounds[t][0]]:
                done = advance(done, chain_loads, chain, C)
            produce(t)
            stage(t, 0)
        for _ in range(chain_per_tick):
            if done < C:
                done = advance(done, chain_loads, chain, C)
        if done == C and mod_start is None:
            mod_start = t
        if mod_start is not None:
            for s in reversed(range(Z + 3)):
                if t - mod_start == mod_offs[s]:
                    mod_stage(0, s)
            busy = busy or t - mod_start < mod_offs[-1]
        if not busy:
            break
        t += 1
    finish()
    mod_finish(0)

def advance(k, chain_loads, chain, total):
    if k + 1 < total:
        for cp in chain_loads(k + 1): cp.start()
    for cp in chain_loads(k): cp.wait()
    chain(k)
    return k + 1

def backward(n, images, weights, acts, mod_height, plan, cid):
    Z, R = n // 8, len(BACK_CHUNKS)
    f32, bf = jnp.float32, jnp.bfloat16
    tok = acts[0].shape[0]
    chain_per_tick, scatter_offs, mod_offs, keep = plan
    most = (144, max(c[2] // c[3] for c in BACK_CHUNKS))
    late = most if LATE else (16, 128)
    shapes = [jax.ShapeDtypeStruct((k // n, w), f32) for k, w in (
        (D, 3 * D), (D, D), (D, FF), (FF, D), (D, P_SIZE), (P_SIZE, P_SIZE), (P_SIZE, Z_OUT))]
    shapes.append(jax.ShapeDtypeStruct((tok, D), bf))
    shapes += [jax.ShapeDtypeStruct((1, w), f32) for w in (3 * D, D, D, FF, P_SIZE, P_SIZE, Z_OUT)]
    hbm, vmem = pl.BlockSpec(memory_space=pltpu.HBM), pl.BlockSpec(memory_space=pltpu.VMEM)
    shapes.append(jax.ShapeDtypeStruct((Z, 2, 2, 2, mod_height, 128), bf))
    D_ = pltpu.SemaphoreType.DMA
    V = pltpu.VMEM
    return pl.pallas_call(
        functools.partial(backward_kernel, n, images, chain_per_tick, scatter_offs, mod_offs),
        out_shape=shapes,
        in_specs=[hbm] * 6 + [vmem] * 6 + [hbm] * (len(acts) - 6),
        out_specs=[vmem] * 15 + [hbm],
        scratch_shapes=[V(a.shape, a.dtype) for a in acts[6:]] + [D_((len(acts) - 6,))] + [
            V((2, 4, Z, 2, 144, 384), bf),
            D_((2, 8)),
            V((keep[0], 2, 2, Z, 2) + most, bf),
            V((keep[1], 2, Z, 2) + most, bf),
            V((keep[2], 2, Z, 2) + most, bf),
            V((keep[3], 3 * Z) + most, bf),
            V((keep[3], Z + 1) + most, bf),
            V((keep[4], 2, Z, 2) + late, bf), V((keep[4], Z + 1, 2, 2) + late, bf), V((keep[4], 3) + late, bf),
            V((tok, Z_OUT), bf), V((tok, P_SIZE), bf), V((tok, P_SIZE), bf), V((tok, D), f32), V((tok, D), bf), V((tok, FF), bf),
            V((tok, D), f32), V((tok, D), bf), V((tok, D), bf), V((tok, 3 * D), bf), V((tok, FF), f32), V((tok, D), f32),
            V((images, 6 * D), f32), V((mod_height, 128), bf), V((mod_height, 128), f32),
        ] + scatter_sems(R, Z)
        + [D_((1,)), D_((1, 2, Z - 1)), D_((1, 2, Z - 1)), D_((1, 4)), D_((1, 4)), D_((1, 4)), D_((1, 4))],
        compiler_params=pltpu.CompilerParams(collective_id=cid, has_side_effects=True, vmem_limit_bytes=63 * 2**20),
    )(*weights, *acts)


def per_device(
    tokens,
    cond,
    image_lengths,
    ada_weight,
    ada_bias,
    qkv_weight,
    qv_bias,
    attn_weight,
    tail_bias,
    up_weight,
    up_bias,
    down_weight,
    projector_in,
    projector_in_bias,
    projector_mid,
    projector_mid_bias,
    projector_out,
    projector_out_bias,
    targets,
    out_grad,
):
    owners = lax.axis_size("fsdp")
    mix_gathered = (
        lax.all_gather(ada_weight, "fsdp", axis=0, tiled=True),
        lax.all_gather(ada_bias, "fsdp", axis=0, tiled=True),
        lax.all_gather(qkv_weight, "fsdp", axis=0, tiled=True),
        lax.all_gather(qv_bias, "fsdp", axis=0, tiled=True),
        lax.all_gather(attn_weight, "fsdp", axis=0, tiled=True),
        lax.all_gather(tail_bias, "fsdp", axis=0, tiled=True),
    )
    mix_full = unpack_mix(mix_gathered)
    ada_full, ada_bias_full, qkv_full, qv_full, attn_full, tail_full = mix_full
    row_count = tokens.shape[0]
    cond_values = cond.astype(jnp.float32)
    cond_low = lowered(sigmoid_linear(cond_values))
    modulation = matmul(cond_low, ada_full) + ada_bias_full
    image_of, onehot = image_onehot(image_lengths[0], row_count)
    per_token = jnp.dot(onehot, modulation, precision=PRECISE)
    shift_one, scale_one, gate_one, shift_two, scale_two, gate_two = jnp.split(per_token, 6, axis=1)
    inputs = tokens.astype(jnp.float32)
    normed_one = layer_norm(inputs)
    first_in = lowered(normed_one * (1.0 + scale_one) + shift_one)
    key_zero = jnp.zeros((D,), jnp.float32)
    bias_full = jnp.concatenate([qv_full[:D], key_zero, qv_full[D:]])
    projected = lowered(matmul(first_in, qkv_full) + bias_full)
    queries = projected[:, :D].reshape(row_count, HEADS, HD)
    keys_all = projected[:, D : 2 * D].reshape(row_count, HEADS, HD)
    values_all = projected[:, 2 * D :].reshape(row_count, HEADS, HD)
    same_image = (image_of[:, None] == image_of[None, :])[None]
    score_scale = HD ** (-0.5)

    def masked_scores():
        raw_scores = (
            jnp.einsum("qhd,khd->hqk", queries, keys_all, preferred_element_type=jnp.float32)
            * score_scale
        )
        return jnp.where(same_image, raw_scores, -1e30)

    masked = masked_scores()
    row_max = jnp.max(masked, axis=-1, keepdims=True)
    exp_scores = jnp.exp(masked - row_max)
    row_total = jnp.sum(exp_scores, axis=-1, keepdims=True)
    attn_probs = exp_scores / row_total
    head_out = jnp.einsum(
        "hqk,khd->qhd", lowered(attn_probs), values_all, preferred_element_type=jnp.float32
    )
    heads_low = lowered(head_out.reshape(row_count, D))
    branch_attn = matmul(heads_low, attn_full) + tail_full[:D]
    middle = inputs + gate_one * branch_attn
    normed_two = layer_norm(middle)
    second_in = lowered(normed_two * (1.0 + scale_two) + shift_two)
    dense_gathered = (
        lax.all_gather(up_weight, "fsdp", axis=0, tiled=True),
        lax.all_gather(up_bias, "fsdp", axis=0, tiled=True),
        lax.all_gather(down_weight, "fsdp", axis=0, tiled=True),
        lax.all_gather(projector_in, "fsdp", axis=0, tiled=True),
        lax.all_gather(projector_in_bias, "fsdp", axis=0, tiled=True),
        lax.all_gather(projector_mid, "fsdp", axis=0, tiled=True),
        lax.all_gather(projector_mid_bias, "fsdp", axis=0, tiled=True),
        lax.all_gather(projector_out, "fsdp", axis=0, tiled=True),
        lax.all_gather(projector_out_bias, "fsdp", axis=0, tiled=True),
    )
    dense_full = unpack_dense(dense_gathered)
    (
        up_full,
        up_bias_full,
        down_full,
        proj_in_full,
        proj_in_bias_full,
        proj_mid_full,
        proj_mid_bias_full,
        proj_out_full,
        proj_out_bias_full,
    ) = dense_full
    up_pre = matmul(second_in, up_full) + up_bias_full
    up_act = lowered(gelu_tanh(up_pre))
    branch_mlp = matmul(up_act, down_full) + tail_full[D:]
    hidden = middle + gate_two * branch_mlp
    mixed = lowered(hidden)
    first_pre = matmul(mixed, proj_in_full) + proj_in_bias_full
    first_act = lowered(sigmoid_linear(first_pre))
    second_pre = matmul(first_act, proj_mid_full) + proj_mid_bias_full
    second_act = lowered(sigmoid_linear(second_pre))
    features = matmul(second_act, proj_out_full) + proj_out_bias_full
    target_values = targets.astype(jnp.float32)

    def cosine_loss(values):
        value_norm = jnp.sqrt(jnp.sum(values * values, axis=1) + EPSILON)
        target_norm = jnp.sqrt(jnp.sum(target_values * target_values, axis=1) + EPSILON)
        return -0.5 * jnp.sum(jnp.sum(values * target_values, axis=1) / (value_norm * target_norm))

    feature_grad = lowered(jax.grad(cosine_loss)(features))
    dense_again = (
        lax.all_gather(up_weight, "fsdp", axis=0, tiled=True),
        lax.all_gather(up_bias, "fsdp", axis=0, tiled=True),
        lax.all_gather(down_weight, "fsdp", axis=0, tiled=True),
        lax.all_gather(projector_in, "fsdp", axis=0, tiled=True),
        lax.all_gather(projector_in_bias, "fsdp", axis=0, tiled=True),
        lax.all_gather(projector_mid, "fsdp", axis=0, tiled=True),
        lax.all_gather(projector_mid_bias, "fsdp", axis=0, tiled=True),
        lax.all_gather(projector_out, "fsdp", axis=0, tiled=True),
        lax.all_gather(projector_out_bias, "fsdp", axis=0, tiled=True),
    )
    dense_back = unpack_dense(dense_again)
    up_back = dense_back[0]
    down_back = dense_back[2]
    proj_in_back = dense_back[3]
    proj_mid_back = dense_back[5]
    proj_out_back = dense_back[7]
    grad_proj_out = transposed_left(second_act, feature_grad)
    second_back = lowered(
        pull_back(sigmoid_linear, second_pre, transposed_right(feature_grad, proj_out_back))
    )
    grad_proj_mid = transposed_left(first_act, second_back)
    first_back = lowered(
        pull_back(sigmoid_linear, first_pre, transposed_right(second_back, proj_mid_back))
    )
    grad_proj_in = transposed_left(mixed, first_back)
    hidden_grad = out_grad.astype(jnp.float32) + transposed_right(first_back, proj_in_back)
    gate_two_grad = hidden_grad * branch_mlp
    branch_mlp_grad = lowered(hidden_grad * gate_two)
    grad_down = transposed_left(up_act, branch_mlp_grad)
    up_grad = lowered(pull_back(gelu_tanh, up_pre, transposed_right(branch_mlp_grad, down_back)))
    grad_up = transposed_left(second_in, up_grad)
    second_in_grad = transposed_right(up_grad, up_back)
    middle_grad = hidden_grad + pull_back(layer_norm, middle, second_in_grad * (1.0 + scale_two))
    up_rows = by_owner(grad_up, owners)
    up_bias_rows = by_owner(column_sums(up_grad), owners)
    down_rows = by_owner(grad_down, owners)
    proj_in_rows = by_owner(grad_proj_in, owners)
    proj_in_sums = by_owner(column_sums(first_back), owners)
    proj_mid_rows = by_owner(grad_proj_mid, owners)
    proj_mid_sums = by_owner(column_sums(second_back), owners)
    proj_out_rows = by_owner(grad_proj_out, owners)
    proj_out_sums = by_owner(column_sums(feature_grad), owners)
    dense_grads = flatten_all(
        (
            lax.psum_scatter(up_rows, "fsdp", scatter_dimension=0, tiled=True),
            lax.psum_scatter(up_bias_rows, "fsdp", scatter_dimension=0, tiled=True),
            lax.psum_scatter(down_rows, "fsdp", scatter_dimension=0, tiled=True),
            lax.psum_scatter(proj_in_rows, "fsdp", scatter_dimension=0, tiled=True),
            lax.psum_scatter(proj_in_sums, "fsdp", scatter_dimension=0, tiled=True),
            lax.psum_scatter(proj_mid_rows, "fsdp", scatter_dimension=0, tiled=True),
            lax.psum_scatter(proj_mid_sums, "fsdp", scatter_dimension=0, tiled=True),
            lax.psum_scatter(proj_out_rows, "fsdp", scatter_dimension=0, tiled=True),
            lax.psum_scatter(proj_out_sums, "fsdp", scatter_dimension=0, tiled=True),
        )
    )
    mix_again = (
        lax.all_gather(ada_weight, "fsdp", axis=0, tiled=True),
        lax.all_gather(ada_bias, "fsdp", axis=0, tiled=True),
        lax.all_gather(qkv_weight, "fsdp", axis=0, tiled=True),
        lax.all_gather(qv_bias, "fsdp", axis=0, tiled=True),
        lax.all_gather(attn_weight, "fsdp", axis=0, tiled=True),
        lax.all_gather(tail_bias, "fsdp", axis=0, tiled=True),
    )
    mix_back = unpack_mix(mix_again)
    ada_back = mix_back[0]
    qkv_back = mix_back[2]
    attn_back = mix_back[4]
    gate_one_grad = middle_grad * branch_attn
    branch_attn_grad = lowered(middle_grad * gate_one)
    grad_attn = transposed_left(heads_low, branch_attn_grad)
    heads_grad = lowered(transposed_right(branch_attn_grad, attn_back)).reshape(
        row_count, HEADS, HD
    )
    again_probs = jnp.exp(masked_scores() - row_max) / row_total
    prob_grad = jnp.einsum(
        "qhd,khd->hqk", heads_grad, values_all, preferred_element_type=jnp.float32
    )
    value_grad = jnp.einsum(
        "hqk,qhd->khd", lowered(again_probs), heads_grad, preferred_element_type=jnp.float32
    )
    score_grad = lowered(
        again_probs * (prob_grad - jnp.sum(again_probs * prob_grad, axis=-1, keepdims=True))
    )
    query_grad = (
        jnp.einsum("hqk,khd->qhd", score_grad, keys_all, preferred_element_type=jnp.float32)
        * score_scale
    )
    key_grad = (
        jnp.einsum("hqk,qhd->khd", score_grad, queries, preferred_element_type=jnp.float32)
        * score_scale
    )
    projected_grad = lowered(
        jnp.concatenate(
            [
                query_grad.reshape(row_count, D),
                key_grad.reshape(row_count, D),
                value_grad.reshape(row_count, D),
            ],
            axis=1,
        )
    )
    grad_qkv = transposed_left(first_in, projected_grad)
    projected_sums = column_sums(projected_grad)
    grad_qv_bias = jnp.concatenate([projected_sums[:D], projected_sums[2 * D :]])
    first_in_grad = transposed_right(projected_grad, qkv_back)
    input_grad = middle_grad + pull_back(layer_norm, inputs, first_in_grad * (1.0 + scale_one))
    token_mod_grad = jnp.concatenate(
        [
            first_in_grad,
            first_in_grad * normed_one,
            gate_one_grad,
            second_in_grad,
            second_in_grad * normed_two,
            gate_two_grad,
        ],
        axis=1,
    )
    modulation_grad = lowered(
        lax.dot_general(onehot, token_mod_grad, (((0,), (0,)), ((), ())), precision=PRECISE)
    )
    grad_ada = transposed_left(cond_low, modulation_grad)
    cond_grad = pull_back(
        sigmoid_linear, cond_values, transposed_right(modulation_grad, ada_back)
    ).astype(jnp.bfloat16)
    grad_tail = jnp.concatenate([column_sums(branch_attn_grad), column_sums(branch_mlp_grad)])
    ada_rows = by_owner(grad_ada, owners)
    ada_sums = by_owner(column_sums(modulation_grad), owners)
    qkv_rows = by_owner(grad_qkv, owners)
    qv_rows = by_owner(grad_qv_bias, owners)
    attn_rows = by_owner(grad_attn, owners)
    tail_rows = by_owner(grad_tail, owners)
    mix_grads = flatten_all(
        (
            lax.psum_scatter(ada_rows, "fsdp", scatter_dimension=0, tiled=True),
            lax.psum_scatter(ada_sums, "fsdp", scatter_dimension=0, tiled=True),
            lax.psum_scatter(qkv_rows, "fsdp", scatter_dimension=0, tiled=True),
            lax.psum_scatter(qv_rows, "fsdp", scatter_dimension=0, tiled=True),
            lax.psum_scatter(attn_rows, "fsdp", scatter_dimension=0, tiled=True),
            lax.psum_scatter(tail_rows, "fsdp", scatter_dimension=0, tiled=True),
        )
    )
    return (
        mixed,
        input_grad.astype(jnp.bfloat16),
        cond_grad,
        mix_grads[0],
        mix_grads[1],
        mix_grads[2],
        mix_grads[3],
        mix_grads[4],
        mix_grads[5],
        dense_grads[0],
        dense_grads[1],
        dense_grads[2],
        dense_grads[3],
        dense_grads[4],
        dense_grads[5],
        dense_grads[6],
        dense_grads[7],
        dense_grads[8],
    )


def per_device_kernels(
    tokens,
    cond,
    image_lengths,
    ada_weight,
    ada_bias,
    qkv_weight,
    qv_bias,
    attn_weight,
    tail_bias,
    up_weight,
    up_bias,
    down_weight,
    projector_in,
    projector_in_bias,
    projector_mid,
    projector_mid_bias,
    projector_out,
    projector_out_bias,
    targets,
    out_grad,
):
    owners = lax.axis_size("fsdp")
    me = lax.axis_index("fsdp")
    row_count = tokens.shape[0]
    rows = D // owners
    images = cond.shape[0]
    cond_values = cond.astype(jnp.float32)
    cond_low = lowered(sigmoid_linear(cond_values))
    letters = [jnp.pad(cond_low.reshape(images, owners, rows).transpose(1, 0, 2), ((0, 0), (0, 0), (0, 128 - rows)))]
    biases = (ada_bias, qv_bias, tail_bias, up_bias, projector_in_bias, projector_mid_bias, projector_out_bias)
    for bias in biases:
        height = -(-bias.shape[0] // 128)
        lines = jnp.pad(bias, (0, height * 128 - bias.shape[0])).reshape(1, height, 128)
        letters.append(jnp.broadcast_to(lines, (owners, height, 128)))
    letters = jnp.concatenate(letters, axis=1)
    letters = jnp.pad(letters, ((0, 0), (0, 16 - letters.shape[1]), (0, 0)))
    ada_mine = ada_weight.reshape(rows, 6 * D)
    used = images * 6 * D // 128
    mod_height = -(-used // 16) * 16
    widths = (6 * D, 2 * D, 2 * D, FF, P_SIZE, P_SIZE, Z)
    image_of, onehot = image_onehot(image_lengths[0], row_count)
    same_image = (image_of[:, None] == image_of[None, :]).astype(jnp.float32)
    onehot = jnp.pad(onehot, ((0, 0), (0, 128 - onehot.shape[1])))
    results = forward(
        owners,
        images,
        (
            qkv_weight.reshape(rows, 3 * D),
            attn_weight.reshape(rows, D),
            up_weight.reshape(rows, FF),
            projector_in.reshape(rows, P_SIZE),
            down_weight.reshape(-1, D),
            projector_mid.reshape(-1, P_SIZE),
            projector_out.reshape(-1, Z),
        ),
        (ada_mine, letters, tokens, onehot, same_image),
        ((0, 1, 2, 3, 5, 7, 8), (0, 1, 2, 4, 6, 8, 9)),
        1,
    )
    mixed = results[15]
    modulation, cond_mine = results[21:]
    sums = backward(
        owners,
        images,
        results[:6],
        (tokens, onehot, same_image, modulation, targets, out_grad) + tuple(results[6:21]),
        mod_height,
        (1, ((0, 1, 3, 5, 6, 7, 8), (0, 1, 4, 6, 8, 9, 10)), (0, 1, 2, 3, 4, 5, 6), (2, 2, 5, 8, 3)),
        2,
    )
    qkv_sum, attn_sum, up_sum, down_sum, in_sum, mid_sum, out_sum, tokens_grad = sums[:8]
    qkv_cols, attn_cols, mlp_cols, up_cols, in_cols, mid_cols, out_cols = [part[0] for part in sums[8:15]]
    modulation_all = sums[15].reshape(owners, mod_height, 128)[:, :used].reshape(owners * images, 6 * D)
    grad_ada = transposed_left(cond_mine, modulation_all)
    cond_back = transposed_right(modulation_all, ada_mine).reshape(owners, images * rows)
    bias_parts = [
        by_owner(part, owners)
        for part in (
            jnp.concatenate([qkv_cols[:D], qkv_cols[2 * D :]]),
            jnp.concatenate([attn_cols, mlp_cols]),
            up_cols,
            in_cols,
            mid_cols,
            out_cols,
        )
    ]
    received = lax.all_to_all(jnp.concatenate([cond_back] + bias_parts, axis=1), "fsdp", 0, 0, tiled=True)
    cond_back = received[:, : images * rows].reshape(owners, images, rows).transpose(1, 0, 2).reshape(images, D)
    cond_grad = pull_back(sigmoid_linear, cond_values, cond_back).astype(jnp.bfloat16)
    small = jnp.sum(received[:, images * rows :], axis=0)
    grad_ada_bias = lax.dynamic_slice(
        column_sums(modulation_all), (me * (6 * D // owners),), (6 * D // owners,)
    )
    small_parts, at = [], 0
    for width in widths[1:]:
        small_parts.append(small[at : at + width // owners])
        at += width // owners
    qv_small, tail_small, up_small, in_small, mid_small, out_small = small_parts
    return (
        mixed,
        tokens_grad,
        cond_grad,
        grad_ada.reshape(-1),
        grad_ada_bias,
        qkv_sum.reshape(-1),
        qv_small,
        attn_sum.reshape(-1),
        tail_small,
        up_sum.reshape(-1),
        up_small,
        down_sum.reshape(-1),
        in_sum.reshape(-1),
        in_small,
        mid_sum.reshape(-1),
        mid_small,
        out_sum.reshape(-1),
        out_small,
    )


def solution(mesh):
    in_specs = (
        P("fsdp", None),
        P("fsdp", None),
        P("fsdp", None),
        P("fsdp"),
        P("fsdp"),
        P("fsdp"),
        P("fsdp"),
        P("fsdp"),
        P("fsdp"),
        P("fsdp"),
        P("fsdp"),
        P("fsdp"),
        P("fsdp"),
        P("fsdp"),
        P("fsdp"),
        P("fsdp"),
        P("fsdp"),
        P("fsdp"),
        P("fsdp", None),
        P("fsdp", None),
    )
    out_specs = (
        P("fsdp", None),
        P("fsdp", None),
        P("fsdp", None),
        P("fsdp"),
        P("fsdp"),
        P("fsdp"),
        P("fsdp"),
        P("fsdp"),
        P("fsdp"),
        P("fsdp"),
        P("fsdp"),
        P("fsdp"),
        P("fsdp"),
        P("fsdp"),
        P("fsdp"),
        P("fsdp"),
        P("fsdp"),
        P("fsdp"),
    )
    owners = mesh.shape["fsdp"]
    program = per_device_kernels if owners % 16 == 0 and D % owners == 0 else per_device
    return jax.shard_map(
        program, mesh=mesh, in_specs=in_specs, out_specs=out_specs, check_vma=False
    )
```
